32 devices in a mesh: dp: 4 (over y, x), expert: 8 (over z, core).
Axes of the slice: x: 2, y: 2, z: 4, core: 2. Of those that a mesh axis runs over, the one named last changes fastest.
Arguments:
- tokens: bfloat16 [64, 128, 1536], P('dp', 'expert'), may hold values from -6 to 6
- cotangent: bfloat16 [64, 128, 1536], P('dp', 'expert'), may hold values from -6 to 6
- lengths: int32 [64, 4], P('dp'), may hold values from 0 to 128, as said below
- placement: int32 [64], P('dp'), may hold values from 0 to 15, as said below
- routes: int32 [8192, 4], P(('dp', 'expert')), may hold values from 0 to 15, all different within a row
- priority: int32 [8192, 4], P(('dp', 'expert')), may hold values from 0 to 1023, as said below
- g_attn: bfloat16 [1536], P(('dp', 'expert')), may hold values from 0.099609375 to 1.8984375
- w_query: bfloat16 [1536, 1536], P(('dp', 'expert')), may hold values from -0.15625 to 0.15625
- key_projection: bfloat16 [1536, 256], P(('dp', 'expert')), may hold values from -0.15625 to 0.15625
- value_projection: bfloat16 [1536, 256], P(('dp', 'expert')), may hold values from -0.15625 to 0.15625
- w_out: bfloat16 [1536, 1536], P(('dp', 'expert')), may hold values from -1.25 to 1.25
- g_moe: bfloat16 [1536], P(('dp', 'expert')), may hold values from 0.099609375 to 1.8984375
- w_router: bfloat16 [1536, 16], P(('dp', 'expert')), may hold values from -0.078125 to 0.078125
- w_gate: bfloat16 [16, 1536, 768], P('expert', 'dp'), may hold values from -0.15625 to 0.15625
- w_up: bfloat16 [16, 1536, 768], P('expert', 'dp'), may hold values from -0.15625 to 0.15625
- w_down: bfloat16 [16, 768, 1536], P('expert', None, 'dp'), may hold values from -0.625 to 0.625
Outputs:
- output: bfloat16 [64, 128, 1536], P('dp', 'expert')
- input_grad: bfloat16 [64, 128, 1536], P('dp', 'expert')
- grad_g_attn: float32 [1536], P(('dp', 'expert'))
- grad_query: float32 [1536, 1536], P(('dp', 'expert'))
- grad_key: float32 [1536, 256], P(('dp', 'expert'))
- value_weight_gradient: float32 [1536, 256], P(('dp', 'expert'))
- grad_out: float32 [1536, 1536], P(('dp', 'expert'))
- grad_g_moe: float32 [1536], P(('dp', 'expert'))
- grad_router: float32 [1536, 16], P(('dp', 'expert'))
- grad_gate: float32 [16, 1536, 768], P('expert', 'dp')
- grad_up: float32 [16, 1536, 768], P('expert', 'dp')
- grad_down: float32 [16, 768, 1536], P('expert', None, 'dp')
The draws below stay inside these ranges and needn't reach their ends.
Inputs may be any that keep to these rules, and one draw needn't show every extreme that they name: `lengths`: each row sums to 128; zeros are empty documents. In every group of 16 sequences of one index of dp, some sequence is one document of 128. `placement`: each aligned group of 16 entries (the sequences of one index of dp) is a permutation of 0 to 15. `routes`: each row names 4 different experts. `priority`: the entries of each aligned block of 256 rows (one device) are a permutation of 0 to 1023.
All inputs are finite; a program needn't handle non-finite values.
Results may differ from the reference program's by a relative error of at most 0.015.
The reference program's roundings to bfloat16 on the way count: a program that leaves them out, or rounds other values in their place, can miss the bound.
Values may be sent and summed in bfloat16 or wider, within the bound.
No kernel may reach another device: no remote copies, remote signals or barrier semaphores. Data moves between devices by JAX's collectives and lax.ppermute only.
A program may use at most 192 MiB of HBM per device.

```python
import math
import jax
import jax.numpy as jnp
from jax import lax

MODEL_WIDTH = 1536
QUERY_HEADS = 12
KEY_VALUE_HEADS = 2
HEAD_SIZE = 128
FF = 768
TOPK = 4
EXPERTS = 16
SEQ_LEN = 128
SEQ_DEV = 2
DOCS = 4
ROW_SEQS = 16
SEQS = 64
TOK_DEV = 256
TOKENS = 8192
CAP = 72


def doc_lengths(key):
    cut_key, split_key, full_key = jax.random.split(key, 3)
    groups = SEQS // ROW_SEQS
    cut_points = jnp.sort(jax.random.randint(cut_key, (SEQS, DOCS - 1), 1, SEQ_LEN), axis=1)
    edge_list = jnp.concatenate([jnp.zeros((SEQS, 1), jnp.int32), cut_points.astype(jnp.int32), jnp.full((SEQS, 1), SEQ_LEN, jnp.int32)], axis=1)
    pieces = edge_list[:, 1:] - edge_list[:, :-1]
    single_doc = jnp.concatenate([jnp.full((SEQS, 1), SEQ_LEN, jnp.int32), jnp.zeros((SEQS, DOCS - 1), jnp.int32)], axis=1)
    split_flag = jax.random.randint(split_key, (SEQS,), 0, 4) == 0
    picked = jax.random.randint(full_key, (groups, 1), 0, ROW_SEQS)
    forced = (jnp.arange(ROW_SEQS, dtype=jnp.int32)[None, :] == picked).reshape(SEQS)
    split_flag = jnp.logical_and(split_flag, jnp.logical_not(forced))
    return jnp.where(split_flag[:, None], pieces, single_doc).astype(jnp.int32)


def draw_lengths(key, part):
    return doc_lengths(key)


def draw_placement(key, part):
    doc_lens = doc_lengths(key)
    key = jax.random.fold_in(key, 7)
    groups = SEQS // ROW_SEQS
    seq_cost = jnp.sum(doc_lens * doc_lens, axis=1).reshape(groups, ROW_SEQS)
    group_keys = jax.random.split(key, groups)
    tie_break = jax.vmap(lambda single: jax.random.permutation(single, ROW_SEQS))(group_keys).astype(jnp.int32)
    score_int = seq_cost * ROW_SEQS + tie_break
    ranked = jnp.argsort(-score_int, axis=1, stable=True).astype(jnp.int32)
    rank_list = jnp.arange(ROW_SEQS, dtype=jnp.int32)
    columns = ROW_SEQS // SEQ_DEV
    slot_of = rank_list // columns
    column_of = rank_list % columns
    device_of = jnp.where(slot_of % 2 == 0, column_of, columns - 1 - column_of)
    code_of = (device_of * SEQ_DEV + slot_of).astype(jnp.int32)
    group_rows = jnp.broadcast_to(jnp.arange(groups, dtype=jnp.int32)[:, None], (groups, ROW_SEQS))
    table = jnp.zeros((groups, ROW_SEQS), jnp.int32).at[group_rows, ranked].set(jnp.broadcast_to(code_of[None, :], (groups, ROW_SEQS)))
    return table.reshape(SEQS)


def draw_priority(key, part):
    key = jax.random.fold_in(key, 11)
    devices = TOKENS // TOK_DEV
    device_keys = jax.random.split(key, devices)
    orders = jax.vmap(lambda single: jax.random.permutation(single, TOK_DEV * TOPK))(device_keys)
    return orders.reshape(TOKENS, TOPK).astype(jnp.int32)


def steps_of(own_key, dims, cuts, smallest, largest):
    loudness = 1.0
    for position, shards_of in cuts:
        draws = jax.random.uniform(jax.random.fold_in(jax.random.fold_in(own_key, 6), position), (shards_of,), jnp.float32, smallest / len(cuts), largest / len(cuts))
        loudness = loudness * jnp.repeat(jnp.exp(draws), dims[position] // shards_of).reshape((-1,) + (1,) * (len(dims) - 1 - position))
    return loudness


def picks_of(stream_key, rows, count, top, lift):
    ranking = jax.random.permutation(jax.random.fold_in(stream_key, 1), count)
    pull = ranking
    for power in range(3):
        pull = pull * pull // count
    pull = pull * lift // count
    chance = jax.random.randint(jax.random.fold_in(stream_key, 2), (rows, count), 0, 4096) + pull
    sure = jax.random.permutation(jax.random.fold_in(stream_key, 3), rows)[jnp.arange(count) % rows]
    chance = jnp.where(jnp.arange(rows)[:, None] == sure[None, :], 1 << 14, chance)
    score = chance * count + jnp.arange(count)
    return lax.top_k(score.astype(jnp.int32), top)[1].astype(jnp.int32)


def bell_draw(key, extent, width, limit, cuts=(), held_as=jnp.bfloat16):
    array = width * jax.random.normal(key, extent, jnp.float32)
    if cuts:
        array = array * steps_of(key, extent, cuts, -0.22, 0.18)
    return jnp.clip(array, -limit, limit).astype(held_as)


def setup_inputs(seed: int = 0) -> dict:
    streams_of = jax.random.split(jax.random.key(seed), 17)
    return {
        "tokens": bell_draw(streams_of[0], (SEQS, SEQ_LEN, MODEL_WIDTH), 1.0, 6.0, ((0, 4), (1, 8))),
        "cotangent": bell_draw(streams_of[1], (SEQS, SEQ_LEN, MODEL_WIDTH), 1.0, 6.0, ((0, 4), (1, 8))),
        "lengths": draw_lengths(jax.random.fold_in(streams_of[16], 71), 0),
        "placement": draw_placement(jax.random.fold_in(streams_of[16], 71), 0),
        "routes": picks_of(streams_of[4], TOKENS, EXPERTS, TOPK, 2048),
        "priority": draw_priority(jax.random.fold_in(streams_of[16], 71), 0),
        "g_attn": jnp.clip(1.0 + 0.18 * jax.random.normal(streams_of[6], (MODEL_WIDTH,), jnp.float32), 0.099609375, 1.8984375).astype(jnp.bfloat16),
        "w_query": bell_draw(streams_of[7], (MODEL_WIDTH, QUERY_HEADS * HEAD_SIZE), MODEL_WIDTH ** -0.5, 0.15625, ((0, 32),)),
        "key_projection": bell_draw(streams_of[8], (MODEL_WIDTH, KEY_VALUE_HEADS * HEAD_SIZE), MODEL_WIDTH ** -0.5, 0.15625, ((0, 32),)),
        "value_projection": bell_draw(streams_of[9], (MODEL_WIDTH, KEY_VALUE_HEADS * HEAD_SIZE), MODEL_WIDTH ** -0.5, 0.15625, ((0, 32),)),
        "w_out": bell_draw(streams_of[10], (QUERY_HEADS * HEAD_SIZE, MODEL_WIDTH), (QUERY_HEADS * HEAD_SIZE // 64) ** -0.5, 1.25, ((0, 32),)),
        "g_moe": jnp.clip(1.0 + 0.18 * jax.random.normal(streams_of[11], (MODEL_WIDTH,), jnp.float32), 0.099609375, 1.8984375).astype(jnp.bfloat16),
        "w_router": bell_draw(streams_of[12], (MODEL_WIDTH, EXPERTS), (4 * MODEL_WIDTH) ** -0.5, 0.078125, ((0, 32),)),
        "w_gate": bell_draw(streams_of[13], (EXPERTS, MODEL_WIDTH, FF), MODEL_WIDTH ** -0.5, 0.15625, ((0, 8), (1, 4))),
        "w_up": bell_draw(streams_of[14], (EXPERTS, MODEL_WIDTH, FF), MODEL_WIDTH ** -0.5, 0.15625, ((0, 8), (1, 4))),
        "w_down": bell_draw(streams_of[15], (EXPERTS, FF, MODEL_WIDTH), (FF // 8) ** -0.5, 0.625, ((0, 8), (2, 4))),
    }


EPSILON = 1e-06
ROPE_BASE = 1000000.0
NEG_FILL = -1e+30
TOP_PRECISION = lax.Precision.HIGHEST

@jax.custom_vjp
def narrow_input(v):
    return lax.optimization_barrier(v.astype(jnp.bfloat16)).astype(jnp.float32)

@jax.custom_vjp
def narrow_backward(v):
    return v

def low_keep(v):
    return (narrow_input(v), None)

def low_pass(kept, grad):
    return (grad,)

def back_keep(v):
    return (v, None)

def back_low(kept, grad):
    return (narrow_input(grad),)
narrow_input.defvjp(low_keep, low_pass)
narrow_backward.defvjp(back_keep, back_low)

def sequence_layout(doc_lens, seq_len):
    token_steps = jnp.arange(seq_len, dtype=jnp.int32)
    doc_ends = jnp.cumsum(doc_lens)
    doc_index = lax.optimization_barrier(jnp.sum((token_steps[:, None] >= doc_ends[None, :-1]).astype(jnp.int32), axis=1))
    doc_starts = doc_ends - doc_lens
    doc_slots = jnp.arange(doc_lens.shape[0], dtype=jnp.int32)
    start_of = lax.optimization_barrier(jnp.sum(jnp.where(doc_slots[None, :] == doc_index[:, None], doc_starts[None, :], 0), axis=1))
    return ((token_steps - start_of).astype(jnp.float32), doc_index)

def device_layout(dev_lens, seq_len):
    positions, doc_index = jax.vmap(lambda single: sequence_layout(single, seq_len))(dev_lens)
    doc_count = dev_lens.shape[1]
    labels = doc_index + doc_count * jnp.arange(dev_lens.shape[0], dtype=jnp.int32)[:, None]
    return (positions.reshape(-1), labels.reshape(-1))

def rope_tables(positions, head_dim):
    freq_index = jnp.arange(head_dim // 2, dtype=jnp.float32)
    frequency = jnp.exp(freq_index * (-2.0 / head_dim) * math.log(ROPE_BASE))
    angle_table = positions[:, None] * frequency[None, :]
    return (jnp.cos(angle_table), jnp.sin(angle_table))

def apply_rotation(values, cosine_table, sine_values):
    half_size = values.shape[-1] // 2
    first_half = values[..., :half_size]
    second_half = values[..., half_size:]
    cos_wide = cosine_table[:, None, :]
    sin_wide = sine_values[:, None, :]
    return jnp.concatenate([first_half * cos_wide - second_half * sin_wide, second_half * cos_wide + first_half * sin_wide], axis=-1)

def slot_ranks(route_flat, prio_flat, expert_count):
    pair_count = route_flat.shape[0]
    by_priority = jnp.zeros((pair_count,), jnp.int32).at[prio_flat].set(jnp.arange(pair_count, dtype=jnp.int32))
    sorted_experts = route_flat[by_priority]
    one_hot = (sorted_experts[:, None] == jnp.arange(expert_count, dtype=jnp.int32)[None, :]).astype(jnp.int32)
    running = jnp.cumsum(one_hot, axis=0)
    sorted_rank = lax.optimization_barrier(jnp.sum(running * one_hot, axis=1)) - 1
    return sorted_rank[prio_flat]

def attend_block(x_block, cosine_table, sine_values, labels, gain_attn, weight_query, weight_key, value_matrix, weight_out):
    token_count = x_block.shape[0]
    query_group_width = QUERY_HEADS // KEY_VALUE_HEADS
    inverse = lax.rsqrt(lax.optimization_barrier(jnp.mean(x_block * x_block, axis=-1, keepdims=True)) + EPSILON)
    normalized_input = narrow_input(x_block * inverse * gain_attn)
    query_rows = narrow_backward(jnp.dot(normalized_input, weight_query, precision=TOP_PRECISION))
    keys_unrotated = narrow_backward(jnp.dot(normalized_input, weight_key, precision=TOP_PRECISION))
    values_narrow = narrow_input(narrow_backward(jnp.dot(normalized_input, value_matrix, precision=TOP_PRECISION))).reshape(token_count, KEY_VALUE_HEADS, HEAD_SIZE)
    query_rotated = narrow_input(apply_rotation(query_rows.reshape(token_count, QUERY_HEADS, HEAD_SIZE), cosine_table, sine_values)).reshape(token_count, KEY_VALUE_HEADS, query_group_width, HEAD_SIZE)
    key_rotated = narrow_input(apply_rotation(keys_unrotated.reshape(token_count, KEY_VALUE_HEADS, HEAD_SIZE), cosine_table, sine_values))
    scores = narrow_backward(jnp.einsum('qhgd,khd->hgqk', query_rotated, key_rotated, precision=TOP_PRECISION) * HEAD_SIZE ** (-0.5))
    token_steps = jnp.arange(token_count, dtype=jnp.int32)
    allowed = jnp.logical_and(labels[:, None] == labels[None, :], token_steps[:, None] >= token_steps[None, :])
    scores = jnp.where(allowed, scores, NEG_FILL)
    score_top = lax.optimization_barrier(jnp.max(scores, axis=-1, keepdims=True))
    exp_scores = jnp.exp(scores - score_top)
    attn_probs = exp_scores / lax.optimization_barrier(jnp.sum(exp_scores, axis=-1, keepdims=True))
    mixed_heads = jnp.einsum('hgqk,khd->qhgd', narrow_input(attn_probs), values_narrow, precision=TOP_PRECISION).reshape(token_count, QUERY_HEADS * HEAD_SIZE)
    mixed_heads = narrow_input(narrow_backward(mixed_heads))
    return x_block + narrow_backward(jnp.dot(mixed_heads, weight_out, precision=TOP_PRECISION))

def reference(tokens, cotangent, lengths, placement, routes, priority, g_attn, w_query, key_projection, value_projection, w_out, g_moe, w_router, w_gate, w_up, w_down):
    groups = SEQS // ROW_SEQS
    devices = SEQS // SEQ_DEV
    code_list = jnp.arange(ROW_SEQS, dtype=jnp.int32)
    group_rows = jnp.broadcast_to(jnp.arange(groups, dtype=jnp.int32)[:, None], (groups, ROW_SEQS))
    dealt_table = jnp.zeros((groups, ROW_SEQS), jnp.int32).at[group_rows, placement.reshape(groups, ROW_SEQS)].set(jnp.broadcast_to(code_list[None, :], (groups, ROW_SEQS)))
    dealt = (dealt_table + group_rows * ROW_SEQS).reshape(-1)
    x_dealt = tokens[dealt].astype(jnp.float32).reshape(devices, TOK_DEV, MODEL_WIDTH)
    dy_dealt = cotangent[dealt].astype(jnp.float32).reshape(devices * TOK_DEV, MODEL_WIDTH)
    lens_dealt = lengths[dealt].reshape(devices, SEQ_DEV, DOCS)
    positions, labels = jax.vmap(lambda single: device_layout(single, SEQ_LEN))(lens_dealt)
    cosine_table, sine_values = jax.vmap(lambda single: rope_tables(single, HEAD_SIZE))(positions)
    route_dev = routes.reshape(devices, TOK_DEV * TOPK)
    ranks = jax.vmap(lambda first, second: slot_ranks(first, second, EXPERTS))(route_dev, priority.reshape(devices, TOK_DEV * TOPK))
    kept = ranks < CAP
    device_ids = jnp.arange(devices, dtype=jnp.int32)[:, None]
    dummy_row = EXPERTS * devices * CAP
    pair_rows = jnp.where(kept, (route_dev * devices + device_ids) * CAP + ranks, dummy_row)
    pair_tokens = device_ids * TOK_DEV + jnp.arange(TOK_DEV * TOPK, dtype=jnp.int32)[None, :] // TOPK
    slot_tokens = jnp.full((dummy_row + 1,), devices * TOK_DEV, jnp.int32).at[pair_rows.reshape(-1)].set(pair_tokens.reshape(-1))
    slot_tokens = slot_tokens[:dummy_row].reshape(EXPERTS, devices * CAP)
    pair_rows = pair_rows.reshape(devices * TOK_DEV, TOPK)
    selector = (routes[:, :, None] == jnp.arange(EXPERTS, dtype=jnp.int32)[None, None, :]).astype(jnp.float32)

    def forward(x_all, gain_attn, weight_query, weight_key, value_matrix, weight_out, gain_moe, weight_router, weight_gate, weight_up, weight_down):

        def attend_one(items):
            return attend_block(items[0], items[1], items[2], items[3], gain_attn, weight_query, weight_key, value_matrix, weight_out)
        residual = lax.map(jax.checkpoint(attend_one), (x_all, cosine_table, sine_values, labels)).reshape(devices * TOK_DEV, MODEL_WIDTH)
        inverse = lax.rsqrt(lax.optimization_barrier(jnp.mean(residual * residual, axis=-1, keepdims=True)) + EPSILON)
        normalized_input = narrow_input(residual * inverse * gain_moe)
        logits = narrow_backward(jnp.dot(normalized_input, weight_router, precision=TOP_PRECISION))
        chosen = lax.optimization_barrier(jnp.sum(selector * logits[:, None, :], axis=-1))
        gates = jax.nn.softmax(chosen, axis=-1)
        padded = jnp.concatenate([normalized_input, jnp.zeros((1, MODEL_WIDTH), jnp.float32)], axis=0)

        def expert_one(items):
            gate_one, up_one, down_one, slot_rows = items
            inputs = narrow_backward(padded[slot_rows])
            pre_gate = narrow_backward(jnp.dot(inputs, gate_one, precision=TOP_PRECISION))
            pre_up = narrow_backward(jnp.dot(inputs, up_one, precision=TOP_PRECISION))
            hidden = narrow_input(jax.nn.gelu(pre_gate) * pre_up)
            return narrow_input(narrow_backward(jnp.dot(hidden, down_one, precision=TOP_PRECISION)))
        expert_out = lax.map(jax.checkpoint(expert_one), (weight_gate, weight_up, weight_down, slot_tokens))
        out_table = jnp.concatenate([expert_out.reshape(dummy_row, MODEL_WIDTH), jnp.zeros((1, MODEL_WIDTH), jnp.float32)], axis=0)
        mixture = residual
        for choice_index in range(TOPK):
            mixture = mixture + gates[:, choice_index:choice_index + 1] * out_table[pair_rows[:, choice_index]]
        return mixture
    final, pullback = jax.vjp(forward, x_dealt, g_attn.astype(jnp.float32), w_query.astype(jnp.float32), key_projection.astype(jnp.float32), value_projection.astype(jnp.float32), w_out.astype(jnp.float32), g_moe.astype(jnp.float32), w_router.astype(jnp.float32), w_gate.astype(jnp.float32), w_up.astype(jnp.float32), w_down.astype(jnp.float32))
    grads = pullback(dy_dealt)
    output = jnp.zeros((SEQS, SEQ_LEN, MODEL_WIDTH), jnp.float32).at[dealt].set(final.reshape(SEQS, SEQ_LEN, MODEL_WIDTH)).astype(jnp.bfloat16)
    input_grad = jnp.zeros((SEQS, SEQ_LEN, MODEL_WIDTH), jnp.float32).at[dealt].set(grads[0].reshape(SEQS, SEQ_LEN, MODEL_WIDTH)).astype(jnp.bfloat16)
    return (output, input_grad, grads[1], grads[2], grads[3], grads[4], grads[5], grads[6], grads[7], grads[8], grads[9], grads[10])
```

```python
import math

import jax
import jax.numpy as jnp
from jax import lax
from jax.experimental import pallas as pl
from jax.experimental.pallas import tpu as pltpu
from jax.sharding import PartitionSpec as P

QUERY_HEADS = 12
KEY_VALUE_HEADS = 2
HEAD_SIZE = 128
TOPK = 4
SEQ_DEV = 2


EPSILON = 1e-06
ROPE_BASE = 1000000.0
NEG_FILL = -1e30


def contract(left, right, left_dims, right_dims):
    return lax.dot_general(
        left, right, ((left_dims, right_dims), ((), ())), preferred_element_type=jnp.float32
    )


def sequence_layout(doc_lens, seq_len):
    token_steps = jnp.arange(seq_len, dtype=jnp.int32)
    doc_ends = jnp.cumsum(doc_lens)
    doc_index = jnp.sum((token_steps[:, None] >= doc_ends[None, :-1]).astype(jnp.int32), axis=1)
    doc_starts = doc_ends - doc_lens
    doc_slots = jnp.arange(doc_lens.shape[0], dtype=jnp.int32)
    start_of = jnp.sum(
        jnp.where(doc_slots[None, :] == doc_index[:, None], doc_starts[None, :], 0), axis=1
    )
    return ((token_steps - start_of).astype(jnp.float32), doc_index)


def device_layout(dev_lens, seq_len):
    positions, doc_index = jax.vmap(lambda single: sequence_layout(single, seq_len))(dev_lens)
    doc_count = dev_lens.shape[1]
    labels = doc_index + doc_count * jnp.arange(dev_lens.shape[0], dtype=jnp.int32)[:, None]
    return (positions.reshape(-1), labels.reshape(-1))


def rope_tables(positions, head_dim):
    freq_index = jnp.arange(head_dim // 2, dtype=jnp.float32)
    frequency = jnp.exp(freq_index * (-2.0 / head_dim) * math.log(ROPE_BASE))
    angle_table = positions[:, None] * frequency[None, :]
    return (jnp.cos(angle_table), jnp.sin(angle_table))


def apply_rotation(values, cosine_table, sine_values):
    half_size = values.shape[-1] // 2
    first_half = values[..., :half_size]
    second_half = values[..., half_size:]
    cos_wide = cosine_table[:, None, :]
    sin_wide = sine_values[:, None, :]
    return jnp.concatenate(
        [
            first_half * cos_wide - second_half * sin_wide,
            second_half * cos_wide + first_half * sin_wide,
        ],
        axis=-1,
    )


def rotate_back(values, cosine_table, sine_values):
    half_size = values.shape[-1] // 2
    first_half = values[..., :half_size]
    second_half = values[..., half_size:]
    cos_wide = cosine_table[:, None, :]
    sin_wide = sine_values[:, None, :]
    return jnp.concatenate(
        [
            first_half * cos_wide + second_half * sin_wide,
            second_half * cos_wide - first_half * sin_wide,
        ],
        axis=-1,
    )


def slot_ranks(route_flat, prio_flat):
    same = route_flat[:, None] == route_flat[None, :]
    ahead = prio_flat[None, :] < prio_flat[:, None]
    return jnp.sum(jnp.logical_and(same, ahead).astype(jnp.int32), axis=1)


def norm_back(inputs, inverse, gain, grad_normed):
    scaled = grad_normed * gain
    grad_gain = jnp.sum(grad_normed * inputs * inverse, axis=0)
    grad_inputs = inverse * scaled - inputs * inverse**3 * jnp.mean(
        scaled * inputs, axis=-1, keepdims=True
    )
    return (grad_gain, grad_inputs)


def swap_x(value):
    return lax.ppermute(value, "dp", [(i, i ^ 1) for i in range(4)])


def swap_y(value):
    return lax.ppermute(value, "dp", [(i, i ^ 2) for i in range(4)])


def swap_core(value):
    return lax.ppermute(value, "expert", [(i, i ^ 1) for i in range(8)])


def shift_up(value):
    return lax.ppermute(value, "expert", [(i, (i + 2) % 8) for i in range(8)])


def shift_down(value):
    return lax.ppermute(value, "expert", [(i, (i + 6) % 8) for i in range(8)])


def halves(value, axis):
    size = value.shape[axis]
    step = {1: 128, 2: 16}.get(value.ndim - axis, 1)
    cut = size // 2 // step * step
    return (
        lax.slice_in_dim(value, 0, cut, axis=axis),
        lax.slice_in_dim(value, cut, size, axis=axis),
    )


def gather_z(value, axis):
    below = shift_up(value)
    above = shift_down(value)
    far = jnp.concatenate(
        [shift_up(halves(below, axis)[0]), shift_down(halves(above, axis)[1])], axis=axis
    )
    return [value, below, above, far]


def gather_plane(value, axis):
    from_x = swap_x(value)
    from_y = swap_y(value)
    far = jnp.concatenate(
        [swap_x(halves(from_y, axis)[0]), swap_y(halves(from_x, axis)[1])], axis=axis
    )
    return [value, from_x, from_y, far]


def add_low(left, right):
    return (left.astype(jnp.float32) + right.astype(jnp.float32)).astype(jnp.bfloat16)


def scatter_z(blocks, axis):
    own, to_below, to_above, far = blocks
    far_a, far_b = halves(far, axis)
    up_a, up_b = halves(to_above, axis)
    down_a, down_b = halves(to_below, axis)
    got_a = shift_up(far_a)
    got_b = shift_down(far_b)
    up_b = shift_up(up_b)
    down_a = shift_down(down_a)
    up_a = shift_up(add_low(up_a, got_a))
    down_b = shift_down(add_low(down_b, got_b))
    first = jnp.concatenate([up_a, up_b], axis=axis).astype(jnp.float32)
    second = jnp.concatenate([down_a, down_b], axis=axis).astype(jnp.float32)
    return own.astype(jnp.float32) + first + second


def scatter_plane(blocks, axis):
    own, to_x, to_y, far = blocks
    far_a, far_b = halves(far, axis)
    x_a, x_b = halves(to_x, axis)
    y_a, y_b = halves(to_y, axis)
    got_a = swap_x(far_a)
    got_b = swap_y(far_b)
    x_a = swap_x(x_a)
    y_b = swap_y(y_b)
    x_b = swap_x(add_low(x_b, got_b))
    y_a = swap_y(add_low(y_a, got_a))
    first = jnp.concatenate([x_a, x_b], axis=axis).astype(jnp.float32)
    second = jnp.concatenate([y_a, y_b], axis=axis).astype(jnp.float32)
    return own.astype(jnp.float32) + first + second


def any_spec():
    return pl.BlockSpec(memory_space=pl.ANY)


def smem_spec():
    return pl.BlockSpec(memory_space=pltpu.SMEM)


def staged(out_ref, hold, sems):
    pltpu.make_async_copy(hold, hold, sems.at[0]).wait()
    copy = pltpu.make_async_copy(hold, out_ref, sems.at[1])
    copy.start()
    copy.wait()


def place_kernel(index_ref, src_ref, out_ref, hold, sems):
    for j in range(src_ref.shape[0]):
        pltpu.make_async_copy(src_ref.at[j], hold.at[index_ref[j]], sems.at[0]).start()
    staged(out_ref, hold, sems)


def take_kernel(index_ref, src_ref, out_ref, hold, sems):
    for j in range(src_ref.shape[0]):
        pltpu.make_async_copy(src_ref.at[index_ref[j]], hold.at[j], sems.at[0]).start()
    staged(out_ref, hold, sems)


def deal_kernel(seq_ref, rel_ref, src_ref, out_ref, hold, sems):
    devices = out_ref.shape[0]
    piece = out_ref.shape[1] // SEQ_DEV // devices
    for b in range(devices):
        for k in range(SEQ_DEV):
            row = pl.multiple_of(seq_ref[b * SEQ_DEV + k] * piece, piece)
            for j in range(devices):
                pltpu.make_async_copy(
                    src_ref.at[rel_ref[j], pl.ds(row, piece), :],
                    hold.at[b, pl.ds((k * devices + j) * piece, piece), :],
                    sems.at[0],
                ).start()
    staged(out_ref, hold, sems)


def move_blocks(kernel, shape, scalars, arrays):
    dtype = arrays[0].dtype
    return pl.pallas_call(
        kernel,
        out_shape=jax.ShapeDtypeStruct(shape, dtype),
        in_specs=[smem_spec()] * len(scalars) + [any_spec()] * len(arrays),
        out_specs=any_spec(),
        scratch_shapes=[pltpu.VMEM(shape, dtype), pltpu.SemaphoreType.DMA((2,))],
        compiler_params=pltpu.CompilerParams(vmem_limit_bytes=40 * 1024 * 1024),
    )(*scalars, *arrays)


def join_kernel(axis, index_ref, own_ref, x_ref, y_ref, a_ref, b_ref, out_ref, hold, sems):
    me = index_ref[0]
    step = own_ref.shape[axis]

    def window(e, owner):
        start = pl.multiple_of(owner * step, step)
        if axis == 1:
            return hold.at[e, pl.ds(start, step), :]
        return hold.at[e, :, pl.ds(start, step)]

    for e in range(2):
        pltpu.make_async_copy(own_ref.at[e], window(e, me), sems.at[0]).start()
        pltpu.make_async_copy(x_ref.at[e], window(e, me ^ 1), sems.at[0]).start()
        pltpu.make_async_copy(y_ref.at[e], window(e, me ^ 2), sems.at[0]).start()
    pltpu.make_async_copy(a_ref.at[0], window(0, me ^ 3), sems.at[0]).start()
    pltpu.make_async_copy(b_ref.at[0], window(1, me ^ 3), sems.at[0]).start()
    staged(out_ref, hold, sems)


def gather_experts(value, axis, tuned):
    if not tuned:
        return lax.all_gather(value, "dp", axis=axis, tiled=True)
    from_x = swap_x(value)
    from_y = swap_y(value)
    far_a = swap_x(from_y[:1])
    far_b = swap_y(from_x[1:])
    shape = list(value.shape)
    shape[axis] *= 4
    index = lax.axis_index("dp").reshape(1)
    return move_blocks(
        lambda *refs: join_kernel(axis, *refs),
        tuple(shape),
        [index],
        [value, from_x, from_y, far_a, far_b],
    )


def scatter_experts(value, axis, tuned):
    if not tuned:
        return lax.psum_scatter(value, "dp", scatter_dimension=axis, tiled=True).astype(jnp.float32)
    me = lax.axis_index("dp")
    step = value.shape[axis] // 4
    blocks = [
        lax.dynamic_slice_in_dim(value, (me ^ k) * step, step, axis=axis) for k in range(4)
    ]
    own, to_x, to_y, far = blocks
    got_a = swap_x(far[:1])
    got_b = swap_y(far[1:])
    x_a = swap_x(to_x[:1])
    y_b = swap_y(to_y[1:])
    x_b = swap_x(add_low(to_x[1:], got_b))
    y_a = swap_y(add_low(to_y[:1], got_a))
    first = jnp.concatenate([x_a, x_b], axis=0).astype(jnp.float32)
    second = jnp.concatenate([y_a, y_b], axis=0).astype(jnp.float32)
    return own.astype(jnp.float32) + first + second


def expert_order(tuned, count):
    if not tuned:
        return jnp.arange(count, dtype=jnp.int32)
    me = lax.axis_index("expert")
    level, core = me // 2, me % 2
    order = [
        ((level + off) % 4) * 2 + (core + flip) % 2 for flip in range(2) for off in (0, 3, 1, 2)
    ]
    return jnp.stack(order).astype(jnp.int32)


def gather_expert_axis(value, tuned):
    if not tuned:
        return lax.all_gather(value, "expert", axis=0, tiled=False)
    parts = jnp.stack(gather_z(value, 0))
    return jnp.concatenate([parts, swap_core(parts)], axis=0)


def scatter_expert_axis(blocks, tuned):
    if not tuned:
        return lax.psum_scatter(blocks, "expert", scatter_dimension=0, tiled=False).astype(
            jnp.float32
        )
    mine = add_low(blocks[:4], swap_core(blocks[4:]))
    return scatter_z([mine[0], mine[1], mine[2], mine[3]], 0)


def all_order():
    me = lax.axis_index("expert")
    plane = lax.axis_index("dp")
    level, core = me // 2, me % 2
    order = [
        ((plane ^ k) * 4 + (level + off) % 4) * 2 + (core + flip) % 2
        for flip in range(2)
        for k in range(4)
        for off in (0, 3, 1, 2)
    ]
    return jnp.stack(order).astype(jnp.int32)


def gather_all(value, tuned):
    if not tuned:
        return lax.all_gather(value, ("dp", "expert"), axis=0, tiled=True)
    level = jnp.stack(gather_z(value, 1))
    parts = jnp.stack(gather_plane(level, 0))
    parts = jnp.stack([parts, swap_core(parts)])
    parts = parts.reshape((32,) + value.shape)
    placed = move_blocks(place_kernel, parts.shape, [all_order()], [parts])
    return placed.reshape(32 * value.shape[0], value.shape[1])


def scatter_all(value, tuned):
    if not tuned:
        return lax.psum_scatter(value, ("dp", "expert"), scatter_dimension=0, tiled=True).astype(
            jnp.float32
        )
    rows = value.shape[0] // 32
    parts = value.reshape(32, rows, value.shape[1])
    parts = move_blocks(take_kernel, parts.shape, [all_order()], [parts])
    parts = parts.reshape(2, 4, 4, rows, value.shape[1])
    mine = add_low(parts[0], swap_core(parts[1]))
    level = scatter_plane([mine[0], mine[1], mine[2], mine[3]], 0).astype(jnp.bfloat16)
    return scatter_z([level[0], level[1], level[2], level[3]], 1)


def pad_columns(value, width):
    return jnp.pad(value, ((0, 0), (0, width - value.shape[1])))


def body(
    tokens,
    cotangent,
    lengths,
    placement,
    routes,
    priority,
    g_attn,
    w_query,
    key_projection,
    value_projection,
    w_out,
    g_moe,
    w_router,
    w_gate,
    w_up,
    w_down,
):
    row_seqs, piece_len, width = tokens.shape
    expert_devices = lax.axis_size("expert")
    tuned = expert_devices == 8 and lax.axis_size("dp") == 4
    my_index = lax.axis_index("expert")
    seq_len = piece_len * expert_devices
    token_count = SEQ_DEV * seq_len
    query_group_width = QUERY_HEADS // KEY_VALUE_HEADS
    query_width = w_query.shape[1]
    kv_width = key_projection.shape[1]
    expert_count = w_router.shape[1]
    per_device = expert_count // expert_devices
    capacity = (9 * token_count * TOPK + 64 * expert_count - 1) // (64 * expert_count) * 8
    score_scale = HEAD_SIZE ** (-0.5)
    code_list = jnp.arange(row_seqs, dtype=jnp.int32)
    source = jnp.sum(
        jnp.where(placement[:, None] == code_list[None, :], code_list[:, None], 0), axis=0
    )
    send_tokens = tokens[source].reshape(expert_devices, SEQ_DEV, piece_len, width)
    got_tokens = lax.all_to_all(send_tokens, "expert", split_axis=0, concat_axis=2, tiled=True)
    x_local = got_tokens.reshape(token_count, width).astype(jnp.float32)
    pack_in = jnp.concatenate(
        [w_query, key_projection, value_projection, pad_columns(g_attn[:, None], 128)], axis=1
    )
    pack_out = jnp.concatenate(
        [w_out, pad_columns(jnp.concatenate([w_router, g_moe[:, None]], axis=1), 128)], axis=1
    )
    full_in = gather_all(pack_in, tuned)
    full_out = gather_all(pack_out, tuned)
    query_full = full_in[:, :query_width]
    key_full = full_in[:, query_width : query_width + kv_width]
    value_full = full_in[:, query_width + kv_width : query_width + 2 * kv_width]
    gain_attn = full_in[:, query_width + 2 * kv_width].astype(jnp.float32)
    out_full = full_out[:, :width]
    router_full = full_out[:, width : width + expert_count]
    gain_moe = full_out[:, width + expert_count].astype(jnp.float32)
    ranks = slot_ranks(routes.reshape(-1), priority.reshape(-1)).reshape(token_count, TOPK)
    codes = jnp.minimum(ranks, capacity) + 1
    expert_list = jnp.arange(expert_count, dtype=jnp.int32)
    picks = routes[None, :, :] == expert_list[:, None, None]
    code_table = jnp.sum(jnp.where(picks, codes[None], 0), axis=2)
    table_rows = -(-expert_count // 16) * 16
    table = jnp.zeros((table_rows, width), jnp.bfloat16)
    table = table.at[:expert_count, :token_count].set(code_table.astype(jnp.bfloat16))
    early = jnp.concatenate([cotangent.reshape(token_count, width), table], axis=0)
    early_all = gather_expert_axis(early, tuned)
    order = expert_order(tuned, expert_devices)
    rel_of = jnp.zeros((expert_devices,), jnp.int32)
    for b in range(expert_devices):
        rel_of = jnp.where(jnp.arange(expert_devices) == order[b], b, rel_of)
    seqs = source.reshape(expert_devices, SEQ_DEV)[order].reshape(-1)
    if piece_len % 16 == 0:
        shape = (expert_devices, token_count, width)
        grads_all = move_blocks(deal_kernel, shape, [seqs, rel_of], [early_all])
    else:
        pieces = early_all[:, :token_count].reshape(expert_devices, row_seqs, piece_len, width)
        pieces = pieces[rel_of][:, seqs].reshape(
            expert_devices, expert_devices, SEQ_DEV, piece_len, width
        )
        grads_all = pieces.transpose(1, 2, 0, 3, 4).reshape(expert_devices, token_count, width)
    codes_all = early_all[:, token_count : token_count + expert_count, :token_count].astype(
        jnp.int32
    )
    own_codes = lax.dynamic_slice_in_dim(codes_all, my_index * per_device, per_device, axis=1)
    dy_local = grads_all[rel_of[my_index]].astype(jnp.float32)
    gate_full = gather_experts(w_gate, 1, tuned)
    up_full = gather_experts(w_up, 1, tuned)
    down_full = gather_experts(w_down, 2, tuned)

    own_seqs = lax.dynamic_slice_in_dim(source, my_index * SEQ_DEV, SEQ_DEV)
    positions, labels = device_layout(lengths[own_seqs], seq_len)
    cosine_table, sine_values = rope_tables(positions, HEAD_SIZE)
    token_steps = jnp.arange(token_count, dtype=jnp.int32)
    allowed = jnp.logical_and(
        labels[:, None] == labels[None, :], token_steps[:, None] >= token_steps[None, :]
    )
    inv_attn = lax.rsqrt(jnp.mean(x_local * x_local, axis=-1, keepdims=True) + EPSILON)
    normed_attn = (x_local * inv_attn * gain_attn).astype(jnp.bfloat16)
    query_raw = jnp.dot(normed_attn, query_full, preferred_element_type=jnp.float32)
    key_unrotated = jnp.dot(normed_attn, key_full, preferred_element_type=jnp.float32)
    value_low = (
        jnp.dot(normed_attn, value_full, preferred_element_type=jnp.float32)
        .astype(jnp.bfloat16)
        .reshape(token_count, KEY_VALUE_HEADS, HEAD_SIZE)
    )
    query_rotated = (
        apply_rotation(
            query_raw.reshape(token_count, QUERY_HEADS, HEAD_SIZE), cosine_table, sine_values
        )
        .astype(jnp.bfloat16)
        .reshape(token_count, KEY_VALUE_HEADS, query_group_width, HEAD_SIZE)
    )
    key_rotated = apply_rotation(
        key_unrotated.reshape(token_count, KEY_VALUE_HEADS, HEAD_SIZE), cosine_table, sine_values
    ).astype(jnp.bfloat16)

    def masked_scores():
        raw_scores = (
            jnp.einsum(
                "qhgd,khd->hgqk", query_rotated, key_rotated, preferred_element_type=jnp.float32
            )
            * score_scale
        )
        return jnp.where(allowed, raw_scores, NEG_FILL)

    scores = masked_scores()
    score_top = jnp.max(scores, axis=-1, keepdims=True)
    exp_scores = jnp.exp(scores - score_top)
    totals = jnp.sum(exp_scores, axis=-1, keepdims=True)
    attn_probs = exp_scores / totals
    log_totals = score_top + jnp.log(totals)
    mixed_heads = jnp.einsum(
        "hgqk,khd->qhgd",
        attn_probs.astype(jnp.bfloat16),
        value_low,
        preferred_element_type=jnp.float32,
    )
    mixed_low = mixed_heads.reshape(token_count, QUERY_HEADS * HEAD_SIZE).astype(jnp.bfloat16)
    residual = x_local + jnp.dot(mixed_low, out_full, preferred_element_type=jnp.float32)
    inv_moe = lax.rsqrt(jnp.mean(residual * residual, axis=-1, keepdims=True) + EPSILON)
    normed_moe = (residual * inv_moe * gain_moe).astype(jnp.bfloat16)
    normed_all = gather_expert_axis(normed_moe, tuned)
    logits_all = jnp.einsum(
        "btd,de->bet", normed_all, router_full, preferred_element_type=jnp.float32
    )
    chosen_all = codes_all > 0
    top_all = jnp.max(jnp.where(chosen_all, logits_all, NEG_FILL), axis=1, keepdims=True)
    exp_all = jnp.where(chosen_all, jnp.exp(logits_all - top_all), 0.0)
    gates_all = exp_all / jnp.sum(exp_all, axis=1, keepdims=True)
    own_gates = lax.dynamic_slice_in_dim(gates_all, my_index * per_device, per_device, axis=1)
    my_block = rel_of[my_index]
    gates = gates_all[my_block]
    chosen = chosen_all[my_block]
    slot_list = jnp.arange(capacity, dtype=jnp.int32) + 1
    slot_hit = own_codes[:, :, None, :] == slot_list[None, None, :, None]
    slot_gate = jnp.sum(jnp.where(slot_hit, own_gates[:, :, None, :], 0.0), axis=-1)
    slot_one = slot_hit.astype(jnp.bfloat16)
    inbound = jnp.einsum(
        "blrt,btd->lbrd", slot_one, normed_all, preferred_element_type=jnp.float32
    ).astype(jnp.bfloat16)
    grad_slots = jnp.einsum(
        "blrt,btd->lbrd", slot_one, grads_all, preferred_element_type=jnp.float32
    )
    slot_gate = jnp.swapaxes(slot_gate, 0, 1)[..., None]
    pre_gate = jnp.einsum("lbrd,ldf->lbrf", inbound, gate_full, preferred_element_type=jnp.float32)
    pre_up = jnp.einsum("lbrd,ldf->lbrf", inbound, up_full, preferred_element_type=jnp.float32)
    activated, gelu_pull = jax.vjp(jax.nn.gelu, pre_gate)
    hidden = (activated * pre_up).astype(jnp.bfloat16)
    expert_out = (
        jnp.einsum("lbrf,lfd->lbrd", hidden, down_full, preferred_element_type=jnp.float32)
        .astype(jnp.bfloat16)
        .astype(jnp.float32)
    )
    grad_gate_slot = jnp.sum(grad_slots * expert_out, axis=-1)
    weighted = (slot_gate * expert_out).astype(jnp.bfloat16)
    back_out = jnp.einsum(
        "blrt,lbrd->btd", slot_one, weighted, preferred_element_type=jnp.float32
    ).astype(jnp.bfloat16)
    gate_grads = jnp.einsum(
        "blrt,lbr->blt",
        slot_hit.astype(jnp.float32),
        grad_gate_slot,
        precision=lax.Precision.HIGHEST,
        preferred_element_type=jnp.float32,
    )
    high = gate_grads.astype(jnp.bfloat16)
    low = (gate_grads - high.astype(jnp.float32)).astype(jnp.bfloat16)
    both = jnp.concatenate([high, low], axis=2)
    grad_table = jnp.zeros((expert_devices, table_rows, width), jnp.bfloat16)
    grad_table = lax.dynamic_update_slice(
        grad_table, both, (0, my_index * per_device, 0)
    )
    summed = scatter_expert_axis(jnp.concatenate([back_out, grad_table], axis=1), tuned)
    out_low = (residual + summed[:token_count]).astype(jnp.bfloat16)
    grad_pair = (
        summed[token_count : token_count + expert_count, :token_count]
        + summed[token_count : token_count + expert_count, token_count : 2 * token_count]
    )
    grad_inbound = (slot_gate * grad_slots).astype(jnp.bfloat16)
    grad_down = jnp.einsum(
        "lbrf,lbrd->lfd", hidden, grad_inbound, preferred_element_type=jnp.float32
    ).astype(jnp.bfloat16)
    grad_hidden = jnp.einsum(
        "lbrd,lfd->lbrf", grad_inbound, down_full, preferred_element_type=jnp.float32
    )
    grad_pre_gate = gelu_pull(grad_hidden * pre_up)[0].astype(jnp.bfloat16)
    grad_pre_up = (grad_hidden * activated).astype(jnp.bfloat16)
    grad_inputs = jnp.einsum(
        "lbrf,ldf->lbrd", grad_pre_gate, gate_full, preferred_element_type=jnp.float32
    )
    grad_inputs = (
        grad_inputs
        + jnp.einsum("lbrf,ldf->lbrd", grad_pre_up, up_full, preferred_element_type=jnp.float32)
    ).astype(jnp.bfloat16)
    back_grad = jnp.einsum(
        "blrt,lbrd->btd", slot_one, grad_inputs, preferred_element_type=jnp.float32
    ).astype(jnp.bfloat16)
    grad_moe = scatter_expert_axis(back_grad, tuned)
    grad_gate = jnp.einsum(
        "lbrd,lbrf->ldf", inbound, grad_pre_gate, preferred_element_type=jnp.float32
    ).astype(jnp.bfloat16)
    grad_up = jnp.einsum(
        "lbrd,lbrf->ldf", inbound, grad_pre_up, preferred_element_type=jnp.float32
    ).astype(jnp.bfloat16)
    owned_down = scatter_experts(grad_down, 2, tuned)
    owned_gate = scatter_experts(grad_gate, 1, tuned)
    owned_up = scatter_experts(grad_up, 1, tuned)
    grad_chosen = gates * (grad_pair - jnp.sum(gates * grad_pair, axis=0, keepdims=True))
    grad_logits = jnp.where(chosen, grad_chosen, 0.0).T.astype(jnp.bfloat16)
    grad_router = contract(normed_moe, grad_logits, (0,), (0,))
    grad_normed_moe = contract(grad_logits, router_full, (1,), (1,)) + grad_moe
    grad_gain_moe, grad_through = norm_back(residual, inv_moe, gain_moe, grad_normed_moe)
    grad_residual = dy_local + grad_through
    grad_attn = grad_residual.astype(jnp.bfloat16)
    grad_out = contract(mixed_low, grad_attn, (0,), (0,))
    side_out = jnp.concatenate([grad_router, grad_gain_moe[:, None]], axis=1)
    owned_out = scatter_all(
        jnp.concatenate([grad_out, pad_columns(side_out, 128)], axis=1).astype(jnp.bfloat16), tuned
    )
    grad_mixed = (
        contract(grad_attn, out_full, (1,), (1,))
        .astype(jnp.bfloat16)
        .reshape(token_count, KEY_VALUE_HEADS, query_group_width, HEAD_SIZE)
    )
    probs_again = jnp.exp(masked_scores() - log_totals)
    grad_probs = jnp.einsum(
        "qhgd,khd->hgqk", grad_mixed, value_low, preferred_element_type=jnp.float32
    )
    value_weight_gradient = jnp.einsum(
        "hgqk,qhgd->khd",
        probs_again.astype(jnp.bfloat16),
        grad_mixed,
        preferred_element_type=jnp.float32,
    )
    inner_sum = jnp.sum(probs_again * grad_probs, axis=-1, keepdims=True)
    grad_scores = (probs_again * (grad_probs - inner_sum)).astype(jnp.bfloat16)
    grad_query_rot = (
        jnp.einsum("hgqk,khd->qhgd", grad_scores, key_rotated, preferred_element_type=jnp.float32)
        * score_scale
    )
    grad_key_rot = (
        jnp.einsum("hgqk,qhgd->khd", grad_scores, query_rotated, preferred_element_type=jnp.float32)
        * score_scale
    )
    grad_query_low = (
        rotate_back(
            grad_query_rot.reshape(token_count, QUERY_HEADS, HEAD_SIZE), cosine_table, sine_values
        )
        .reshape(token_count, QUERY_HEADS * HEAD_SIZE)
        .astype(jnp.bfloat16)
    )
    grad_key_low = (
        rotate_back(grad_key_rot, cosine_table, sine_values)
        .reshape(token_count, KEY_VALUE_HEADS * HEAD_SIZE)
        .astype(jnp.bfloat16)
    )
    value_gradient_narrow = value_weight_gradient.reshape(
        token_count, KEY_VALUE_HEADS * HEAD_SIZE
    ).astype(jnp.bfloat16)
    grad_query = contract(normed_attn, grad_query_low, (0,), (0,))
    grad_key = contract(normed_attn, grad_key_low, (0,), (0,))
    grad_value_w = contract(normed_attn, value_gradient_narrow, (0,), (0,))
    grad_normed_attn = contract(grad_query_low, query_full, (1,), (1,))
    grad_normed_attn = grad_normed_attn + contract(grad_key_low, key_full, (1,), (1,))
    grad_normed_attn = grad_normed_attn + contract(value_gradient_narrow, value_full, (1,), (1,))
    grad_gain_attn, grad_through_attn = norm_back(x_local, inv_attn, gain_attn, grad_normed_attn)
    grad_x = (grad_residual + grad_through_attn).astype(jnp.bfloat16)
    owned_in = scatter_all(
        jnp.concatenate(
            [grad_query, grad_key, grad_value_w, pad_columns(grad_gain_attn[:, None], 128)], axis=1
        ).astype(jnp.bfloat16),
        tuned,
    )
    deal_out, deal_grad = (
        lax.all_to_all(
            out_low.reshape(1, SEQ_DEV, seq_len, width),
            "expert",
            split_axis=2,
            concat_axis=0,
            tiled=True,
        ),
        lax.all_to_all(
            grad_x.reshape(1, SEQ_DEV, seq_len, width),
            "expert",
            split_axis=2,
            concat_axis=0,
            tiled=True,
        ),
    )
    output = deal_out.reshape(row_seqs, piece_len, width)[placement]
    input_grad = deal_grad.reshape(row_seqs, piece_len, width)[placement]
    return (
        output,
        input_grad,
        owned_in[:, query_width + 2 * kv_width],
        owned_in[:, :query_width],
        owned_in[:, query_width : query_width + kv_width],
        owned_in[:, query_width + kv_width : query_width + 2 * kv_width],
        owned_out[:, :width],
        owned_out[:, width + expert_count],
        owned_out[:, width : width + expert_count],
        owned_gate,
        owned_up,
        owned_down,
    )


def solution(mesh):
    return jax.shard_map(
        body,
        mesh=mesh,
        in_specs=(
            P("dp", "expert", None),
            P("dp", "expert", None),
            P("dp", None),
            P("dp"),
            P(("dp", "expert"), None),
            P(("dp", "expert"), None),
            P(("dp", "expert")),
            P(("dp", "expert"), None),
            P(("dp", "expert"), None),
            P(("dp", "expert"), None),
            P(("dp", "expert"), None),
            P(("dp", "expert")),
            P(("dp", "expert"), None),
            P("expert", "dp", None),
            P("expert", "dp", None),
            P("expert", None, "dp"),
        ),
        out_specs=(
            P("dp", "expert", None),
            P("dp", "expert", None),
            P(("dp", "expert")),
            P(("dp", "expert"), None),
            P(("dp", "expert"), None),
            P(("dp", "expert"), None),
            P(("dp", "expert"), None),
            P(("dp", "expert")),
            P(("dp", "expert"), None),
            P("expert", "dp", None),
            P("expert", "dp", None),
            P("expert", None, "dp"),
        ),
        check_vma=False,
    )
```

```python
import math

import jax
import jax.numpy as jnp
from jax import lax
from jax.experimental import pallas as pl
from jax.experimental.pallas import tpu as pltpu
from jax.sharding import PartitionSpec as P

QUERY_HEADS = 12
KEY_VALUE_HEADS = 2
HEAD_SIZE = 128
TOPK = 4
SEQ_DEV = 2


EPSILON = 1e-06
ROPE_BASE = 1000000.0
NEG_FILL = -1e30


def sequence_layout(doc_lens, seq_len):
    token_steps = jnp.arange(seq_len, dtype=jnp.int32)
    doc_ends = jnp.cumsum(doc_lens)
    doc_index = jnp.sum((token_steps[:, None] >= doc_ends[None, :-1]).astype(jnp.int32), axis=1)
    doc_starts = doc_ends - doc_lens
    doc_slots = jnp.arange(doc_lens.shape[0], dtype=jnp.int32)
    start_of = jnp.sum(
        jnp.where(doc_slots[None, :] == doc_index[:, None], doc_starts[None, :], 0), axis=1
    )
    return ((token_steps - start_of).astype(jnp.float32), doc_index)


def device_layout(dev_lens, seq_len):
    positions, doc_index = jax.vmap(lambda single: sequence_layout(single, seq_len))(dev_lens)
    doc_count = dev_lens.shape[1]
    labels = doc_index + doc_count * jnp.arange(dev_lens.shape[0], dtype=jnp.int32)[:, None]
    return (positions.reshape(-1), labels.reshape(-1))


def rope_tables(positions, head_dim):
    freq_index = jnp.arange(head_dim // 2, dtype=jnp.float32)
    frequency = jnp.exp(freq_index * (-2.0 / head_dim) * math.log(ROPE_BASE))
    angle_table = positions[:, None] * frequency[None, :]
    return (jnp.cos(angle_table), jnp.sin(angle_table))


def slot_ranks(route_flat, prio_flat):
    same = route_flat[:, None] == route_flat[None, :]
    ahead = prio_flat[None, :] < prio_flat[:, None]
    return jnp.sum(jnp.logical_and(same, ahead).astype(jnp.int32), axis=1)


def swap_x(value):
    return lax.ppermute(value, "dp", [(i, i ^ 1) for i in range(4)])


def swap_y(value):
    return lax.ppermute(value, "dp", [(i, i ^ 2) for i in range(4)])


def swap_core(value):
    return lax.ppermute(value, "expert", [(i, i ^ 1) for i in range(8)])


def shift_up(value):
    return lax.ppermute(value, "expert", [(i, (i + 2) % 8) for i in range(8)])


def shift_down(value):
    return lax.ppermute(value, "expert", [(i, (i + 6) % 8) for i in range(8)])


def add_low(left, right):
    return (left.astype(jnp.float32) + right.astype(jnp.float32)).astype(jnp.bfloat16)


def any_spec():
    return pl.BlockSpec(memory_space=pl.ANY)


def smem_spec():
    return pl.BlockSpec(memory_space=pltpu.SMEM)


def staged(out_ref, hold, sems):
    pltpu.make_async_copy(hold, hold, sems.at[0]).wait()
    copy = pltpu.make_async_copy(hold, out_ref, sems.at[1])
    copy.start()
    copy.wait()


def deal_kernel(seq_ref, rel_ref, src_ref, out_ref, hold, sems):
    devices = out_ref.shape[0]
    piece = out_ref.shape[1] // SEQ_DEV // devices
    for b in range(devices):
        for k in range(SEQ_DEV):
            row = pl.multiple_of(seq_ref[b * SEQ_DEV + k] * piece, piece)
            for j in range(devices):
                pltpu.make_async_copy(
                    src_ref.at[rel_ref[j], pl.ds(row, piece), :],
                    hold.at[b, pl.ds((k * devices + j) * piece, piece), :],
                    sems.at[0],
                ).start()
    staged(out_ref, hold, sems)


def move_blocks(kernel, shape, scalars, arrays):
    dtype = arrays[0].dtype
    return pl.pallas_call(
        kernel,
        out_shape=jax.ShapeDtypeStruct(shape, dtype),
        in_specs=[smem_spec()] * len(scalars) + [any_spec()] * len(arrays),
        out_specs=any_spec(),
        scratch_shapes=[pltpu.VMEM(shape, dtype), pltpu.SemaphoreType.DMA((2,))],
        compiler_params=pltpu.CompilerParams(vmem_limit_bytes=40 * 1024 * 1024),
    )(*scalars, *arrays)


def expert_order(tuned, count):
    if not tuned:
        return jnp.arange(count, dtype=jnp.int32)
    me = lax.axis_index("expert")
    level, core = me // 2, me % 2
    order = [
        ((level + off) % 4) * 2 + (core + flip) % 2 for flip in range(2) for off in (0, 3, 1, 2)
    ]
    return jnp.stack(order).astype(jnp.int32)


def all_order():
    me = lax.axis_index("expert")
    plane = lax.axis_index("dp")
    level, core = me // 2, me % 2
    order = [
        ((plane ^ k) * 4 + (level + off) % 4) * 2 + (core + flip) % 2
        for flip in range(2)
        for k in range(4)
        for off in (0, 3, 1, 2)
    ]
    return jnp.stack(order).astype(jnp.int32)


def dot_nn(left, right):
    return lax.dot_general(
        left, right, (((1,), (0,)), ((), ())), preferred_element_type=jnp.float32
    )


def dot_nt(left, right):
    return lax.dot_general(
        left, right, (((1,), (1,)), ((), ())), preferred_element_type=jnp.float32
    )


def dot_tn(left, right):
    return lax.dot_general(
        left, right, (((0,), (0,)), ((), ())), preferred_element_type=jnp.float32
    )


GELU_SCALE = math.sqrt(2.0 / math.pi)
GELU_CUBE = 0.044715
MIB = 1024 * 1024


def expert_kernel(plan, capacity, *refs):
    count = plan["inputs"]
    my_ref, codes_ref, router_ref, grads_ref = refs[:4]
    inputs = refs[4 : 4 + count]
    (
        back_keep,
        back_send,
        out_keep,
        out_send,
        x_out,
        dy_out,
        hid_out,
        dga_out,
        dua_out,
    ) = refs[4 + count : 13 + count]
    (
        gate_w,
        up_w,
        down_w,
        h_buf,
        d_buf,
        hot,
        x_s,
        dy_s,
        y_s,
        dx_s,
        hid_s,
        dga_s,
        dua_s,
        act_s,
        slope_s,
        code_s,
        gates_s,
        sgate_s,
        dg_s,
        stage_b,
        stage_o,
        sem_w,
        sem_h,
        sem_d,
        sem_s,
        sem_b,
        sem_o,
    ) = refs[13 + count :]
    blocks = plan["blocks"]
    pairs = blocks // 2
    per_device, width, ff = gate_w.shape
    tokens = h_buf.shape[1] // 2
    slots = 2 * capacity
    experts = codes_ref.shape[1]
    my_first = my_ref[0] * per_device
    dtype = jnp.bfloat16

    def window(hold, axis, e, owner, step):
        start = (owner or 0) * step
        if axis == 1:
            return hold.at[e, pl.ds(start, step), :]
        return hold.at[e, :, pl.ds(start, step)]

    weight_copies = []
    for t, (hold, axis) in enumerate(((gate_w, 1), (up_w, 1), (down_w, 2))):
        for e in range(per_device):
            copies = []
            for ref_index, lead, owner in plan["weights"][t][e]:
                src = inputs[ref_index].at[lead]
                step = src.shape[axis - 1]
                sem = sem_w.at[t * per_device + e, len(copies)]
                copy = pltpu.make_async_copy(src, window(hold, axis, e, owner, step), sem)
                copy.start()
                copies.append(copy)
            weight_copies.append(copies)

    def fetch(p):
        slot = p % 2
        copies = []
        for half in range(2):
            for k, (ref_index, lead, row, rows) in enumerate(plan["tokens"][2 * p + half]):
                src = inputs[ref_index] if lead is None else inputs[ref_index].at[lead]
                dst = h_buf.at[slot, pl.ds(half * tokens + row, rows), :]
                copies.append(pltpu.make_async_copy(src, dst, sem_h.at[slot, half, k]))
            dst = d_buf.at[slot, pl.ds(half * tokens, tokens), :]
            copies.append(pltpu.make_async_copy(grads_ref.at[2 * p + half], dst, sem_d.at[slot, half]))
        for copy in copies:
            copy.start()
        return copies

    row = lax.broadcasted_iota(jnp.int32, (slots, 2 * tokens), 0)
    col = lax.broadcasted_iota(jnp.int32, (slots, 2 * tokens), 1)
    second = row >= capacity
    same = jnp.logical_xor(second, col < tokens)
    target = (row - jnp.where(second, capacity, 0) + 1).astype(jnp.float32)
    flying = fetch(0)
    for p in range(pairs):
        slot = p % 2
        later = fetch(p + 1) if p + 1 < pairs else []
        for copy in flying:
            copy.wait()
        flying = later
        codes = jnp.concatenate([codes_ref[2 * p], codes_ref[2 * p + 1]], axis=1)
        logits = dot_nt(router_ref[...], h_buf[slot])
        chosen = codes > 0.0
        top = jnp.max(jnp.where(chosen, logits, NEG_FILL), axis=0, keepdims=True)
        raised = jnp.where(chosen, jnp.exp(logits - top), 0.0)
        code_s[...] = codes
        gates_s[...] = raised / jnp.sum(raised, axis=0, keepdims=True)
        for e in range(per_device):
            code_row = code_s[pl.ds(my_first + e, 1), :]
            gate_row = gates_s[pl.ds(my_first + e, 1), :]
            hit = jnp.logical_and(same, code_row == target)
            one = jnp.where(hit, 1.0, 0.0).astype(dtype)
            hot[e, p] = one
            gate_slot = jnp.sum(jnp.where(hit, gate_row, 0.0), axis=1, keepdims=True)
            rows = pl.ds(p * slots, slots)
            sgate_s[e, rows, :] = jnp.broadcast_to(gate_slot, (slots, 128))
            x_s[e, rows, :] = dot_nn(one, h_buf[slot]).astype(dtype)
            dy_s[e, rows, :] = dot_nn(one, d_buf[slot]).astype(dtype)

    saves = []
    for e in range(per_device):
        for copy in weight_copies[e] + weight_copies[per_device + e]:
            copy.wait()
        save = pltpu.make_async_copy(x_s.at[e], x_out.at[e], sem_s.at[0, e])
        save.start()
        saves.append(save)
        gate_slot = sgate_s[e][:, :1]

        @pl.loop(0, ff // 256)
        def _(j):
            cols = pl.ds(pl.multiple_of(j * 256, 256), 256)
            ga = dot_nn(x_s[e], gate_w[e, :, cols])
            ua = dot_nn(x_s[e], up_w[e, :, cols])
            square = ga * ga
            tan = jnp.tanh(GELU_SCALE * (ga + GELU_CUBE * square * ga))
            act = 0.5 * ga * (1.0 + tan)
            slope = 0.5 * (1.0 + tan) + 0.5 * ga * (1.0 - tan * tan) * GELU_SCALE * (
                1.0 + 3.0 * GELU_CUBE * square
            )
            act_s[:, cols] = act
            slope_s[:, cols] = ua * slope
            hid_s[e, :, cols] = (act * ua).astype(dtype)

        save = pltpu.make_async_copy(hid_s.at[e], hid_out.at[e], sem_s.at[1, e])
        save.start()
        saves.append(save)
        for copy in weight_copies[2 * per_device + e]:
            copy.wait()
        dg_s[e] = jnp.zeros(dg_s.shape[1:], jnp.float32)

        @pl.loop(0, width // 256)
        def _(j):
            cols = pl.ds(pl.multiple_of(j * 256, 256), 256)
            y = dot_nn(hid_s[e], down_w[e, :, cols]).astype(dtype).astype(jnp.float32)
            dy = dy_s[e, :, cols].astype(jnp.float32)
            dg_s[e] += jnp.broadcast_to(
                jnp.sum(dy * y, axis=1, keepdims=True), dg_s.shape[1:]
            )
            y_s[e, :, cols] = (gate_slot * y).astype(dtype)
            dy_s[e, :, cols] = (gate_slot * dy).astype(dtype)

        save = pltpu.make_async_copy(dy_s.at[e], dy_out.at[e], sem_s.at[2, e])
        save.start()
        saves.append(save)

        @pl.loop(0, ff // 256)
        def _(j):
            cols = pl.ds(pl.multiple_of(j * 256, 256), 256)
            dhid = dot_nt(dy_s[e], down_w[e, cols, :])
            dga_s[e, :, cols] = (dhid * slope_s[:, cols]).astype(dtype)
            dua_s[e, :, cols] = (dhid * act_s[:, cols]).astype(dtype)

        for k, (hold, out) in enumerate(((dga_s, dga_out), (dua_s, dua_out))):
            save = pltpu.make_async_copy(hold.at[e], out.at[e], sem_s.at[3 + k, e])
            save.start()
            saves.append(save)

        @pl.loop(0, width // 256)
        def _(j):
            cols = pl.ds(pl.multiple_of(j * 256, 256), 256)
            dx = dot_nt(dga_s[e], gate_w[e, cols, :]) + dot_nt(dua_s[e], up_w[e, cols, :])
            dx_s[e, :, cols] = dx.astype(dtype)

    table_rows = stage_b.shape[2] - tokens
    table_row = lax.broadcasted_iota(jnp.int32, (table_rows, 2 * tokens), 0)
    sends = {}
    for p in range(pairs):
        slot = p % 2
        for copy in sends.pop(p - 2, []):
            copy.wait()
        rows = pl.ds(p * slots, slots)

        @pl.loop(0, width // 512)
        def _(j):
            cols = pl.ds(pl.multiple_of(j * 512, 512), 512)
            back = jnp.zeros((2 * tokens, 512), jnp.float32)
            outs = jnp.zeros((2 * tokens, 512), jnp.float32)
            for e in range(per_device):
                back += dot_tn(hot[e, p], dx_s[e, rows, cols])
                outs += dot_tn(hot[e, p], y_s[e, rows, cols])
            for half in range(2):
                part = slice(half * tokens, (half + 1) * tokens)
                stage_b[slot, half, :tokens, cols] = back[part].astype(dtype)
                stage_o[slot, half, :, cols] = outs[part].astype(dtype)

        tables = [jnp.zeros((table_rows, 2 * tokens), jnp.float32) for _ in range(2)]
        for e in range(per_device):
            dg = dg_s[e, rows, :][:, :1]
            line = jnp.sum(hot[e, p].astype(jnp.float32) * dg, axis=0, keepdims=True)
            mine = table_row == my_first + e
            for half in range(2):
                part = line[:, half * tokens : (half + 1) * tokens]
                high = part.astype(dtype).astype(jnp.float32)
                both = jnp.concatenate([high, part - high], axis=1)
                tables[half] = jnp.where(mine, both, tables[half])
        for half in range(2):
            stage_b[slot, half, tokens:, : 2 * tokens] = tables[half].astype(dtype)
            stage_b[slot, half, tokens:, 2 * tokens :] = jnp.zeros(
                (table_rows, width - 2 * tokens), dtype
            )
        first = 2 * p
        keep = first < blocks // 2
        at = pl.ds(first if keep else first - blocks // 2, 2)
        copies = [
            pltpu.make_async_copy(
                stage_b.at[slot], (back_keep if keep else back_send).at[at], sem_b.at[slot]
            ),
            pltpu.make_async_copy(
                stage_o.at[slot], (out_keep if keep else out_send).at[at], sem_o.at[slot]
            ),
        ]
        for copy in copies:
            copy.start()
        sends[p] = copies
    for copies in sends.values():
        for copy in copies:
            copy.wait()
    for save in saves:
        save.wait()


def run_experts(plan, capacity, table_rows, scalars, codes, router_t, grads_all, inputs):
    blocks, tokens, width = grads_all.shape
    experts = codes.shape[1]
    per_device, ff = plan["per_device"], plan["ff"]
    rows = blocks * capacity
    bf, f32 = jnp.bfloat16, jnp.float32
    half = blocks // 2
    back = jax.ShapeDtypeStruct((half, tokens + table_rows, width), bf)
    outs = jax.ShapeDtypeStruct((half, tokens, width), bf)
    wide = jax.ShapeDtypeStruct((per_device, rows, width), bf)
    thin = jax.ShapeDtypeStruct((per_device, rows, ff), bf)
    vmem = pl.BlockSpec(memory_space=pltpu.VMEM)
    sem = pltpu.SemaphoreType.DMA
    return pl.pallas_call(
        lambda *refs: expert_kernel(plan, capacity, *refs),
        out_shape=(back, back, outs, outs, wide, wide, thin, thin, thin),
        in_specs=[smem_spec(), vmem, vmem, any_spec()] + [any_spec()] * len(inputs),
        out_specs=tuple([any_spec()] * 9),
        scratch_shapes=[
            pltpu.VMEM((per_device, width, ff), bf),
            pltpu.VMEM((per_device, width, ff), bf),
            pltpu.VMEM((per_device, ff, width), bf),
            pltpu.VMEM((2, 2 * tokens, width), bf),
            pltpu.VMEM((2, 2 * tokens, width), bf),
            pltpu.VMEM((per_device, blocks // 2, 2 * capacity, 2 * tokens), bf),
            pltpu.VMEM((per_device, rows, width), bf),
            pltpu.VMEM((per_device, rows, width), bf),
            pltpu.VMEM((per_device, rows, width), bf),
            pltpu.VMEM((per_device, rows, width), bf),
            pltpu.VMEM((per_device, rows, ff), bf),
            pltpu.VMEM((per_device, rows, ff), bf),
            pltpu.VMEM((per_device, rows, ff), bf),
            pltpu.VMEM((rows, ff), f32),
            pltpu.VMEM((rows, ff), f32),
            pltpu.VMEM((experts, 2 * tokens), f32),
            pltpu.VMEM((experts, 2 * tokens), f32),
            pltpu.VMEM((per_device, rows, 128), f32),
            pltpu.VMEM((per_device, rows, 128), f32),
            pltpu.VMEM((2, 2, tokens + table_rows, width), bf),
            pltpu.VMEM((2, 2, tokens, width), bf),
            sem((3 * per_device, 4)),
            sem((2, 2, 2)),
            sem((2, 2)),
            sem((5, per_device)),
            sem((2,)),
            sem((2,)),
        ],
        cost_estimate=pl.CostEstimate(flops=55000000000, transcendentals=0, bytes_accessed=50000000),
        compiler_params=pltpu.CompilerParams(vmem_limit_bytes=61 * MIB),
    )(scalars, codes, router_t, grads_all, *inputs)


def down_kernel(hid_ref, dy_ref, out_ref):
    out_ref[0, 0] = dot_tn(hid_ref[0], dy_ref[0]).astype(jnp.bfloat16)


def grad_down_blocks(hid, dy, parts):
    per_device, rows, ff = hid.shape
    step = dy.shape[2] // parts
    return pl.pallas_call(
        down_kernel,
        grid=(per_device, parts),
        out_shape=jax.ShapeDtypeStruct((parts, per_device, ff, step), jnp.bfloat16),
        in_specs=[
            pl.BlockSpec((1, rows, ff), lambda e, d: (e, 0, 0)),
            pl.BlockSpec((1, rows, step), lambda e, d: (e, 0, d)),
        ],
        out_specs=pl.BlockSpec((1, 1, ff, step), lambda e, d: (d, e, 0, 0)),
        cost_estimate=pl.CostEstimate(flops=7700000000, transcendentals=0, bytes_accessed=7000000),
        compiler_params=pltpu.CompilerParams(vmem_limit_bytes=40 * MIB),
    )(hid, dy)


def gate_up_kernel(x_ref, dga_ref, dua_ref, out_ref):
    out_ref[0, 0, 0] = dot_tn(x_ref[0], dga_ref[0]).astype(jnp.bfloat16)
    out_ref[0, 1, 0] = dot_tn(x_ref[0], dua_ref[0]).astype(jnp.bfloat16)


def grad_gate_up_blocks(x, dga, dua, parts):
    per_device, rows, ff = dga.shape
    step = x.shape[2] // parts
    return pl.pallas_call(
        gate_up_kernel,
        grid=(per_device, parts),
        out_shape=jax.ShapeDtypeStruct((parts, 2, per_device, step, ff), jnp.bfloat16),
        in_specs=[
            pl.BlockSpec((1, rows, step), lambda e, d: (e, 0, d)),
            pl.BlockSpec((1, rows, ff), lambda e, d: (e, 0, 0)),
            pl.BlockSpec((1, rows, ff), lambda e, d: (e, 0, 0)),
        ],
        out_specs=pl.BlockSpec((1, 2, 1, step, ff), lambda e, d: (d, 0, e, 0, 0)),
        cost_estimate=pl.CostEstimate(flops=11000000000, transcendentals=0, bytes_accessed=10000000),
        compiler_params=pltpu.CompilerParams(vmem_limit_bytes=40 * MIB),
    )(x, dga, dua)


def gather_weight_pieces(w_gate, w_up, w_down, tuned):
    if not tuned:
        parts = [
            lax.all_gather(w_gate, "dp", axis=1, tiled=True),
            lax.all_gather(w_up, "dp", axis=1, tiled=True),
            lax.all_gather(w_down, "dp", axis=2, tiled=True),
        ]
        count = w_gate.shape[0]
        return parts, [[[(t, (e,), None)] for e in range(count)] for t in range(3)]
    both = jnp.stack([w_gate, w_up])
    flat = lax.all_gather(both.reshape(-1, both.shape[-1]), "dp", axis=0, tiled=True)
    down = lax.all_gather(w_down.reshape(-1, w_down.shape[-1]), "dp", axis=0, tiled=True)
    parts = [flat.reshape((4,) + both.shape), down.reshape((4,) + w_down.shape)]
    places = [
        [[(0, (d, t, e), d) for d in range(4)] for e in range(w_gate.shape[0])] for t in range(2)
    ]
    places.append([[(1, (d, e), d) for d in range(4)] for e in range(w_gate.shape[0])])
    return parts, places


def gather_token_pieces(value, tuned, wait_for):
    rows = value.shape[0]
    if not tuned:
        full = lax.all_gather(value, "expert", axis=0, tiled=False)
        return [full], [[(0, b, 0, rows)] for b in range(full.shape[0])]
    below = shift_up(value)
    above = shift_down(value)
    far_a = shift_up(after(below[: rows // 2], wait_for))
    far_b = shift_down(after(above[rows // 2 :], wait_for))
    arrays = [value, below, above, far_a, far_b]
    arrays = arrays + [swap_core(v) for v in arrays]
    places = []
    for base in (0, 5):
        places += [[(base + k, None, 0, rows)] for k in range(3)]
        places += [[(base + 3, None, 0, rows // 2), (base + 4, None, rows // 2, rows // 2)]]
    return arrays, places


def rotate(values, cos_wide, sin_wide):
    return values * cos_wide + pltpu.roll(values, HEAD_SIZE // 2, 1) * sin_wide


def tile_cols(j, size):
    return pl.ds(pl.multiple_of(j * size, size), size)


def forward_kernel(plan, *refs):
    order_ref, x_ref, cos_ref, sin_ref, lab_col_ref, lab_row_ref = refs[:6]
    count = plan["inputs"]
    inputs = refs[6 : 6 + count]
    (
        h2_ref,
        res_ref,
        h1_ref,
        q_ref,
        k_ref,
        v_ref,
        p_ref,
        o_ref,
        aux_ref,
        w_full_out,
        w_full,
        sem_in,
        sem_save,
    ) = refs[6 + count :]
    width = x_ref.shape[1]
    tokens = x_ref.shape[0]
    bf = jnp.bfloat16
    heads = QUERY_HEADS // KEY_VALUE_HEADS
    kv_width = KEY_VALUE_HEADS * HEAD_SIZE
    main = width + 2 * kv_width
    base = main + 128
    for ref_index, lead, order_index in plan["places"]:
        src = inputs[ref_index]
        for at in lead:
            src = src.at[at]
        rows = src.shape[0]
        if order_index is None:
            dst = w_full
        else:
            start = pl.multiple_of(order_ref[order_index] * rows, rows)
            dst = w_full.at[pl.ds(start, rows), :]
        pltpu.make_async_copy(src, dst, sem_in).start()
    x = x_ref[...].astype(jnp.float32)
    inverse = lax.rsqrt(jnp.mean(x * x, axis=1, keepdims=True) + EPSILON)
    pltpu.make_async_copy(w_full, w_full, sem_in).wait()
    save = pltpu.make_async_copy(w_full, w_full_out, sem_save)
    save.start()
    side = w_full[:, main : main + 128].astype(jnp.float32).T
    gain = side[:1]
    h1_ref[...] = (x * inverse * gain).astype(bf)
    cos_wide, sin_wide = cos_ref[...], sin_ref[...]

    @pl.loop(0, width // 256)
    def _(j):
        raw = dot_nn(h1_ref[...], w_full[:, tile_cols(j, 256)])
        both = [
            rotate(raw[:, half * HEAD_SIZE : (half + 1) * HEAD_SIZE], cos_wide, sin_wide)
            for half in range(2)
        ]
        q_ref[:, tile_cols(j, 256)] = jnp.concatenate(both, axis=1).astype(bf)

    raw = dot_nn(h1_ref[...], w_full[:, width : width + kv_width])
    both = [
        rotate(raw[:, half * HEAD_SIZE : (half + 1) * HEAD_SIZE], cos_wide, sin_wide)
        for half in range(KEY_VALUE_HEADS)
    ]
    k_ref[...] = jnp.concatenate(both, axis=1).astype(bf)
    v_ref[...] = dot_nn(h1_ref[...], w_full[:, width + kv_width : main]).astype(bf)
    seq_len = tokens // SEQ_DEV
    query_step = lax.broadcasted_iota(jnp.int32, (seq_len, seq_len), 0)
    key_step = lax.broadcasted_iota(jnp.int32, (seq_len, seq_len), 1)
    for s in range(SEQ_DEV):
        rows = slice(s * seq_len, (s + 1) * seq_len)
        same = lab_col_ref[rows, :] == lab_row_ref[:, rows]
        allowed = jnp.logical_and(same, query_step >= key_step)[None]
        for h in range(KEY_VALUE_HEADS):
            cols = slice(h * HEAD_SIZE, (h + 1) * HEAD_SIZE)
            stack = jnp.concatenate(
                [
                    q_ref[rows, (h * heads + g) * HEAD_SIZE : (h * heads + g + 1) * HEAD_SIZE]
                    for g in range(heads)
                ],
                axis=0,
            )
            scores = dot_nt(stack, k_ref[rows, cols]) * HEAD_SIZE ** (-0.5)
            scores = scores.reshape(heads, seq_len, seq_len)
            scores = jnp.where(allowed, scores, NEG_FILL)
            top = jnp.max(scores, axis=2, keepdims=True)
            raised = jnp.exp(scores - top)
            probs = raised / jnp.sum(raised, axis=2, keepdims=True)
            probs = probs.reshape(heads * seq_len, seq_len)
            p_ref[s, h] = probs
            mixed = dot_nn(probs.astype(bf), v_ref[rows, cols]).astype(bf)
            for g in range(heads):
                o_ref[rows, (h * heads + g) * HEAD_SIZE : (h * heads + g + 1) * HEAD_SIZE] = mixed[
                    g * seq_len : (g + 1) * seq_len
                ]
    side_out = w_full[:, base + width : base + width + 128].astype(jnp.float32).T
    aux_ref[...] = jnp.concatenate([side_out, side[:8]], axis=0)

    @pl.loop(0, width // 256)
    def _(j):
        cols = tile_cols(j, 256)
        at = pl.ds(pl.multiple_of(base + j * 256, 128), 256)
        res_ref[:, cols] = x_ref[:, cols].astype(jnp.float32) + dot_nn(o_ref[...], w_full[:, at])

    res = res_ref[...]
    inverse = lax.rsqrt(jnp.mean(res * res, axis=1, keepdims=True) + EPSILON)
    moe_row = plan["experts"]
    h2_ref[...] = (res * inverse * side_out[moe_row : moe_row + 1]).astype(bf)
    save.wait()


def run_forward(plan, order, x, cos_wide, sin_wide, lab_col, lab_row, inputs, w_cols):
    tokens, width = x.shape
    bf, f32 = jnp.bfloat16, jnp.float32
    kv_width = KEY_VALUE_HEADS * HEAD_SIZE
    seq_len = tokens // SEQ_DEV
    stack = QUERY_HEADS // KEY_VALUE_HEADS * seq_len
    vmem = pl.BlockSpec(memory_space=pltpu.VMEM)
    shape = jax.ShapeDtypeStruct
    sem = pltpu.SemaphoreType.DMA
    return pl.pallas_call(
        lambda *refs: forward_kernel(plan, *refs),
        out_shape=(
            shape((tokens, width), bf),
            shape((tokens, width), f32),
            shape((tokens, width), bf),
            shape((tokens, width), bf),
            shape((tokens, kv_width), bf),
            shape((tokens, kv_width), bf),
            shape((SEQ_DEV, KEY_VALUE_HEADS, stack, seq_len), f32),
            shape((tokens, width), bf),
            shape((136, width), f32),
            shape((width, w_cols), bf),
        ),
        in_specs=[smem_spec()] + [vmem] * 5 + [any_spec()] * len(inputs),
        out_specs=tuple([vmem] * 9 + [any_spec()]),
        scratch_shapes=[
            pltpu.VMEM((width, w_cols), bf),
            sem,
            sem,
        ],
        cost_estimate=pl.CostEstimate(flops=17600000000, transcendentals=0, bytes_accessed=16000000),
        compiler_params=pltpu.CompilerParams(vmem_limit_bytes=56 * MIB),
    )(order, x, cos_wide, sin_wide, lab_col, lab_row, *inputs)


def send_payload(order_ref, payload, outs, sem):
    if len(outs) == 1:
        copies = [pltpu.make_async_copy(payload, outs[0], sem)]
    else:
        copies = []
        rows = payload.shape[0] // 32
        for j in range(32):
            start = pl.multiple_of(order_ref[j] * rows, rows)
            dst = outs[j // 4].at[j % 4]
            copies.append(pltpu.make_async_copy(payload.at[pl.ds(start, rows), :], dst, sem))
    for copy in copies:
        copy.start()
    pltpu.make_async_copy(payload, payload, sem).wait()


def payload_shapes(tuned, rows, cols):
    if not tuned:
        return (jax.ShapeDtypeStruct((rows, cols), jnp.bfloat16),)
    return (jax.ShapeDtypeStruct((4, rows // 32, cols), jnp.bfloat16),) * 8


def middle_kernel(experts, sums, order_ref, own_ref, dy_all, codes_ref, *refs):
    back_refs = refs[: sums]
    res_ref, h2_ref, o_ref, aux_ref, w_full_ref = refs[sums : sums + 5]
    base = w_full_ref.shape[1] - refs[sums].shape[1] - 128
    rest = refs[sums + 5 :]
    outs = rest[:-8]
    dres_ref, dmix_ref, w_out, dy, payload, dres_low, sem_w, sem_p = rest[-8:]
    tokens, width = res_ref.shape
    bf = jnp.bfloat16
    load = pltpu.make_async_copy(w_full_ref.at[:, pl.ds(base, width)], w_out, sem_w.at[0])
    load.start()
    load_dy = pltpu.make_async_copy(dy_all.at[own_ref[0]], dy, sem_w.at[1])
    load_dy.start()
    back = back_refs[0][...]
    if sums == 5:
        cut = tokens // 2
        up_one, down_one, up_two, down_two = [ref[...].astype(jnp.float32) for ref in back_refs[1:]]
        first = jnp.concatenate([up_two, up_one[cut:]], axis=0)
        second = jnp.concatenate([down_one[:cut], down_two], axis=0)
        back = back + first + second
    grad_pair = (
        back[tokens : tokens + experts, :tokens]
        + back[tokens : tokens + experts, tokens : 2 * tokens]
    )
    back = back[:tokens]
    router_t = aux_ref[:experts, :].astype(bf)
    gain = aux_ref[experts : experts + 1, :]
    logits = dot_nt(router_t, h2_ref[...])
    chosen = codes_ref[...] > 0.0
    top = jnp.max(jnp.where(chosen, logits, NEG_FILL), axis=0, keepdims=True)
    raised = jnp.where(chosen, jnp.exp(logits - top), 0.0)
    gates = raised / jnp.sum(raised, axis=0, keepdims=True)
    inner = jnp.sum(gates * grad_pair, axis=0, keepdims=True)
    dlog = jnp.where(chosen, gates * (grad_pair - inner), 0.0).astype(bf)
    grad_router = dot_nn(dlog, h2_ref[...])
    dh2 = back + dot_tn(dlog, router_t)
    res = res_ref[...]
    inverse = lax.rsqrt(jnp.mean(res * res, axis=1, keepdims=True) + EPSILON)
    scaled = dh2 * gain
    grad_gain = jnp.sum(dh2 * res * inverse, axis=0, keepdims=True)
    load_dy.wait()
    dres = (
        dy[...].astype(jnp.float32)
        + inverse * scaled
        - res * inverse**3 * jnp.mean(scaled * res, axis=1, keepdims=True)
    )
    dres_ref[...] = dres
    dres_low[...] = dres.astype(bf)
    pad = jnp.zeros((128 - experts - 8, width), jnp.float32)
    side = jnp.concatenate(
        [grad_router, jnp.broadcast_to(grad_gain, (8, width)), pad], axis=0
    )
    payload[:, width : width + 128] = side.T.astype(bf)

    @pl.loop(0, width // 256)
    def _(j):
        cols = tile_cols(j, 256)
        payload[:, cols] = dot_tn(o_ref[...], dres_low[:, cols]).astype(bf)

    load.wait()

    @pl.loop(0, width // 256)
    def _(j):
        cols = tile_cols(j, 256)
        dmix_ref[:, cols] = dot_nt(dres_low[...], w_out[cols, :]).astype(bf)

    send_payload(order_ref, payload, outs, sem_p)


def run_middle(tuned, experts, order, own, dy_all, codes, backs, res, h2, o, aux, w_full):
    tokens, width = res.shape
    bf, f32 = jnp.bfloat16, jnp.float32
    vmem = pl.BlockSpec(memory_space=pltpu.VMEM)
    shape = jax.ShapeDtypeStruct
    sem = pltpu.SemaphoreType.DMA
    payload = payload_shapes(tuned, width, width + 128)
    return pl.pallas_call(
        lambda *refs: middle_kernel(experts, len(backs), *refs),
        out_shape=payload + (shape((tokens, width), f32), shape((tokens, width), bf)),
        in_specs=[smem_spec()] * 2 + [any_spec()] + [vmem] * (len(backs) + 5) + [any_spec()],
        out_specs=tuple([any_spec()] * len(payload) + [vmem] * 2),
        scratch_shapes=[
            pltpu.VMEM((width, width), bf),
            pltpu.VMEM((tokens, width), bf),
            pltpu.VMEM((width, width + 128), bf),
            pltpu.VMEM((tokens, width), bf),
            sem((2,)),
            sem,
        ],
        cost_estimate=pl.CostEstimate(flops=17600000000, transcendentals=0, bytes_accessed=16000000),
        compiler_params=pltpu.CompilerParams(vmem_limit_bytes=56 * MIB),
    )(order, own, dy_all, codes, *backs, res, h2, o, aux, w_full)


def backward_kernel(order_ref, x_ref, cos_ref, sin_ref, *refs):
    dres_ref, dmix_ref, h1_ref, q_ref, k_ref, v_ref, p_ref, aux_ref, w_full_ref = refs[:9]
    rest = refs[9:]
    outs = rest[:-7]
    dx_ref, w_in, payload, dqkv, dh1, sem_w, sem_p = rest[-7:]
    tokens, width = x_ref.shape
    bf = jnp.bfloat16
    heads = QUERY_HEADS // KEY_VALUE_HEADS
    kv_width = KEY_VALUE_HEADS * HEAD_SIZE
    main = width + 2 * kv_width
    scale = HEAD_SIZE ** (-0.5)
    load = pltpu.make_async_copy(w_full_ref.at[:, pl.ds(0, main)], w_in, sem_w)
    load.start()
    seq_len = tokens // SEQ_DEV
    for s in range(SEQ_DEV):
        rows = slice(s * seq_len, (s + 1) * seq_len)
        cos_wide, sin_wide = cos_ref[rows, :], -sin_ref[rows, :]
        cos_tall = jnp.concatenate([cos_wide] * heads, axis=0)
        sin_tall = jnp.concatenate([sin_wide] * heads, axis=0)
        for h in range(KEY_VALUE_HEADS):
            cols = slice(h * HEAD_SIZE, (h + 1) * HEAD_SIZE)
            places = [
                slice((h * heads + g) * HEAD_SIZE, (h * heads + g + 1) * HEAD_SIZE)
                for g in range(heads)
            ]
            q_tall = jnp.concatenate([q_ref[rows, place] for place in places], axis=0)
            dmix = jnp.concatenate([dmix_ref[rows, place] for place in places], axis=0)
            probs = p_ref[s, h]
            dprobs = dot_nt(dmix, v_ref[rows, cols])
            dv = dot_tn(probs.astype(bf), dmix)
            inner = jnp.sum(probs * dprobs, axis=1, keepdims=True)
            dscores = (probs * (dprobs - inner)).astype(bf)
            dq = rotate(dot_nn(dscores, k_ref[rows, cols]) * scale, cos_tall, sin_tall)
            dk = rotate(dot_tn(dscores, q_tall) * scale, cos_wide, sin_wide)
            for g, place in enumerate(places):
                dqkv[rows, place] = dq[g * seq_len : (g + 1) * seq_len].astype(bf)
            dqkv[rows, width + h * HEAD_SIZE : width + (h + 1) * HEAD_SIZE] = dk.astype(bf)
            at = width + kv_width + h * HEAD_SIZE
            dqkv[rows, at : at + HEAD_SIZE] = dv.astype(bf)
    load.wait()

    @pl.loop(0, width // 256)
    def _(j):
        cols = tile_cols(j, 256)
        dh1[:, cols] = dot_nt(dqkv[...], w_in[cols, :])

    @pl.loop(0, main // 256)
    def _(j):
        cols = tile_cols(j, 256)
        payload[:, cols] = dot_tn(h1_ref[...], dqkv[:, cols]).astype(bf)

    x = x_ref[...].astype(jnp.float32)
    gain = aux_ref[128:129, :]
    inverse = lax.rsqrt(jnp.mean(x * x, axis=1, keepdims=True) + EPSILON)
    grad = dh1[...]
    scaled = grad * gain
    grad_gain = jnp.sum(grad * x * inverse, axis=0, keepdims=True)
    payload[:, main : main + 128] = jnp.broadcast_to(grad_gain, (128, width)).T.astype(bf)
    dx = (
        dres_ref[...]
        + inverse * scaled
        - x * inverse**3 * jnp.mean(scaled * x, axis=1, keepdims=True)
    )
    dx_ref[...] = dx.astype(bf)
    send_payload(order_ref, payload, outs, sem_p)


def run_backward(tuned, order, x, cos_wide, sin_wide, dres, dmix, h1, q, k, v, p, aux, w_full):
    tokens, width = x.shape
    bf, f32 = jnp.bfloat16, jnp.float32
    vmem = pl.BlockSpec(memory_space=pltpu.VMEM)
    shape = jax.ShapeDtypeStruct
    sem = pltpu.SemaphoreType.DMA
    main = width + 2 * KEY_VALUE_HEADS * HEAD_SIZE
    payload = payload_shapes(tuned, width, main + 128)
    return pl.pallas_call(
        backward_kernel,
        out_shape=payload + (shape((tokens, width), bf),),
        in_specs=[smem_spec()] + [vmem] * 11 + [any_spec()],
        out_specs=tuple([any_spec()] * len(payload) + [vmem]),
        scratch_shapes=[
            pltpu.VMEM((width, main), bf),
            pltpu.VMEM((width, main + 128), bf),
            pltpu.VMEM((tokens, main), bf),
            pltpu.VMEM((tokens, width), f32),
            sem,
            sem,
        ],
        cost_estimate=pl.CostEstimate(flops=18700000000, transcendentals=0, bytes_accessed=17000000),
        compiler_params=pltpu.CompilerParams(vmem_limit_bytes=56 * MIB),
    )(order, x, cos_wide, sin_wide, dres, dmix, h1, q, k, v, p, aux, w_full)


def after(value, *others):
    return lax.optimization_barrier((value,) + others)[0]


def swap_diagonal(value):
    return lax.ppermute(value, "dp", [(i, i ^ 3) for i in range(4)])


def shift_two(value):
    return lax.ppermute(value, "expert", [(i, (i + 4) % 8) for i in range(8)])


def gather_all_pieces(value, tuned):
    if not tuned:
        full = lax.all_gather(value, ("dp", "expert"), axis=0, tiled=True)
        return [full], [(0, (), None)], None
    level = jnp.stack([value, shift_up(value), shift_down(value), shift_two(value)])
    from_x = swap_x(level)
    from_y = swap_y(level)
    far_a = swap_x(from_y[:2])
    far_b = swap_y(from_x[2:])
    arrays = [level, from_x, from_y, far_a, far_b]
    arrays = arrays + [swap_core(v) for v in arrays]
    places = []
    for c in range(2):
        for k in range(4):
            for r in range(4):
                ref, lead = (k, r) if k < 3 else ((3, r) if r < 2 else (4, r - 2))
                places.append((c * 5 + ref, (lead,), (c * 4 + k) * 4 + r))
    return arrays, places, (level, from_x, from_y)


def scatter_payload(outs, tuned):
    if not tuned:
        return lax.psum_scatter(
            outs[0], ("dp", "expert"), scatter_dimension=0, tiled=True
        ).astype(jnp.float32)
    f32, bf = jnp.float32, jnp.bfloat16
    sums = [outs[k].astype(f32) + swap_core(outs[4 + k]).astype(f32) for k in range(4)]
    from_x = swap_x(sums[1].astype(bf))
    from_y = swap_y(sums[2].astype(bf))
    from_far = swap_diagonal(sums[3].astype(bf))
    level = [
        sums[0][r] + from_x[r].astype(f32) + from_y[r].astype(f32) + from_far[r].astype(f32)
        for r in range(4)
    ]
    below, above, far = [v.astype(bf) for v in level[1:]]
    got = [shift_down(below), shift_up(above), shift_two(far)]
    return level[0] + got[0].astype(f32) + got[1].astype(f32) + got[2].astype(f32)


def sum_blocks(keep, send, cut, tuned, got=None, wait_for=()):
    if not tuned:
        blocks = jnp.concatenate([keep, send], axis=0)
        return [
            lax.psum_scatter(blocks, "expert", scatter_dimension=0, tiled=False).astype(jnp.float32)
        ], None
    got = swap_core(send) if got is None else got
    sums = [keep[i].astype(jnp.float32) + got[i].astype(jnp.float32) for i in range(4)]
    own = sums[0]
    to_below, to_above, far = [v.astype(jnp.bfloat16) for v in sums[1:]]
    top = lax.broadcasted_iota(jnp.int32, own.shape, 0) < cut
    messages = (jnp.where(top, far, to_above), jnp.where(top, to_below, far))
    up_one = shift_up(after(messages[0], *wait_for))
    down_one = shift_down(after(messages[1], *wait_for))
    up_two = shift_up(add_low(to_above[:cut], up_one[:cut]))
    down_two = shift_down(add_low(to_below[cut:], down_one[cut:]))
    return [own, up_one, down_one, up_two, down_two], messages


def gather_dealt(value, tuned, level):
    if not tuned:
        return lax.all_gather(value, "expert", axis=0, tiled=False)
    cut = value.shape[0] // 32 * 16
    below = shift_up(value)
    above = shift_down(value)
    far_a = shift_up(after(below[:cut], level[1]))
    far_b = shift_down(after(above[cut:], level[2]))
    parts = jnp.stack([value, below, above, jnp.concatenate([far_a, far_b], axis=0)])
    return jnp.concatenate([parts, swap_core(parts)], axis=0)


def pad_columns(value, width):
    return jnp.pad(value, ((0, 0), (0, width - value.shape[1])))


def body(
    tokens,
    cotangent,
    lengths,
    placement,
    routes,
    priority,
    g_attn,
    w_query,
    key_projection,
    value_projection,
    w_out,
    g_moe,
    w_router,
    w_gate,
    w_up,
    w_down,
):
    row_seqs, piece_len, width = tokens.shape
    expert_devices = lax.axis_size("expert")
    plane_size = lax.axis_size("dp")
    tuned = expert_devices == 8 and plane_size == 4
    my_index = lax.axis_index("expert")
    seq_len = piece_len * expert_devices
    token_count = SEQ_DEV * seq_len
    query_width = w_query.shape[1]
    kv_width = key_projection.shape[1]
    expert_count = w_router.shape[1]
    per_device = expert_count // expert_devices
    capacity = (9 * token_count * TOPK + 64 * expert_count - 1) // (64 * expert_count) * 8
    code_list = jnp.arange(row_seqs, dtype=jnp.int32)
    source = jnp.sum(
        jnp.where(placement[:, None] == code_list[None, :], code_list[:, None], 0), axis=0
    )
    pack = jnp.concatenate(
        [
            w_query,
            key_projection,
            value_projection,
            pad_columns(g_attn[:, None], 128),
            w_out,
            pad_columns(jnp.concatenate([w_router, g_moe[:, None]], axis=1), 128),
        ],
        axis=1,
    )
    pack_parts, pack_places, level = gather_all_pieces(pack, tuned)
    send_tokens = tokens[source].reshape(expert_devices, SEQ_DEV, piece_len, width)
    if tuned:
        send_tokens = after(send_tokens, level[0])
    got_tokens = lax.all_to_all(send_tokens, "expert", split_axis=0, concat_axis=2, tiled=True)
    x_local = got_tokens.reshape(token_count, width)
    ranks = slot_ranks(routes.reshape(-1), priority.reshape(-1)).reshape(token_count, TOPK)
    codes = jnp.minimum(ranks, capacity) + 1
    expert_list = jnp.arange(expert_count, dtype=jnp.int32)
    picks = routes[None, :, :] == expert_list[:, None, None]
    code_table = jnp.sum(jnp.where(picks, codes[None], 0), axis=2)
    table_rows = -(-expert_count // 16) * 16
    table = jnp.zeros((table_rows, width), jnp.bfloat16)
    table = table.at[:expert_count, :token_count].set(code_table.astype(jnp.bfloat16))
    early = jnp.concatenate([cotangent.reshape(token_count, width), table], axis=0)
    if tuned:
        early = after(early, x_local)
    early_all = gather_dealt(early, tuned, level)
    order = expert_order(tuned, expert_devices)
    rel_of = jnp.zeros((expert_devices,), jnp.int32)
    for b in range(expert_devices):
        rel_of = jnp.where(jnp.arange(expert_devices) == order[b], b, rel_of)
    seqs = source.reshape(expert_devices, SEQ_DEV)[order].reshape(-1)
    if piece_len % 16 == 0:
        shape = (expert_devices, token_count, width)
        grads_all = move_blocks(deal_kernel, shape, [seqs, rel_of], [early_all])
    else:
        pieces = early_all[:, :token_count].reshape(expert_devices, row_seqs, piece_len, width)
        pieces = pieces[rel_of][:, seqs].reshape(
            expert_devices, expert_devices, SEQ_DEV, piece_len, width
        )
        grads_all = pieces.transpose(1, 2, 0, 3, 4).reshape(expert_devices, token_count, width)
    codes_all = early_all[:, token_count : token_count + expert_count, :token_count].astype(
        jnp.float32
    )
    own_block = rel_of[my_index].reshape(1)
    weight_parts, weight_places = gather_weight_pieces(w_gate, w_up, w_down, tuned)

    own_seqs = lax.dynamic_slice_in_dim(source, my_index * SEQ_DEV, SEQ_DEV)
    positions, labels = device_layout(lengths[own_seqs], seq_len)
    cosine_table, sine_values = rope_tables(positions, HEAD_SIZE)
    cos_wide = jnp.concatenate([cosine_table, cosine_table], axis=1)
    sin_wide = jnp.concatenate([-sine_values, sine_values], axis=1)
    plan = {
        "inputs": len(pack_parts),
        "experts": expert_count,
        "places": pack_places,
    }
    row_order = all_order()
    normed_moe, residual, h1, q, k, v, probs, mixed, aux, w_full = run_forward(
        plan,
        row_order,
        x_local,
        cos_wide,
        sin_wide,
        labels[:, None],
        labels[None, :],
        pack_parts,
        pack.shape[1],
    )
    token_parts, token_places = gather_token_pieces(normed_moe, tuned, grads_all)
    token_places = [
        [(r + len(weight_parts), lead, row, rows) for r, lead, row, rows in line]
        for line in token_places
    ]
    inputs = weight_parts + token_parts
    plan = {
        "inputs": len(inputs),
        "blocks": expert_devices,
        "per_device": per_device,
        "ff": w_gate.shape[2],
        "weights": weight_places,
        "tokens": token_places,
    }
    scalars = jnp.stack([my_index, lax.axis_index("dp")]).astype(jnp.int32)
    router_t = aux[:expert_count].astype(jnp.bfloat16)
    back_keep, back_send, out_keep, out_send, x_slots, dy_slots, hid, dga, dua = run_experts(
        plan, capacity, table_rows, scalars, codes_all, router_t, grads_all, inputs
    )
    cut = token_count // 2
    back_got, out_got = None, None
    if tuned:
        back_got = swap_core(back_send)
        out_got = swap_core(after(out_send, back_got))
    backs, messages = sum_blocks(back_keep, back_send, cut, tuned, back_got)
    if tuned:
        hid, x_slots = after(hid, *messages), after(x_slots, *messages)
    even = width % (128 * plane_size) == 0
    down_blocks = grad_down_blocks(hid, dy_slots, plane_size if even else 1)
    gate_up_blocks = grad_gate_up_blocks(x_slots, dga, dua, plane_size if even else 1)
    if even:
        flat = down_blocks.reshape(-1, down_blocks.shape[-1])
        owned_down = lax.psum_scatter(flat, "dp", scatter_dimension=0, tiled=True)
        owned_down = owned_down.reshape(down_blocks.shape[1:])
        flat = gate_up_blocks.reshape(-1, gate_up_blocks.shape[-1])
        owned_gate_up = lax.psum_scatter(flat, "dp", scatter_dimension=0, tiled=True)
        owned_gate_up = owned_gate_up.reshape(gate_up_blocks.shape[1:])
    else:
        owned_down = lax.psum_scatter(down_blocks[0], "dp", scatter_dimension=2, tiled=True)
        owned_gate_up = lax.psum_scatter(gate_up_blocks[0], "dp", scatter_dimension=2, tiled=True)
    owned_down = owned_down.astype(jnp.float32)
    owned_gate = owned_gate_up[0].astype(jnp.float32)
    owned_up = owned_gate_up[1].astype(jnp.float32)
    if tuned:
        residual, out_keep = after(residual, out_got), after(out_keep, *backs[1:3])
    sums, messages = sum_blocks(out_keep, out_send, cut, tuned, out_got, backs[3:])
    if tuned:
        backs[0] = after(backs[0], *messages)
    middle = run_middle(
        tuned,
        expert_count,
        row_order,
        own_block,
        grads_all,
        codes_all[0] if tuned else codes_all[own_block[0]],
        backs,
        residual,
        normed_moe,
        mixed,
        aux,
        w_full,
    )
    payload_out, dres, dmix = middle[:-2], middle[-2], middle[-1]
    owned_out = scatter_payload(payload_out, tuned)
    final = run_backward(
        tuned,
        row_order,
        x_local,
        cos_wide,
        sin_wide,
        dres,
        dmix,
        h1,
        q,
        k,
        v,
        probs,
        aux,
        w_full,
    )
    payload_in, grad_x = final[:-1], final[-1]
    if tuned:
        payload_in = [after(v, sums[1], sums[2]) for v in payload_in]
    owned_in = scatter_payload(payload_in, tuned)
    total = residual + sums[0]
    if tuned:
        total = total + jnp.concatenate([sums[3], sums[1][cut:]], axis=0).astype(jnp.float32)
        total = total + jnp.concatenate([sums[2][:cut], sums[4]], axis=0).astype(jnp.float32)
    out_low = total.astype(jnp.bfloat16)
    deal_out, deal_grad = (
        lax.all_to_all(
            out_low.reshape(1, SEQ_DEV, seq_len, width),
            "expert",
            split_axis=2,
            concat_axis=0,
            tiled=True,
        ),
        lax.all_to_all(
            grad_x.reshape(1, SEQ_DEV, seq_len, width),
            "expert",
            split_axis=2,
            concat_axis=0,
            tiled=True,
        ),
    )
    output = deal_out.reshape(row_seqs, piece_len, width)[placement]
    input_grad = deal_grad.reshape(row_seqs, piece_len, width)[placement]
    return (
        output,
        input_grad,
        owned_in[:, query_width + 2 * kv_width],
        owned_in[:, :query_width],
        owned_in[:, query_width : query_width + kv_width],
        owned_in[:, query_width + kv_width : query_width + 2 * kv_width],
        owned_out[:, :width],
        owned_out[:, width + expert_count],
        owned_out[:, width : width + expert_count],
        owned_gate,
        owned_up,
        owned_down,
    )


def solution(mesh):
    return jax.shard_map(
        body,
        mesh=mesh,
        in_specs=(
            P("dp", "expert", None),
            P("dp", "expert", None),
            P("dp", None),
            P("dp"),
            P(("dp", "expert"), None),
            P(("dp", "expert"), None),
            P(("dp", "expert")),
            P(("dp", "expert"), None),
            P(("dp", "expert"), None),
            P(("dp", "expert"), None),
            P(("dp", "expert"), None),
            P(("dp", "expert")),
            P(("dp", "expert"), None),
            P("expert", "dp", None),
            P("expert", "dp", None),
            P("expert", None, "dp"),
        ),
        out_specs=(
            P("dp", "expert", None),
            P("dp", "expert", None),
            P(("dp", "expert")),
            P(("dp", "expert"), None),
            P(("dp", "expert"), None),
            P(("dp", "expert"), None),
            P(("dp", "expert"), None),
            P(("dp", "expert")),
            P(("dp", "expert"), None),
            P("expert", "dp", None),
            P("expert", "dp", None),
            P("expert", None, "dp"),
        ),
        check_vma=False,
    )
```

```python
import math

import jax
import jax.numpy as jnp
from jax import lax
from jax.experimental import pallas as pl
from jax.experimental.pallas import tpu as pltpu
from jax.sharding import PartitionSpec as P

QUERY_HEADS = 12
KEY_VALUE_HEADS = 2
HEAD_SIZE = 128
TOPK = 4
SEQ_DEV = 2


EPSILON = 1e-06
ROPE_BASE = 1000000.0
NEG_FILL = -1e30


def sequence_layout(doc_lens, seq_len):
    token_steps = jnp.arange(seq_len, dtype=jnp.int32)
    doc_ends = jnp.cumsum(doc_lens)
    doc_index = jnp.sum((token_steps[:, None] >= doc_ends[None, :-1]).astype(jnp.int32), axis=1)
    doc_starts = doc_ends - doc_lens
    doc_slots = jnp.arange(doc_lens.shape[0], dtype=jnp.int32)
    start_of = jnp.sum(
        jnp.where(doc_slots[None, :] == doc_index[:, None], doc_starts[None, :], 0), axis=1
    )
    return ((token_steps - start_of).astype(jnp.float32), doc_index)


def device_layout(dev_lens, seq_len):
    positions, doc_index = jax.vmap(lambda single: sequence_layout(single, seq_len))(dev_lens)
    doc_count = dev_lens.shape[1]
    labels = doc_index + doc_count * jnp.arange(dev_lens.shape[0], dtype=jnp.int32)[:, None]
    return (positions.reshape(-1), labels.reshape(-1))


def rope_tables(positions, head_dim):
    freq_index = jnp.arange(head_dim // 2, dtype=jnp.float32)
    frequency = jnp.exp(freq_index * (-2.0 / head_dim) * math.log(ROPE_BASE))
    angle_table = positions[:, None] * frequency[None, :]
    return (jnp.cos(angle_table), jnp.sin(angle_table))


def slot_ranks(route_flat, prio_flat):
    same = route_flat[:, None] == route_flat[None, :]
    ahead = prio_flat[None, :] < prio_flat[:, None]
    return jnp.sum(jnp.logical_and(same, ahead).astype(jnp.int32), axis=1)


def swap_x(value):
    return lax.ppermute(value, "dp", [(i, i ^ 1) for i in range(4)])


def swap_y(value):
    return lax.ppermute(value, "dp", [(i, i ^ 2) for i in range(4)])


def swap_core(value):
    return lax.ppermute(value, "expert", [(i, i ^ 1) for i in range(8)])


def shift_up(value):
    return lax.ppermute(value, "expert", [(i, (i + 2) % 8) for i in range(8)])


def shift_down(value):
    return lax.ppermute(value, "expert", [(i, (i + 6) % 8) for i in range(8)])


def add_low(left, right):
    return (left.astype(jnp.float32) + right.astype(jnp.float32)).astype(jnp.bfloat16)


def any_spec():
    return pl.BlockSpec(memory_space=pl.ANY)


def smem_spec():
    return pl.BlockSpec(memory_space=pltpu.SMEM)


def expert_order(tuned, count):
    if not tuned:
        return jnp.arange(count, dtype=jnp.int32)
    me = lax.axis_index("expert")
    level, core = me // 2, me % 2
    order = [
        ((level + off) % 4) * 2 + (core + flip) % 2 for flip in range(2) for off in (0, 3, 1, 2)
    ]
    return jnp.stack(order).astype(jnp.int32)


def all_order():
    me = lax.axis_index("expert")
    plane = lax.axis_index("dp")
    level, core = me // 2, me % 2
    order = [
        ((plane ^ k) * 4 + (level + off) % 4) * 2 + (core + flip) % 2
        for flip in range(2)
        for k in range(4)
        for off in (0, 3, 1, 2)
    ]
    return jnp.stack(order).astype(jnp.int32)


def dot_nn(left, right):
    return lax.dot_general(
        left, right, (((1,), (0,)), ((), ())), preferred_element_type=jnp.float32
    )


def dot_nt(left, right):
    return lax.dot_general(
        left, right, (((1,), (1,)), ((), ())), preferred_element_type=jnp.float32
    )


def dot_tn(left, right):
    return lax.dot_general(
        left, right, (((0,), (0,)), ((), ())), preferred_element_type=jnp.float32
    )


GELU_SCALE = math.sqrt(2.0 / math.pi)
GELU_CUBE = 0.044715
MIB = 1024 * 1024


def deal_copies(scalar_ref, early, piece, block, dst, row, sem):
    devices = len(early)
    copies = []
    for k in range(SEQ_DEV):
        start = pl.multiple_of(scalar_ref[1 + block * SEQ_DEV + k] * piece, piece)
        for q in range(devices):
            place = scalar_ref[1 + devices * SEQ_DEV + q] * piece
            to = pl.multiple_of(row + k * devices * piece + place, piece)
            copies.append(
                pltpu.make_async_copy(
                    early[q].at[pl.ds(start, piece), :], dst.at[pl.ds(to, piece), :], sem
                )
            )
    return copies


def give_back(scalar_ref, piece, block, src, keep, send, sem):
    devices = keep.shape[0] + send.shape[0]
    half = devices // 2
    for j in range(devices):
        to = scalar_ref[1 + devices * SEQ_DEV + devices + j]
        for k in range(SEQ_DEV):
            start = pl.multiple_of(scalar_ref[1 + block * SEQ_DEV + k] * piece, piece)
            part = src.at[pl.ds((k * devices + j) * piece, piece), :]

            @pl.when(to < half)
            def _(part=part, to=to, start=start):
                dst = keep.at[to, pl.ds(start, piece), :]
                pltpu.make_async_copy(part, dst, sem).start()

            @pl.when(to >= half)
            def _(part=part, to=to, start=start):
                dst = send.at[to - half, pl.ds(start, piece), :]
                pltpu.make_async_copy(part, dst, sem).start()


def expert_kernel(plan, capacity, *refs):
    count = plan["inputs"]
    my_ref, router_ref, codes_ref, grads_ref, res_ref = refs[:5]
    inputs = refs[5 : 5 + count]
    (
        back_keep,
        back_send,
        out_keep,
        out_send,
        x_out,
        dy_out,
        hid_out,
        dga_out,
        dua_out,
    ) = refs[5 + count : 14 + count]
    (
        gate_w,
        up_w,
        down_w,
        h_buf,
        d_buf,
        hot,
        x_s,
        dy_s,
        y_s,
        dx_s,
        hid_s,
        dga_s,
        dua_s,
        act_s,
        slope_s,
        codes_all,
        code_s,
        gates_s,
        sgate_s,
        dg_s,
        stage_b,
        stage_o,
        sem_w,
        sem_h,
        sem_d,
        sem_c,
        sem_s,
        sem_b,
        sem_o,
    ) = refs[14 + count :]
    blocks = plan["blocks"]
    pairs = blocks // 2
    per_device, width, ff = gate_w.shape
    tokens = h_buf.shape[1] // 2
    slots = 2 * capacity
    experts = router_ref.shape[0]
    my_first = my_ref[0] * per_device
    dtype = jnp.bfloat16

    plane = my_ref[my_ref.shape[0] - 1]

    def window(hold, axis, e, flip, step):
        start = 0 if flip is None else pl.multiple_of((plane ^ flip) * step, step)
        if axis == 1:
            return hold.at[e, pl.ds(start, step), :]
        return hold.at[e, :, pl.ds(start, step)]

    weight_copies = []
    for t, (hold, axis) in enumerate(((gate_w, 1), (up_w, 1), (down_w, 2))):
        for e in range(per_device):
            copies = []
            for ref_index, lead, flip in plan["weights"][t][e]:
                src = inputs[ref_index].at[lead]
                step = src.shape[axis - 1]
                sem = sem_w.at[t * per_device + e, len(copies)]
                copy = pltpu.make_async_copy(src, window(hold, axis, e, flip, step), sem)
                copy.start()
                copies.append(copy)
            weight_copies.append(copies)

    early = [inputs[i] for i in plan["early"]]
    if early:
        for b, ref in enumerate(early):
            src = ref.at[pl.ds(tokens, codes_all.shape[1]), pl.ds(0, tokens)]
            pltpu.make_async_copy(src, codes_all.at[b], sem_c).start()
    else:
        pltpu.make_async_copy(codes_ref, codes_all, sem_c).start()

    def fetch(p):
        slot = p % 2
        copies = []
        for half in range(2):
            for k, (ref_index, lead, row, rows) in enumerate(plan["tokens"][2 * p + half]):
                src = inputs[ref_index] if lead is None else inputs[ref_index].at[lead]
                dst = h_buf.at[slot, pl.ds(half * tokens + row, rows), :]
                copies.append(pltpu.make_async_copy(src, dst, sem_h.at[slot, half, k]))
        if early:
            deals = []
            for half in range(2):
                deals += deal_copies(
                    my_ref,
                    early,
                    plan["piece"],
                    2 * p + half,
                    d_buf.at[slot],
                    half * tokens,
                    sem_d.at[slot],
                )
        else:
            deals = [
                pltpu.make_async_copy(
                    grads_ref.at[2 * p + half],
                    d_buf.at[slot, pl.ds(half * tokens, tokens), :],
                    sem_d.at[slot],
                )
                for half in range(2)
            ]
        for copy in copies + deals:
            copy.start()
        return copies + [pltpu.make_async_copy(d_buf.at[slot], d_buf.at[slot], sem_d.at[slot])]

    row = lax.broadcasted_iota(jnp.int32, (slots, 2 * tokens), 0)
    col = lax.broadcasted_iota(jnp.int32, (slots, 2 * tokens), 1)
    second = row >= capacity
    same = jnp.logical_xor(second, col < tokens)
    target = (row - jnp.where(second, capacity, 0) + 1).astype(jnp.float32)
    flying = fetch(0)
    pltpu.make_async_copy(codes_all, codes_all, sem_c).wait()
    for p in range(pairs):
        slot = p % 2
        later = fetch(p + 1) if p + 1 < pairs else []
        for copy in flying:
            copy.wait()
        flying = later
        codes = jnp.concatenate([codes_all[2 * p], codes_all[2 * p + 1]], axis=1)
        codes = codes.astype(jnp.float32)[:experts]
        logits = dot_nt(router_ref[...], h_buf[slot])
        chosen = codes > 0.0
        top = jnp.max(jnp.where(chosen, logits, NEG_FILL), axis=0, keepdims=True)
        raised = jnp.where(chosen, jnp.exp(logits - top), 0.0)
        code_s[...] = codes
        gates_s[...] = raised / jnp.sum(raised, axis=0, keepdims=True)
        for e in range(per_device):
            code_row = code_s[pl.ds(my_first + e, 1), :]
            gate_row = gates_s[pl.ds(my_first + e, 1), :]
            hit = jnp.logical_and(same, code_row == target)
            one = jnp.where(hit, 1.0, 0.0).astype(dtype)
            hot[e, p] = one
            gate_slot = jnp.sum(jnp.where(hit, gate_row, 0.0), axis=1, keepdims=True)
            rows = pl.ds(p * slots, slots)
            sgate_s[e, rows, :] = jnp.broadcast_to(gate_slot, (slots, 128))
            x_s[e, rows, :] = dot_nn(one, h_buf[slot]).astype(dtype)
            dy_s[e, rows, :] = dot_nn(one, d_buf[slot]).astype(dtype)

    saves = []
    for e in range(per_device):
        for copy in weight_copies[e] + weight_copies[per_device + e]:
            copy.wait()
        save = pltpu.make_async_copy(x_s.at[e], x_out.at[e], sem_s.at[0, e])
        save.start()
        saves.append(save)
        gate_slot = sgate_s[e][:, :1]

        @pl.loop(0, ff // 256)
        def _(j):
            cols = pl.ds(pl.multiple_of(j * 256, 256), 256)
            ga = dot_nn(x_s[e], gate_w[e, :, cols])
            ua = dot_nn(x_s[e], up_w[e, :, cols])
            square = ga * ga
            tan = jnp.tanh(GELU_SCALE * (ga + GELU_CUBE * square * ga))
            act = 0.5 * ga * (1.0 + tan)
            slope = 0.5 * (1.0 + tan) + 0.5 * ga * (1.0 - tan * tan) * GELU_SCALE * (
                1.0 + 3.0 * GELU_CUBE * square
            )
            act_s[:, cols] = act
            slope_s[:, cols] = ua * slope
            hid_s[e, :, cols] = (act * ua).astype(dtype)

        save = pltpu.make_async_copy(hid_s.at[e], hid_out.at[e], sem_s.at[1, e])
        save.start()
        saves.append(save)
        for copy in weight_copies[2 * per_device + e]:
            copy.wait()
        dg_s[e] = jnp.zeros(dg_s.shape[1:], jnp.float32)

        @pl.loop(0, width // 256)
        def _(j):
            cols = pl.ds(pl.multiple_of(j * 256, 256), 256)
            y = dot_nn(hid_s[e], down_w[e, :, cols]).astype(dtype).astype(jnp.float32)
            dy = dy_s[e, :, cols].astype(jnp.float32)
            dg_s[e] += jnp.broadcast_to(
                jnp.sum(dy * y, axis=1, keepdims=True), dg_s.shape[1:]
            )
            y_s[e, :, cols] = (gate_slot * y).astype(dtype)
            dy_s[e, :, cols] = (gate_slot * dy).astype(dtype)

        save = pltpu.make_async_copy(dy_s.at[e], dy_out.at[e], sem_s.at[2, e])
        save.start()
        saves.append(save)

        @pl.loop(0, ff // 256)
        def _(j):
            cols = pl.ds(pl.multiple_of(j * 256, 256), 256)
            dhid = dot_nt(dy_s[e], down_w[e, cols, :])
            dga_s[e, :, cols] = (dhid * slope_s[:, cols]).astype(dtype)
            dua_s[e, :, cols] = (dhid * act_s[:, cols]).astype(dtype)

        for k, (hold, out) in enumerate(((dga_s, dga_out), (dua_s, dua_out))):
            save = pltpu.make_async_copy(hold.at[e], out.at[e], sem_s.at[3 + k, e])
            save.start()
            saves.append(save)

        @pl.loop(0, width // 256)
        def _(j):
            cols = pl.ds(pl.multiple_of(j * 256, 256), 256)
            dx = dot_nt(dga_s[e], gate_w[e, cols, :]) + dot_nt(dua_s[e], up_w[e, cols, :])
            dx_s[e, :, cols] = dx.astype(dtype)

    table_rows = stage_b.shape[2] - tokens
    table_row = lax.broadcasted_iota(jnp.int32, (table_rows, 2 * tokens), 0)
    sends = {}
    for p in range(pairs):
        slot = p % 2
        for copy in sends.pop(p - 2, []):
            copy.wait()
        rows = pl.ds(p * slots, slots)

        @pl.loop(0, width // 512)
        def _(j):
            cols = pl.ds(pl.multiple_of(j * 512, 512), 512)
            back = jnp.zeros((2 * tokens, 512), jnp.float32)
            outs = jnp.zeros((2 * tokens, 512), jnp.float32)
            for e in range(per_device):
                back += dot_tn(hot[e, p], dx_s[e, rows, cols])
                outs += dot_tn(hot[e, p], y_s[e, rows, cols])
            for half in range(2):
                part = slice(half * tokens, (half + 1) * tokens)
                stage_b[slot, half, :tokens, cols] = back[part].astype(dtype)
                mixed = outs[part]
                if early and p == 0 and half == 0:
                    mixed = mixed + res_ref[:, cols]
                stage_o[slot, half, :, cols] = mixed.astype(dtype)

        tables = [jnp.zeros((table_rows, 2 * tokens), jnp.float32) for _ in range(2)]
        for e in range(per_device):
            dg = dg_s[e, rows, :][:, :1]
            line = jnp.sum(hot[e, p].astype(jnp.float32) * dg, axis=0, keepdims=True)
            mine = table_row == my_first + e
            for half in range(2):
                part = line[:, half * tokens : (half + 1) * tokens]
                high = part.astype(dtype).astype(jnp.float32)
                both = jnp.concatenate([high, part - high], axis=1)
                tables[half] = jnp.where(mine, both, tables[half])
        for half in range(2):
            stage_b[slot, half, tokens:, : 2 * tokens] = tables[half].astype(dtype)
            stage_b[slot, half, tokens:, 2 * tokens :] = jnp.zeros(
                (table_rows, width - 2 * tokens), dtype
            )
        first = 2 * p
        keep = first < blocks // 2
        at = pl.ds(first if keep else first - blocks // 2, 2)
        copies = [
            pltpu.make_async_copy(
                stage_b.at[slot], (back_keep if keep else back_send).at[at], sem_b.at[slot]
            )
        ]
        if early:
            for half in range(2):
                give_back(
                    my_ref,
                    plan["piece"],
                    first + half,
                    stage_o.at[slot, half],
                    out_keep,
                    out_send,
                    sem_o.at[slot],
                )
        else:
            copies.append(
                pltpu.make_async_copy(
                    stage_o.at[slot], (out_keep if keep else out_send).at[at], sem_o.at[slot]
                )
            )
        for copy in copies:
            copy.start()
        if early:
            copies.append(
                pltpu.make_async_copy(stage_o.at[slot], stage_o.at[slot], sem_o.at[slot])
            )
        sends[p] = copies
    for copies in sends.values():
        for copy in copies:
            copy.wait()
    for save in saves:
        save.wait()


def run_experts(plan, capacity, table_rows, scalars, router_t, codes, grads_all, res, inputs):
    experts, width = router_t.shape
    blocks, tokens = plan["blocks"], plan["token_count"]
    per_device, ff = plan["per_device"], plan["ff"]
    rows = blocks * capacity
    bf, f32 = jnp.bfloat16, jnp.float32
    half = blocks // 2
    back = jax.ShapeDtypeStruct((half, tokens + table_rows, width), bf)
    outs = jax.ShapeDtypeStruct((half, tokens, width), bf)
    wide = jax.ShapeDtypeStruct((per_device, rows, width), bf)
    thin = jax.ShapeDtypeStruct((per_device, rows, ff), bf)
    vmem = pl.BlockSpec(memory_space=pltpu.VMEM)
    sem = pltpu.SemaphoreType.DMA
    return pl.pallas_call(
        lambda *refs: expert_kernel(plan, capacity, *refs),
        out_shape=(back, back, outs, outs, wide, wide, thin, thin, thin),
        in_specs=[smem_spec(), vmem, any_spec(), any_spec(), vmem] + [any_spec()] * len(inputs),
        out_specs=tuple([any_spec()] * 9),
        scratch_shapes=[
            pltpu.VMEM((per_device, width, ff), bf),
            pltpu.VMEM((per_device, width, ff), bf),
            pltpu.VMEM((per_device, ff, width), bf),
            pltpu.VMEM((2, 2 * tokens, width), bf),
            pltpu.VMEM((2, 2 * tokens, width), bf),
            pltpu.VMEM((per_device, blocks // 2, 2 * capacity, 2 * tokens), bf),
            pltpu.VMEM((per_device, rows, width), bf),
            pltpu.VMEM((per_device, rows, width), bf),
            pltpu.VMEM((per_device, rows, width), bf),
            pltpu.VMEM((per_device, rows, width), bf),
            pltpu.VMEM((per_device, rows, ff), bf),
            pltpu.VMEM((per_device, rows, ff), bf),
            pltpu.VMEM((per_device, rows, ff), bf),
            pltpu.VMEM((rows, ff), f32),
            pltpu.VMEM((rows, ff), f32),
            pltpu.VMEM((blocks, table_rows, tokens), bf),
            pltpu.VMEM((experts, 2 * tokens), f32),
            pltpu.VMEM((experts, 2 * tokens), f32),
            pltpu.VMEM((per_device, rows, 128), f32),
            pltpu.VMEM((per_device, rows, 128), f32),
            pltpu.VMEM((2, 2, tokens + table_rows, width), bf),
            pltpu.VMEM((2, 2, tokens, width), bf),
            sem((3 * per_device, 4)),
            sem((2, 2, 2)),
            sem((2,)),
            sem,
            sem((5, per_device)),
            sem((2,)),
            sem((2,)),
        ],
        cost_estimate=pl.CostEstimate(flops=55000000000, transcendentals=0, bytes_accessed=50000000),
        compiler_params=pltpu.CompilerParams(vmem_limit_bytes=61 * MIB),
    )(scalars, router_t, codes, grads_all, res, *inputs)


def weight_kernel(x_ref, dga_ref, dua_ref, hid_ref, dy_ref, out_ref):
    dtype = jnp.bfloat16
    out_ref[0, 0, 0] = dot_tn(x_ref[0], dga_ref[0]).astype(dtype)
    out_ref[0, 1, 0] = dot_tn(x_ref[0], dua_ref[0]).astype(dtype)
    ff = hid_ref.shape[2]
    step = dy_ref.shape[2]
    for i in range(ff // step):
        part = dot_tn(hid_ref[0, :, i * step : (i + 1) * step], dy_ref[0])
        out_ref[0, 2, 0, :, i * step : (i + 1) * step] = part.astype(dtype)


def expert_weight_grads(x, dga, dua, hid, dy, parts):
    per_device, rows, ff = dga.shape
    step = x.shape[2] // parts
    whole = pl.BlockSpec((1, rows, ff), lambda e, d: (e, 0, 0))
    piece = pl.BlockSpec((1, rows, step), lambda e, d: (e, 0, d))
    return pl.pallas_call(
        weight_kernel,
        grid=(per_device, parts),
        out_shape=jax.ShapeDtypeStruct((parts, 3, per_device, step, ff), jnp.bfloat16),
        in_specs=[piece, whole, whole, whole, piece],
        out_specs=pl.BlockSpec((1, 3, 1, step, ff), lambda e, d: (d, 0, e, 0, 0)),
        cost_estimate=pl.CostEstimate(
            flops=18700000000, transcendentals=0, bytes_accessed=17000000
        ),
        compiler_params=pltpu.CompilerParams(vmem_limit_bytes=56 * MIB),
    )(x, dga, dua, hid, dy)


def down_kernel(hid_ref, dy_ref, out_ref):
    out_ref[0] = dot_tn(hid_ref[0], dy_ref[0]).astype(jnp.bfloat16)


def gate_up_kernel(x_ref, dga_ref, dua_ref, out_ref):
    out_ref[0, 0] = dot_tn(x_ref[0], dga_ref[0]).astype(jnp.bfloat16)
    out_ref[1, 0] = dot_tn(x_ref[0], dua_ref[0]).astype(jnp.bfloat16)


def whole_weight_grads(x, dga, dua, hid, dy):
    per_device, rows, ff = dga.shape
    width = x.shape[2]
    thin = pl.BlockSpec((1, rows, ff), lambda e: (e, 0, 0))
    wide = pl.BlockSpec((1, rows, width), lambda e: (e, 0, 0))
    down = pl.pallas_call(
        down_kernel,
        grid=(per_device,),
        out_shape=jax.ShapeDtypeStruct((per_device, ff, width), jnp.bfloat16),
        in_specs=[thin, wide],
        out_specs=pl.BlockSpec((1, ff, width), lambda e: (e, 0, 0)),
        compiler_params=pltpu.CompilerParams(vmem_limit_bytes=40 * MIB),
    )(hid, dy)
    gate_up = pl.pallas_call(
        gate_up_kernel,
        grid=(per_device,),
        out_shape=jax.ShapeDtypeStruct((2, per_device, width, ff), jnp.bfloat16),
        in_specs=[wide, thin, thin],
        out_specs=pl.BlockSpec((2, 1, width, ff), lambda e: (0, e, 0, 0)),
        compiler_params=pltpu.CompilerParams(vmem_limit_bytes=40 * MIB),
    )(x, dga, dua)
    return gate_up, down


def gather_inputs(value, weights, count, tuned):
    rows = value.shape[0]
    if not tuned:
        full = lax.all_gather(value, "expert", axis=0, tiled=False)
        places = [[[(t, (e,), None)] for e in range(count)] for t in range(3)]
        return list(weights) + [full], places, [[(3, b, 0, rows)] for b in range(full.shape[0])]
    both, both_x, both_y, down, down_x, down_y, down_a, down_b = weights
    below = shift_up(value)
    above = shift_down(value)
    below, above, both_x, both_y = lax.optimization_barrier((below, above, both_x, both_y))
    tokens = [value, below, above, shift_up(below)]
    tokens = tokens + [swap_core(v) for v in tokens]
    arrays = [both, both_x, both_y, swap_x(both_y[0]), swap_y(both_x[1])]
    arrays = arrays + [down, down_x, down_y, down_a, down_b]
    places = [
        [[(k, (t, e), k) for k in range(3)] + [(3 + t, (e,), 3)] for e in range(count)]
        for t in range(2)
    ]
    places.append(
        [[(5 + k, (e,), k) for k in range(3)] + [(8 + e, (0,), 3)] for e in range(count)]
    )
    token_places = []
    for base in (10, 14):
        token_places += [[(base + k, None, 0, rows)] for k in range(4)]
    return arrays + tokens, places, token_places


def rotate(values, cos_wide, sin_wide):
    return values * cos_wide + pltpu.roll(values, HEAD_SIZE // 2, 1) * sin_wide


def tile_cols(j, size):
    return pl.ds(pl.multiple_of(j * size, size), size)


def forward_kernel(plan, *refs):
    order_ref, x_ref, cos_ref, sin_ref, lab_col_ref, lab_row_ref = refs[:6]
    count = plan["inputs"]
    inputs = refs[6 : 6 + count]
    (
        h2_ref,
        res_ref,
        h1_ref,
        q_ref,
        k_ref,
        v_ref,
        p_ref,
        o_ref,
        aux_ref,
        w_full_out,
        w_full,
        sem_in,
        sem_save,
    ) = refs[6 + count :]
    width = x_ref.shape[1]
    tokens = x_ref.shape[0]
    bf = jnp.bfloat16
    heads = QUERY_HEADS // KEY_VALUE_HEADS
    kv_width = KEY_VALUE_HEADS * HEAD_SIZE
    main = width + 2 * kv_width
    base = main + 128
    for ref_index, lead, order_index in plan["places"]:
        src = inputs[ref_index]
        for at in lead:
            src = src.at[at]
        rows = src.shape[0]
        if order_index is None:
            dst = w_full
        else:
            start = pl.multiple_of(order_ref[order_index] * rows, rows)
            dst = w_full.at[pl.ds(start, rows), :]
        pltpu.make_async_copy(src, dst, sem_in).start()
    x = x_ref[...].astype(jnp.float32)
    inverse = lax.rsqrt(jnp.mean(x * x, axis=1, keepdims=True) + EPSILON)
    pltpu.make_async_copy(w_full, w_full, sem_in).wait()
    save = pltpu.make_async_copy(w_full, w_full_out, sem_save)
    save.start()
    side = w_full[:, main : main + 128].astype(jnp.float32).T
    gain = side[:1]
    h1_ref[...] = (x * inverse * gain).astype(bf)
    cos_wide, sin_wide = cos_ref[...], sin_ref[...]

    @pl.loop(0, width // 256)
    def _(j):
        raw = dot_nn(h1_ref[...], w_full[:, tile_cols(j, 256)])
        both = [
            rotate(raw[:, half * HEAD_SIZE : (half + 1) * HEAD_SIZE], cos_wide, sin_wide)
            for half in range(2)
        ]
        q_ref[:, tile_cols(j, 256)] = jnp.concatenate(both, axis=1).astype(bf)

    raw = dot_nn(h1_ref[...], w_full[:, width : width + kv_width])
    both = [
        rotate(raw[:, half * HEAD_SIZE : (half + 1) * HEAD_SIZE], cos_wide, sin_wide)
        for half in range(KEY_VALUE_HEADS)
    ]
    k_ref[...] = jnp.concatenate(both, axis=1).astype(bf)
    v_ref[...] = dot_nn(h1_ref[...], w_full[:, width + kv_width : main]).astype(bf)
    seq_len = tokens // SEQ_DEV
    query_step = lax.broadcasted_iota(jnp.int32, (seq_len, seq_len), 0)
    key_step = lax.broadcasted_iota(jnp.int32, (seq_len, seq_len), 1)
    for s in range(SEQ_DEV):
        rows = slice(s * seq_len, (s + 1) * seq_len)
        same = lab_col_ref[rows, :] == lab_row_ref[:, rows]
        allowed = jnp.logical_and(same, query_step >= key_step)[None]
        for h in range(KEY_VALUE_HEADS):
            cols = slice(h * HEAD_SIZE, (h + 1) * HEAD_SIZE)
            stack = jnp.concatenate(
                [
                    q_ref[rows, (h * heads + g) * HEAD_SIZE : (h * heads + g + 1) * HEAD_SIZE]
                    for g in range(heads)
                ],
                axis=0,
            )
            scores = dot_nt(stack, k_ref[rows, cols]) * HEAD_SIZE ** (-0.5)
            scores = scores.reshape(heads, seq_len, seq_len)
            scores = jnp.where(allowed, scores, NEG_FILL)
            top = jnp.max(scores, axis=2, keepdims=True)
            raised = jnp.exp(scores - top)
            probs = raised / jnp.sum(raised, axis=2, keepdims=True)
            probs = probs.reshape(heads * seq_len, seq_len)
            p_ref[s, h] = probs
            mixed = dot_nn(probs.astype(bf), v_ref[rows, cols]).astype(bf)
            for g in range(heads):
                o_ref[rows, (h * heads + g) * HEAD_SIZE : (h * heads + g + 1) * HEAD_SIZE] = mixed[
                    g * seq_len : (g + 1) * seq_len
                ]
    side_out = w_full[:, base + width : base + width + 128].astype(jnp.float32).T
    aux_ref[...] = jnp.concatenate([side_out, side[:8]], axis=0)

    @pl.loop(0, width // 256)
    def _(j):
        cols = tile_cols(j, 256)
        at = pl.ds(pl.multiple_of(base + j * 256, 128), 256)
        res_ref[:, cols] = x_ref[:, cols].astype(jnp.float32) + dot_nn(o_ref[...], w_full[:, at])

    res = res_ref[...]
    inverse = lax.rsqrt(jnp.mean(res * res, axis=1, keepdims=True) + EPSILON)
    moe_row = plan["experts"]
    h2_ref[...] = (res * inverse * side_out[moe_row : moe_row + 1]).astype(bf)
    save.wait()


def run_forward(plan, order, x, cos_wide, sin_wide, lab_col, lab_row, inputs, w_cols):
    tokens, width = x.shape
    bf, f32 = jnp.bfloat16, jnp.float32
    kv_width = KEY_VALUE_HEADS * HEAD_SIZE
    seq_len = tokens // SEQ_DEV
    stack = QUERY_HEADS // KEY_VALUE_HEADS * seq_len
    vmem = pl.BlockSpec(memory_space=pltpu.VMEM)
    shape = jax.ShapeDtypeStruct
    sem = pltpu.SemaphoreType.DMA
    return pl.pallas_call(
        lambda *refs: forward_kernel(plan, *refs),
        out_shape=(
            shape((tokens, width), bf),
            shape((tokens, width), f32),
            shape((tokens, width), bf),
            shape((tokens, width), bf),
            shape((tokens, kv_width), bf),
            shape((tokens, kv_width), bf),
            shape((SEQ_DEV, KEY_VALUE_HEADS, stack, seq_len), f32),
            shape((tokens, width), bf),
            shape((136, width), f32),
            shape((width, w_cols), bf),
        ),
        in_specs=[smem_spec()] + [vmem] * 5 + [any_spec()] * len(inputs),
        out_specs=tuple([vmem] * 9 + [any_spec()]),
        scratch_shapes=[
            pltpu.VMEM((width, w_cols), bf),
            sem,
            sem,
        ],
        cost_estimate=pl.CostEstimate(flops=110000000000, transcendentals=0, bytes_accessed=16000000),
        compiler_params=pltpu.CompilerParams(vmem_limit_bytes=56 * MIB),
    )(order, x, cos_wide, sin_wide, lab_col, lab_row, *inputs)


def send_payload(order_ref, payload, start_col, outs, sem):
    cols = pl.ds(start_col, outs[0].shape[-1])
    if len(outs) == 1:
        pltpu.make_async_copy(payload.at[:, cols], outs[0], sem).start()
        return
    rows = payload.shape[0] // 32
    for c in range(2):
        x_one, y_one, x_two, y_two, own = outs[c * 5 : c * 5 + 5]
        places = [own.at[r] for r in range(4)]
        places += [x_one.at[1, 0], x_one.at[1, 1], x_two.at[0], x_two.at[1]]
        places += [y_two.at[0], y_two.at[1], y_one.at[1, 0], y_one.at[1, 1]]
        places += [x_one.at[0, 0], x_one.at[0, 1], y_one.at[0, 0], y_one.at[0, 1]]
        for j, dst in enumerate(places):
            start = pl.multiple_of(order_ref[c * 16 + j] * rows, rows)
            pltpu.make_async_copy(payload.at[pl.ds(start, rows), cols], dst, sem).start()


def payload_shapes(tuned, rows, cols):
    if not tuned:
        return (jax.ShapeDtypeStruct((rows, cols), jnp.bfloat16),)
    piece = rows // 32
    shapes = [(2, 2), (2, 2), (2,), (2,), (4,)]
    one = tuple(jax.ShapeDtypeStruct(v + (piece, cols), jnp.bfloat16) for v in shapes)
    return one + one


def backward_kernel(experts, sums, piece, order_ref, own_ref, *refs):
    given = 8 if piece else 2
    early, refs = refs[:given], refs[given:]
    back_refs = refs[:sums]
    res_ref, h2_ref, o_ref, aux_ref, x_ref, cos_ref, sin_ref = refs[sums : sums + 7]
    h1_ref, q_ref, k_ref, v_ref, p_ref, w_full_ref = refs[sums + 7 : sums + 13]
    rest = refs[sums + 13 :]
    outs = rest[:-13]
    dx_ref, w_full, dy, codes, payload, dres_ref, dres_low, dmix_ref, dqkv, dh1 = rest[-13:-3]
    sem_w, sem_d, sem_p = rest[-3:]
    tokens, width = res_ref.shape
    bf = jnp.bfloat16
    heads = QUERY_HEADS // KEY_VALUE_HEADS
    kv_width = KEY_VALUE_HEADS * HEAD_SIZE
    main = width + 2 * kv_width
    base = main + 128
    scale = HEAD_SIZE ** (-0.5)
    load = pltpu.make_async_copy(w_full_ref, w_full, sem_w.at[0])
    load.start()
    if piece:
        src = early[0].at[pl.ds(tokens, codes.shape[0]), pl.ds(0, tokens)]
        loads = deal_copies(own_ref, early, piece, 0, dy, 0, sem_d)
    else:
        src = early[1].at[own_ref[0]]
        loads = [pltpu.make_async_copy(early[0].at[own_ref[0]], dy, sem_d)]
    load_codes = pltpu.make_async_copy(src, codes, sem_w.at[1])
    load_codes.start()
    for copy in loads:
        copy.start()
    back = back_refs[0][...]
    for ref in back_refs[1:]:
        back = back + ref[...].astype(jnp.float32)
    grad_pair = (
        back[tokens : tokens + experts, :tokens]
        + back[tokens : tokens + experts, tokens : 2 * tokens]
    )
    back = back[:tokens]
    router_t = aux_ref[:experts, :].astype(bf)
    gain = aux_ref[experts : experts + 1, :]
    logits = dot_nt(router_t, h2_ref[...])
    load_codes.wait()
    chosen = codes[...].astype(jnp.float32)[:experts] > 0.0
    top = jnp.max(jnp.where(chosen, logits, NEG_FILL), axis=0, keepdims=True)
    raised = jnp.where(chosen, jnp.exp(logits - top), 0.0)
    gates = raised / jnp.sum(raised, axis=0, keepdims=True)
    inner = jnp.sum(gates * grad_pair, axis=0, keepdims=True)
    dlog = jnp.where(chosen, gates * (grad_pair - inner), 0.0).astype(bf)
    grad_router = dot_nn(dlog, h2_ref[...])
    dh2 = back + dot_tn(dlog, router_t)
    res = res_ref[...]
    inverse = lax.rsqrt(jnp.mean(res * res, axis=1, keepdims=True) + EPSILON)
    scaled = dh2 * gain
    grad_gain = jnp.sum(dh2 * res * inverse, axis=0, keepdims=True)
    pltpu.make_async_copy(dy, dy, sem_d).wait()
    dres = (
        dy[...].astype(jnp.float32)
        + inverse * scaled
        - res * inverse**3 * jnp.mean(scaled * res, axis=1, keepdims=True)
    )
    dres_ref[...] = dres
    dres_low[...] = dres.astype(bf)
    pad = jnp.zeros((128 - experts - 8, width), jnp.float32)
    side = jnp.concatenate(
        [grad_router, jnp.broadcast_to(grad_gain, (8, width)), pad], axis=0
    )
    payload[:, base + width : base + width + 128] = side.T.astype(bf)

    @pl.loop(0, width // 256)
    def _(j):
        cols = tile_cols(j, 256)
        at = pl.ds(pl.multiple_of(base + j * 256, 128), 256)
        payload[:, at] = dot_tn(o_ref[...], dres_low[:, cols]).astype(bf)

    send_payload(order_ref, payload, base, outs[len(outs) // 2 :], sem_p)
    load.wait()

    @pl.loop(0, width // 256)
    def _(j):
        cols = tile_cols(j, 256)
        dmix_ref[:, cols] = dot_nt(dres_low[...], w_full[cols, base : base + width]).astype(bf)

    seq_len = tokens // SEQ_DEV
    for s in range(SEQ_DEV):
        rows = slice(s * seq_len, (s + 1) * seq_len)
        cos_wide, sin_wide = cos_ref[rows, :], -sin_ref[rows, :]
        cos_tall = jnp.concatenate([cos_wide] * heads, axis=0)
        sin_tall = jnp.concatenate([sin_wide] * heads, axis=0)
        for h in range(KEY_VALUE_HEADS):
            cols = slice(h * HEAD_SIZE, (h + 1) * HEAD_SIZE)
            places = [
                slice((h * heads + g) * HEAD_SIZE, (h * heads + g + 1) * HEAD_SIZE)
                for g in range(heads)
            ]
            q_tall = jnp.concatenate([q_ref[rows, place] for place in places], axis=0)
            dmix = jnp.concatenate([dmix_ref[rows, place] for place in places], axis=0)
            probs = p_ref[s, h]
            dprobs = dot_nt(dmix, v_ref[rows, cols])
            dv = dot_tn(probs.astype(bf), dmix)
            inner = jnp.sum(probs * dprobs, axis=1, keepdims=True)
            dscores = (probs * (dprobs - inner)).astype(bf)
            dq = rotate(dot_nn(dscores, k_ref[rows, cols]) * scale, cos_tall, sin_tall)
            dk = rotate(dot_tn(dscores, q_tall) * scale, cos_wide, sin_wide)
            for g, place in enumerate(places):
                dqkv[rows, place] = dq[g * seq_len : (g + 1) * seq_len].astype(bf)
            dqkv[rows, width + h * HEAD_SIZE : width + (h + 1) * HEAD_SIZE] = dk.astype(bf)
            at = width + kv_width + h * HEAD_SIZE
            dqkv[rows, at : at + HEAD_SIZE] = dv.astype(bf)
    @pl.loop(0, width // 256)
    def _(j):
        cols = tile_cols(j, 256)
        dh1[:, cols] = dot_nt(dqkv[...], w_full[cols, :main])

    @pl.loop(0, main // 256)
    def _(j):
        cols = tile_cols(j, 256)
        payload[:, cols] = dot_tn(h1_ref[...], dqkv[:, cols]).astype(bf)

    x = x_ref[...].astype(jnp.float32)
    gain = aux_ref[128:129, :]
    inverse = lax.rsqrt(jnp.mean(x * x, axis=1, keepdims=True) + EPSILON)
    grad = dh1[...]
    scaled = grad * gain
    grad_gain = jnp.sum(grad * x * inverse, axis=0, keepdims=True)
    payload[:, main : main + 128] = jnp.broadcast_to(grad_gain, (128, width)).T.astype(bf)
    dx = (
        dres_ref[...]
        + inverse * scaled
        - x * inverse**3 * jnp.mean(scaled * x, axis=1, keepdims=True)
    )
    send_payload(order_ref, payload, 0, outs[: len(outs) // 2], sem_p)
    dx_ref[...] = dx.astype(bf)
    pltpu.make_async_copy(payload, payload, sem_p).wait()


def run_backward(tuned, experts, piece, order, own, early, rows, backs, saved, w_full):
    tokens, width = saved[0].shape
    bf, f32 = jnp.bfloat16, jnp.float32
    vmem = pl.BlockSpec(memory_space=pltpu.VMEM)
    shape = jax.ShapeDtypeStruct
    sem = pltpu.SemaphoreType.DMA
    main = width + 2 * KEY_VALUE_HEADS * HEAD_SIZE
    payload = payload_shapes(tuned, width, main + 128)
    payload = payload + payload_shapes(tuned, width, width + 128)
    return pl.pallas_call(
        lambda *refs: backward_kernel(experts, len(backs), piece, *refs),
        out_shape=payload + (shape((tokens, width), bf),),
        in_specs=[smem_spec()] * 2
        + [any_spec()] * len(early)
        + [vmem] * (len(backs) + len(saved))
        + [any_spec()],
        out_specs=tuple([any_spec()] * len(payload) + [vmem]),
        scratch_shapes=[
            pltpu.VMEM(w_full.shape, bf),
            pltpu.VMEM((tokens, width), bf),
            pltpu.VMEM((rows, tokens), bf),
            pltpu.VMEM(w_full.shape, bf),
            pltpu.VMEM((tokens, width), f32),
            pltpu.VMEM((tokens, width), bf),
            pltpu.VMEM((tokens, width), bf),
            pltpu.VMEM((tokens, main), bf),
            pltpu.VMEM((tokens, width), f32),
            sem((2,)),
            sem,
            sem,
        ],
        cost_estimate=pl.CostEstimate(
            flops=181000000000, transcendentals=0, bytes_accessed=32000000
        ),
        compiler_params=pltpu.CompilerParams(vmem_limit_bytes=60 * MIB),
    )(order, own, *early, *backs, *saved, w_full)


def after(value, *others):
    return lax.optimization_barrier((value,) + others)[0]


def swap_diagonal(value):
    return lax.ppermute(value, "dp", [(i, i ^ 3) for i in range(4)])


def shift_two(value):
    return lax.ppermute(value, "expert", [(i, (i + 4) % 8) for i in range(8)])


def gather_front(pack, early, sent, w_gate, w_up, w_down, tuned):
    if not tuned:
        got = lax.all_to_all(sent, "expert", split_axis=0, concat_axis=2, tiled=True)
        full = lax.all_gather(pack, ("dp", "expert"), axis=0, tiled=True)
        dealt = [lax.all_gather(early, "expert", axis=0, tiled=False)]
        weights = [
            lax.all_gather(w_gate, "dp", axis=1, tiled=True),
            lax.all_gather(w_up, "dp", axis=1, tiled=True),
            lax.all_gather(w_down, "dp", axis=2, tiled=True),
        ]
        return got, [full], [(0, (), None)], dealt, weights
    both = jnp.stack([w_gate, w_up])
    ring = (pack, shift_up(pack), shift_down(pack), shift_two(pack))
    down_x = swap_x(w_down)
    down_y = swap_y(w_down)
    down = [w_down, down_x, down_y, swap_x(down_y[:1]), swap_y(down_x[1:])]
    *ring, _, _, both = lax.optimization_barrier(ring + tuple(down[1:3]) + (both,))
    level = after(jnp.stack(ring), *down)
    from_x = swap_x(level)
    from_y = swap_y(level)
    sent = after(sent, level)
    got = lax.all_to_all(sent, "expert", split_axis=0, concat_axis=2, tiled=True)
    early = after(early, level)
    below = shift_up(early)
    above = shift_down(early)
    far_a = swap_x(from_y[:2])
    far_b = swap_y(from_x[2:])
    both = after(both, far_a, far_b)
    both_x = swap_x(both)
    both_y = swap_y(both)
    dealt = [early, below, above, shift_up(below)]
    dealt = dealt + [swap_core(v) for v in dealt]
    arrays = [level, from_x, from_y, far_a, far_b]
    late = lax.optimization_barrier((far_a, far_b, below, above))[:2]
    arrays = arrays + [swap_core(v) for v in arrays[:3]] + [swap_core(v) for v in late]
    places = []
    for c in range(2):
        for k in range(4):
            for r in range(4):
                ref, lead = (k, r) if k < 3 else ((3, r) if r < 2 else (4, r - 2))
                places.append((c * 5 + ref, (lead,), (c * 4 + k) * 4 + r))
    return got, arrays, places, dealt, (both, both_x, both_y) + tuple(down)


def scatter_core(outs):
    got = [swap_core(v) for v in outs[5:]]
    return [add_low(outs[k], got[k]) for k in range(4)] + [outs[4], got[4]]


def scatter_planes(sums, first):
    x_one, y_one, x_two, y_two, own, got_own = sums
    x_two = swap_x(add_low(x_two, first[1][0]))
    y_two = swap_y(add_low(y_two, first[0][0]))
    level = []
    for r in range(4):
        near = (first[0][1, r], y_two[r]) if r < 2 else (x_two[r - 2], first[1][1, r - 2])
        total = own[r].astype(jnp.float32) + got_own[r].astype(jnp.float32)
        total = total + near[0].astype(jnp.float32) + near[1].astype(jnp.float32)
        level.append(total if r == 0 else total.astype(jnp.bfloat16))
    return level


def scatter_ring(level, others, short):
    below, above, far = level[1:]
    if short:
        got = [shift_down(below), shift_up(add_low(above, shift_up(far)))]
    else:
        got = [shift_down(below), shift_up(above), shift_two(far)]
    last, *others = lax.optimization_barrier((level[0],) + tuple(others))
    for v in got:
        last = last + v.astype(jnp.float32)
    return last, others


def scatter_payload(outs, tuned, others, more, grad_x):
    half = len(outs) // 2
    if not tuned:
        owned = [
            lax.psum_scatter(v, ("dp", "expert"), scatter_dimension=0, tiled=True) for v in outs
        ]
        return [v.astype(jnp.float32) for v in owned], others, more, grad_x
    first = scatter_core(outs[:half])
    second = scatter_core(outs[half:])
    first_got = [swap_x(first[0]), swap_y(first[1])]
    first_level = scatter_planes(first, first_got)
    *sent, grad_x = lax.optimization_barrier((second[0], second[1], grad_x))
    sent = lax.optimization_barrier(tuple(sent) + tuple(first_got))
    second_got = [swap_x(sent[0]), swap_y(sent[1])]
    second_level = scatter_planes(second, second_got)
    more = lax.optimization_barrier(tuple(more) + (first_level[1],))[:-1]
    owned_in, _ = scatter_ring(first_level, second_level[1:2], True)
    owned_out, others = scatter_ring(second_level, others, False)
    return [owned_in, owned_out], others, more, grad_x


def sum_whole(keep, send):
    blocks = jnp.concatenate([keep, send], axis=0)
    sums = lax.psum_scatter(blocks, "expert", scatter_dimension=0, tiled=False)
    return [sums.astype(jnp.float32)]


def sum_messages(keep, got):
    sums = [keep[i].astype(jnp.float32) + got[i].astype(jnp.float32) for i in range(4)]
    return [sums[0]] + [v.astype(jnp.bfloat16) for v in sums[1:]]


def sum_ring(messages, between):
    own, to_below, to_above, far = messages
    got_far = shift_up(far)
    from_above = shift_down(to_below)
    if between is not None:
        to_above = after(to_above, between)
    onward = add_low(to_above, got_far)
    return [own, from_above, shift_up(onward)], onward


def deal_back(value, placement):
    tokens, width = value.shape
    value = value.reshape(1, SEQ_DEV, tokens // SEQ_DEV, width)
    value = lax.all_to_all(value, "expert", split_axis=2, concat_axis=0, tiled=True)
    return value.reshape(placement.shape[0], -1, width)[placement]


def pad_columns(value, width):
    return jnp.pad(value, ((0, 0), (0, width - value.shape[1])))


def body(
    tokens,
    cotangent,
    lengths,
    placement,
    routes,
    priority,
    g_attn,
    w_query,
    key_projection,
    value_projection,
    w_out,
    g_moe,
    w_router,
    w_gate,
    w_up,
    w_down,
):
    row_seqs, piece_len, width = tokens.shape
    expert_devices = lax.axis_size("expert")
    plane_size = lax.axis_size("dp")
    tuned = expert_devices == 8 and plane_size == 4
    my_index = lax.axis_index("expert")
    seq_len = piece_len * expert_devices
    token_count = SEQ_DEV * seq_len
    query_width = w_query.shape[1]
    kv_width = key_projection.shape[1]
    expert_count = w_router.shape[1]
    per_device = expert_count // expert_devices
    capacity = (9 * token_count * TOPK + 64 * expert_count - 1) // (64 * expert_count) * 8
    code_list = jnp.arange(row_seqs, dtype=jnp.int32)
    source = jnp.sum(
        jnp.where(placement[:, None] == code_list[None, :], code_list[:, None], 0), axis=0
    )
    pack = jnp.concatenate(
        [
            w_query,
            key_projection,
            value_projection,
            pad_columns(g_attn[:, None], 128),
            w_out,
            pad_columns(jnp.concatenate([w_router, g_moe[:, None]], axis=1), 128),
        ],
        axis=1,
    )
    sent = tokens[source].reshape(expert_devices, SEQ_DEV, piece_len, width)
    ranks = slot_ranks(routes.reshape(-1), priority.reshape(-1)).reshape(token_count, TOPK)
    codes = jnp.minimum(ranks, capacity) + 1
    expert_list = jnp.arange(expert_count, dtype=jnp.int32)
    picks = routes[None, :, :] == expert_list[:, None, None]
    code_table = jnp.sum(jnp.where(picks, codes[None], 0), axis=2)
    table_rows = -(-expert_count // 16) * 16
    table = jnp.zeros((table_rows, width), jnp.bfloat16)
    table = table.at[:expert_count, :token_count].set(code_table.astype(jnp.bfloat16))
    early = jnp.concatenate([cotangent.reshape(token_count, width), table], axis=0)
    got_tokens, pack_parts, pack_places, early_parts, weights = gather_front(
        pack, early, sent, w_gate, w_up, w_down, tuned
    )
    x_local = got_tokens.reshape(token_count, width)
    order = expert_order(tuned, expert_devices)
    seqs = source.reshape(expert_devices, SEQ_DEV)[order].reshape(-1)
    rel_of = jnp.sum(
        jnp.where(
            order[None, :] == jnp.arange(expert_devices)[:, None],
            jnp.arange(expert_devices)[None, :],
            0,
        ),
        axis=1,
    )
    plane = lax.axis_index("dp").reshape(1)
    scalars = jnp.concatenate([my_index.reshape(1), seqs, order, rel_of, plane])
    scalars = scalars.astype(jnp.int32)
    grads_all = jnp.zeros((16, 128), jnp.bfloat16)
    codes_all = grads_all
    if not tuned:
        early_all = early_parts[0]
        pieces = early_all[:, :token_count].reshape(expert_devices, row_seqs, piece_len, width)
        pieces = pieces[:, seqs].reshape(
            expert_devices, expert_devices, SEQ_DEV, piece_len, width
        )
        grads_all = pieces.transpose(1, 2, 0, 3, 4).reshape(expert_devices, token_count, width)
        codes_all = early_all[:, token_count:, :token_count]
        early_parts = []
    own_seqs = lax.dynamic_slice_in_dim(source, my_index * SEQ_DEV, SEQ_DEV)
    positions, labels = device_layout(lengths[own_seqs], seq_len)
    cosine_table, sine_values = rope_tables(positions, HEAD_SIZE)
    cos_wide = jnp.concatenate([cosine_table, cosine_table], axis=1)
    sin_wide = jnp.concatenate([-sine_values, sine_values], axis=1)
    plan = {
        "inputs": len(pack_parts),
        "experts": expert_count,
        "places": pack_places,
    }
    row_order = all_order()
    normed_moe, residual, h1, q, k, v, probs, mixed, aux, w_full = run_forward(
        plan,
        row_order,
        x_local,
        cos_wide,
        sin_wide,
        labels[:, None],
        labels[None, :],
        pack_parts,
        pack.shape[1],
    )
    inputs, weight_places, token_places = gather_inputs(normed_moe, weights, per_device, tuned)
    inputs = inputs + early_parts
    plan = {
        "inputs": len(inputs),
        "blocks": expert_devices,
        "per_device": per_device,
        "ff": w_gate.shape[2],
        "weights": weight_places,
        "tokens": token_places,
        "token_count": token_count,
        "piece": piece_len,
        "early": list(range(len(inputs) - len(early_parts), len(inputs))),
    }
    router_t = aux[:expert_count].astype(jnp.bfloat16)
    back_keep, back_send, out_keep, out_send, x_slots, dy_slots, hid, dga, dua = run_experts(
        plan, capacity, table_rows, scalars, router_t, codes_all, grads_all, residual, inputs
    )
    if tuned:
        back_got = swap_core(back_send)
        out_got = swap_core(after(out_send, back_got))
        messages = sum_messages(back_keep, back_got)
        x_slots = after(x_slots, *messages)
    if width // plane_size * 2 == w_gate.shape[2] and width % (128 * plane_size) == 0:
        weight_grads = expert_weight_grads(x_slots, dga, dua, hid, dy_slots, plane_size)
        flat = weight_grads.reshape(-1, weight_grads.shape[-1])
        owned = lax.psum_scatter(flat, "dp", scatter_dimension=0, tiled=True)
        owned = owned.reshape(weight_grads.shape[1:])
        half = owned.shape[-1] // 2
        owned_gate, owned_up = owned[0].astype(jnp.float32), owned[1].astype(jnp.float32)
        owned_down = jnp.concatenate([owned[2, :, :, :half], owned[2, :, :, half:]], axis=1)
    else:
        gate_up, down = whole_weight_grads(x_slots, dga, dua, hid, dy_slots)
        owned = lax.psum_scatter(gate_up, "dp", scatter_dimension=2, tiled=True)
        owned_gate, owned_up = owned[0].astype(jnp.float32), owned[1].astype(jnp.float32)
        owned_down = lax.psum_scatter(down, "dp", scatter_dimension=2, tiled=True)
    owned_down = owned_down.astype(jnp.float32)
    if tuned:
        backs, _ = sum_ring(messages, weight_grads)
        messages = sum_messages(after(out_keep, backs[1]), out_got)
        backs[0] = after(backs[0], *messages)
        messages[1:] = lax.optimization_barrier(tuple(messages[1:]) + tuple(backs[1:]))[:3]
    else:
        backs = sum_whole(back_keep, back_send)
        sums = sum_whole(out_keep, out_send)
    final = run_backward(
        tuned,
        expert_count,
        piece_len if tuned else 0,
        row_order,
        scalars,
        early_parts if tuned else [grads_all, codes_all],
        table_rows,
        backs,
        [
            residual,
            normed_moe,
            mixed,
            aux,
            x_local,
            cos_wide,
            sin_wide,
            h1,
            q,
            k,
            v,
            probs,
        ],
        w_full,
    )
    payload, grad_x = final[:-1], final[-1]
    if tuned:
        sums, onward = sum_ring(messages, grad_x)
        *payload, _ = lax.optimization_barrier(tuple(payload) + (onward,))
    others = (owned_gate, owned_up, owned_down)
    (owned_in, owned_out), others, more, grad_x = scatter_payload(
        payload, tuned, others, sums, grad_x
    )
    owned_gate, owned_up, owned_down = others
    if tuned:
        sums = list(more)
    if tuned:
        total = sums[0] + sums[1].astype(jnp.float32) + sums[2].astype(jnp.float32)
        output = total.astype(jnp.bfloat16).reshape(row_seqs, piece_len, width)
    else:
        output = deal_back((residual + sums[0]).astype(jnp.bfloat16), placement)
    input_grad = deal_back(grad_x, placement)
    return (
        output,
        input_grad,
        owned_in[:, query_width + 2 * kv_width],
        owned_in[:, :query_width],
        owned_in[:, query_width : query_width + kv_width],
        owned_in[:, query_width + kv_width : query_width + 2 * kv_width],
        owned_out[:, :width],
        owned_out[:, width + expert_count],
        owned_out[:, width : width + expert_count],
        owned_gate,
        owned_up,
        owned_down,
    )


def solution(mesh):
    return jax.shard_map(
        body,
        mesh=mesh,
        in_specs=(
            P("dp", "expert", None),
            P("dp", "expert", None),
            P("dp", None),
            P("dp"),
            P(("dp", "expert"), None),
            P(("dp", "expert"), None),
            P(("dp", "expert")),
            P(("dp", "expert"), None),
            P(("dp", "expert"), None),
            P(("dp", "expert"), None),
            P(("dp", "expert"), None),
            P(("dp", "expert")),
            P(("dp", "expert"), None),
            P("expert", "dp", None),
            P("expert", "dp", None),
            P("expert", None, "dp"),
        ),
        out_specs=(
            P("dp", "expert", None),
            P("dp", "expert", None),
            P(("dp", "expert")),
            P(("dp", "expert"), None),
            P(("dp", "expert"), None),
            P(("dp", "expert"), None),
            P(("dp", "expert"), None),
            P(("dp", "expert")),
            P(("dp", "expert"), None),
            P("expert", "dp", None),
            P("expert", "dp", None),
            P("expert", None, "dp"),
        ),
        check_vma=False,
    )
```

```python
import math

import jax
import jax.numpy as jnp
from jax import lax
from jax.experimental import pallas as pl
from jax.experimental.pallas import tpu as pltpu
from jax.sharding import PartitionSpec as P

QUERY_HEADS = 12
KEY_VALUE_HEADS = 2
HEAD_SIZE = 128
TOPK = 4
SEQ_DEV = 2


EPSILON = 1e-06
ROPE_BASE = 1000000.0
NEG_FILL = -1e30


def sequence_layout(doc_lens, seq_len):
    token_steps = jnp.arange(seq_len, dtype=jnp.int32)
    doc_ends = jnp.cumsum(doc_lens)
    doc_index = jnp.sum((token_steps[:, None] >= doc_ends[None, :-1]).astype(jnp.int32), axis=1)
    doc_starts = doc_ends - doc_lens
    doc_slots = jnp.arange(doc_lens.shape[0], dtype=jnp.int32)
    start_of = jnp.sum(
        jnp.where(doc_slots[None, :] == doc_index[:, None], doc_starts[None, :], 0), axis=1
    )
    return ((token_steps - start_of).astype(jnp.float32), doc_index)


def device_layout(dev_lens, seq_len):
    positions, doc_index = jax.vmap(lambda single: sequence_layout(single, seq_len))(dev_lens)
    doc_count = dev_lens.shape[1]
    labels = doc_index + doc_count * jnp.arange(dev_lens.shape[0], dtype=jnp.int32)[:, None]
    return (positions.reshape(-1), labels.reshape(-1))


def rope_tables(positions, head_dim):
    freq_index = jnp.arange(head_dim // 2, dtype=jnp.float32)
    frequency = jnp.exp(freq_index * (-2.0 / head_dim) * math.log(ROPE_BASE))
    angle_table = positions[:, None] * frequency[None, :]
    return (jnp.cos(angle_table), jnp.sin(angle_table))


def slot_ranks(route_flat, prio_flat):
    same = route_flat[:, None] == route_flat[None, :]
    ahead = prio_flat[None, :] < prio_flat[:, None]
    return jnp.sum(jnp.logical_and(same, ahead).astype(jnp.int32), axis=1)


def swap_x(value):
    return lax.ppermute(value, "dp", [(i, i ^ 1) for i in range(4)])


def swap_y(value):
    return lax.ppermute(value, "dp", [(i, i ^ 2) for i in range(4)])


def swap_core(value):
    return lax.ppermute(value, "expert", [(i, i ^ 1) for i in range(8)])


def shift_up(value):
    return lax.ppermute(value, "expert", [(i, (i + 2) % 8) for i in range(8)])


def shift_down(value):
    return lax.ppermute(value, "expert", [(i, (i + 6) % 8) for i in range(8)])


def add_low(left, right):
    return (left.astype(jnp.float32) + right.astype(jnp.float32)).astype(jnp.bfloat16)


def any_spec():
    return pl.BlockSpec(memory_space=pl.ANY)


def smem_spec():
    return pl.BlockSpec(memory_space=pltpu.SMEM)


def expert_order(tuned, count):
    if not tuned:
        return jnp.arange(count, dtype=jnp.int32)
    me = lax.axis_index("expert")
    level, core = me // 2, me % 2
    order = [
        ((level + off) % 4) * 2 + (core + flip) % 2 for flip in range(2) for off in (0, 3, 1, 2)
    ]
    return jnp.stack(order).astype(jnp.int32)


def all_order():
    me = lax.axis_index("expert")
    plane = lax.axis_index("dp")
    level, core = me // 2, me % 2
    order = [
        ((plane ^ k) * 4 + (level + off) % 4) * 2 + (core + flip) % 2
        for flip in range(2)
        for k in range(4)
        for off in (0, 3, 1, 2)
    ]
    return jnp.stack(order).astype(jnp.int32)


def dot_nn(left, right):
    return lax.dot_general(
        left, right, (((1,), (0,)), ((), ())), preferred_element_type=jnp.float32
    )


def dot_nt(left, right):
    return lax.dot_general(
        left, right, (((1,), (1,)), ((), ())), preferred_element_type=jnp.float32
    )


def dot_tn(left, right):
    return lax.dot_general(
        left, right, (((0,), (0,)), ((), ())), preferred_element_type=jnp.float32
    )


GELU_SCALE = math.sqrt(2.0 / math.pi)
GELU_CUBE = 0.044715
MIB = 1024 * 1024


def deal_copies(scalar_ref, early, piece, block, dst, row, sem):
    devices = len(early)
    copies = []
    for k in range(SEQ_DEV):
        start = pl.multiple_of(scalar_ref[1 + block * SEQ_DEV + k] * piece, piece)
        for q in range(devices):
            place = scalar_ref[1 + devices * SEQ_DEV + q] * piece
            to = pl.multiple_of(row + k * devices * piece + place, piece)
            copies.append(
                pltpu.make_async_copy(
                    early[q].at[pl.ds(start, piece), :], dst.at[pl.ds(to, piece), :], sem
                )
            )
    return copies


def give_back(scalar_ref, piece, block, src, keep, send, sem):
    devices = keep.shape[0] + send.shape[0]
    half = devices // 2
    for j in range(devices):
        to = scalar_ref[1 + devices * SEQ_DEV + devices + j]
        for k in range(SEQ_DEV):
            start = pl.multiple_of(scalar_ref[1 + block * SEQ_DEV + k] * piece, piece)
            part = src.at[pl.ds((k * devices + j) * piece, piece), :]

            @pl.when(to < half)
            def _(part=part, to=to, start=start):
                dst = keep.at[to, pl.ds(start, piece), :]
                pltpu.make_async_copy(part, dst, sem).start()

            @pl.when(to >= half)
            def _(part=part, to=to, start=start):
                dst = send.at[to - half, pl.ds(start, piece), :]
                pltpu.make_async_copy(part, dst, sem).start()


def expert_kernel(plan, capacity, *refs):
    count = plan["inputs"]
    my_ref, router_ref, codes_ref, grads_ref, res_ref = refs[:5]
    inputs = refs[5 : 5 + count]
    (
        back_keep,
        back_send,
        out_keep,
        out_send,
        x_out,
        dy_out,
        hid_out,
        dga_out,
        dua_out,
    ) = refs[5 + count : 14 + count]
    (
        gate_w,
        up_w,
        down_w,
        h_buf,
        d_buf,
        hot,
        x_s,
        dy_s,
        y_s,
        dx_s,
        hid_s,
        dga_s,
        dua_s,
        act_s,
        slope_s,
        codes_all,
        code_lines,
        code_s,
        gates_s,
        sgate_s,
        dg_s,
        stage_b,
        stage_o,
        sem_w,
        sem_h,
        sem_d,
        sem_c,
        sem_s,
        sem_b,
        sem_o,
    ) = refs[14 + count :]
    blocks = plan["blocks"]
    pairs = blocks // 2
    per_device, width, ff = gate_w.shape
    tokens = h_buf.shape[1] // 2
    slots = 2 * capacity
    experts = router_ref.shape[0]
    rows_all = x_s.shape[1]
    my_first = my_ref[0] * per_device
    dtype = jnp.bfloat16

    plane = my_ref[my_ref.shape[0] - 1]

    def window(hold, axis, e, flip, step):
        start = 0 if flip is None else pl.multiple_of((plane ^ flip) * step, step)
        if axis == 1:
            return hold.at[e, pl.ds(start, step), :]
        return hold.at[e, :, pl.ds(start, step)]

    weight_copies = []
    for t, (hold, axis) in enumerate(((gate_w, 1), (up_w, 1), (down_w, 2))):
        for e in range(per_device):
            copies = []
            for ref_index, lead, flip in plan["weights"][t][e]:
                src = inputs[ref_index].at[lead]
                step = src.shape[axis - 1]
                sem = sem_w.at[t * per_device + e, len(copies)]
                copy = pltpu.make_async_copy(src, window(hold, axis, e, flip, step), sem)
                copy.start()
                copies.append(copy)
            weight_copies.append(copies)

    early = [inputs[i] for i in plan["early"]]
    if early:
        for b, ref in enumerate(early):
            src = ref.at[pl.ds(tokens, codes_all.shape[1]), pl.ds(0, tokens)]
            pltpu.make_async_copy(src, codes_all.at[b], sem_c).start()
    else:
        pltpu.make_async_copy(codes_ref, codes_all, sem_c).start()

    def fetch(p):
        slot = p % 2
        copies = []
        for half in range(2):
            for k, (ref_index, lead, row, rows) in enumerate(plan["tokens"][2 * p + half]):
                src = inputs[ref_index] if lead is None else inputs[ref_index].at[lead]
                dst = h_buf.at[slot, pl.ds(half * tokens + row, rows), :]
                copies.append(pltpu.make_async_copy(src, dst, sem_h.at[slot, half, k]))
        if early:
            deals = []
            for half in range(2):
                deals += deal_copies(
                    my_ref,
                    early,
                    plan["piece"],
                    2 * p + half,
                    d_buf.at[slot],
                    half * tokens,
                    sem_d.at[slot],
                )
        else:
            deals = [
                pltpu.make_async_copy(
                    grads_ref.at[2 * p + half],
                    d_buf.at[slot, pl.ds(half * tokens, tokens), :],
                    sem_d.at[slot],
                )
                for half in range(2)
            ]
        for copy in copies + deals:
            copy.start()
        return copies + [pltpu.make_async_copy(d_buf.at[slot], d_buf.at[slot], sem_d.at[slot])]

    def hits(codes_of, shape, slot_axis):
        slot = lax.broadcasted_iota(jnp.int32, shape, slot_axis)
        token = lax.broadcasted_iota(jnp.int32, shape, 1 - slot_axis)
        second = slot >= capacity
        same = jnp.logical_xor(second, token < tokens)
        rank = slot - jnp.where(second, capacity, 0)
        return jnp.logical_and(same, codes_of == (rank + 1).astype(jnp.float32))

    flying = fetch(0)
    pltpu.make_async_copy(codes_all, codes_all, sem_c).wait()
    for p in range(pairs):
        slot = p % 2
        later = fetch(p + 1) if p + 1 < pairs else []
        for copy in flying:
            copy.wait()
        flying = later
        codes = jnp.concatenate([codes_all[2 * p], codes_all[2 * p + 1]], axis=1)
        codes = codes.astype(jnp.float32)[:experts]
        logits = dot_nt(router_ref[...], h_buf[slot])
        chosen = codes > 0.0
        top = jnp.max(jnp.where(chosen, logits, NEG_FILL), axis=0, keepdims=True)
        raised = jnp.where(chosen, jnp.exp(logits - top), 0.0)
        code_s[...] = codes
        gates_s[...] = raised / jnp.sum(raised, axis=0, keepdims=True)
        flipped = codes.T
        lane = lax.broadcasted_iota(jnp.int32, flipped.shape, 1)
        picks, ones = [], []
        for e in range(per_device):
            code_row = code_s[pl.ds(my_first + e, 1), :]
            gate_row = gates_s[pl.ds(my_first + e, 1), :]
            hit = hits(code_row, (slots, 2 * tokens), 0)
            code_lines[e, p] = code_row
            picks.append(jnp.where(hit, 1.0, 0.0).astype(dtype))
            gate_slot = jnp.sum(jnp.where(hit, gate_row, 0.0), axis=1, keepdims=True)
            sgate_s[e, pl.ds(p * slots, slots), :] = jnp.broadcast_to(gate_slot, (slots, 128))
            code_col = jnp.sum(
                jnp.where(lane == my_first + e, flipped, 0.0), axis=1, keepdims=True
            )
            ones.append(jnp.where(hits(code_col, (2 * tokens, slots), 1), 1.0, 0.0).astype(dtype))
        pick = jnp.concatenate(picks, axis=0)
        hot[p] = jnp.concatenate(ones, axis=1)
        for hold, buf in ((x_s, h_buf), (dy_s, d_buf)):
            taken = dot_nn(pick, buf[slot]).astype(dtype)
            for e in range(per_device):
                hold[e, pl.ds(p * slots, slots), :] = taken[e * slots : (e + 1) * slots]

    saves = []
    for e in range(per_device):
        for copy in weight_copies[e] + weight_copies[per_device + e]:
            copy.wait()
        save = pltpu.make_async_copy(x_s.at[e], x_out.at[e], sem_s.at[0, e])
        save.start()
        saves.append(save)
        gate_slot = sgate_s[e][:, :1]

        act_s[...] = dot_nn(x_s[e], gate_w[e])
        slope_s[...] = dot_nn(x_s[e], up_w[e])

        @pl.loop(0, rows_all // slots)
        def _(j):
            rows = pl.ds(pl.multiple_of(j * slots, slots), slots)
            ga = act_s[rows, :]
            ua = slope_s[rows, :]
            square = ga * ga
            tan = jnp.tanh(GELU_SCALE * (ga + GELU_CUBE * square * ga))
            act = 0.5 * ga * (1.0 + tan)
            slope = 0.5 * (1.0 + tan) + 0.5 * ga * (1.0 - tan * tan) * GELU_SCALE * (
                1.0 + 3.0 * GELU_CUBE * square
            )
            act_s[rows, :] = act
            slope_s[rows, :] = ua * slope
            hid_s[e, rows, :] = (act * ua).astype(dtype)

        save = pltpu.make_async_copy(hid_s.at[e], hid_out.at[e], sem_s.at[1, e])
        save.start()
        saves.append(save)
        for copy in weight_copies[2 * per_device + e]:
            copy.wait()
        dg_s[e] = jnp.zeros(dg_s.shape[1:], jnp.float32)

        @pl.loop(0, width // 768)
        def _(j):
            cols = pl.ds(pl.multiple_of(j * 768, 768), 768)
            y = dot_nn(hid_s[e], down_w[e, :, cols]).astype(dtype).astype(jnp.float32)
            dy = dy_s[e, :, cols].astype(jnp.float32)
            dg_s[e] += jnp.broadcast_to(
                jnp.sum(dy * y, axis=1, keepdims=True), dg_s.shape[1:]
            )
            y_s[e, :, cols] = (gate_slot * y).astype(dtype)
            dy_s[e, :, cols] = (gate_slot * dy).astype(dtype)

        save = pltpu.make_async_copy(dy_s.at[e], dy_out.at[e], sem_s.at[2, e])
        save.start()
        saves.append(save)

        dhid = dot_nt(dy_s[e], down_w[e])
        dga_s[e] = (dhid * slope_s[...]).astype(dtype)
        dua_s[e] = (dhid * act_s[...]).astype(dtype)

        for k, (hold, out) in enumerate(((dga_s, dga_out), (dua_s, dua_out))):
            save = pltpu.make_async_copy(hold.at[e], out.at[e], sem_s.at[3 + k, e])
            save.start()
            saves.append(save)

        @pl.loop(0, width // 768)
        def _(j):
            cols = pl.ds(pl.multiple_of(j * 768, 768), 768)
            dx = dot_nt(dga_s[e], gate_w[e, cols, :]) + dot_nt(dua_s[e], up_w[e, cols, :])
            dx_s[e, :, cols] = dx.astype(dtype)

    table_rows = stage_b.shape[2] - tokens
    table_row = lax.broadcasted_iota(jnp.int32, (table_rows, 2 * tokens), 0)
    sends = {}
    for p in range(pairs):
        slot = p % 2
        for copy in sends.pop(p - 2, []):
            copy.wait()
        rows = pl.ds(p * slots, slots)

        @pl.loop(0, width // 768)
        def _(j):
            cols = pl.ds(pl.multiple_of(j * 768, 768), 768)
            back, outs = [
                dot_nn(
                    hot[p],
                    jnp.concatenate([hold[e, rows, cols] for e in range(per_device)], axis=0),
                )
                for hold in (dx_s, y_s)
            ]
            for half in range(2):
                part = slice(half * tokens, (half + 1) * tokens)
                stage_b[slot, half, :tokens, cols] = back[part].astype(dtype)
                mixed = outs[part]
                if early and p == 0 and half == 0:
                    mixed = mixed + res_ref[:, cols]
                stage_o[slot, half, :, cols] = mixed.astype(dtype)

        tables = [jnp.zeros((table_rows, 2 * tokens), jnp.float32) for _ in range(2)]
        for e in range(per_device):
            dg = dg_s[e, rows, :][:, :1]
            code_row = code_lines[e, p]
            line = jnp.sum(
                jnp.where(hits(code_row, (slots, 2 * tokens), 0), dg, 0.0), axis=0, keepdims=True
            )
            mine = table_row == my_first + e
            for half in range(2):
                part = line[:, half * tokens : (half + 1) * tokens]
                high = part.astype(dtype).astype(jnp.float32)
                both = jnp.concatenate([high, part - high], axis=1)
                tables[half] = jnp.where(mine, both, tables[half])
        for half in range(2):
            stage_b[slot, half, tokens:, : 2 * tokens] = tables[half].astype(dtype)
            stage_b[slot, half, tokens:, 2 * tokens :] = jnp.zeros(
                (table_rows, width - 2 * tokens), dtype
            )
        first = 2 * p
        keep = first < blocks // 2
        at = pl.ds(first if keep else first - blocks // 2, 2)
        copies = [
            pltpu.make_async_copy(
                stage_b.at[slot], (back_keep if keep else back_send).at[at], sem_b.at[slot]
            )
        ]
        if early:
            for half in range(2):
                give_back(
                    my_ref,
                    plan["piece"],
                    first + half,
                    stage_o.at[slot, half],
                    out_keep,
                    out_send,
                    sem_o.at[slot],
                )
        else:
            copies.append(
                pltpu.make_async_copy(
                    stage_o.at[slot], (out_keep if keep else out_send).at[at], sem_o.at[slot]
                )
            )
        for copy in copies:
            copy.start()
        if early:
            copies.append(
                pltpu.make_async_copy(stage_o.at[slot], stage_o.at[slot], sem_o.at[slot])
            )
        sends[p] = copies
    for copies in sends.values():
        for copy in copies:
            copy.wait()
    for save in saves:
        save.wait()


def run_experts(plan, capacity, table_rows, scalars, router_t, codes, grads_all, res, inputs):
    experts, width = router_t.shape
    blocks, tokens = plan["blocks"], plan["token_count"]
    per_device, ff = plan["per_device"], plan["ff"]
    rows = blocks * capacity
    bf, f32 = jnp.bfloat16, jnp.float32
    half = blocks // 2
    back = jax.ShapeDtypeStruct((half, tokens + table_rows, width), bf)
    outs = jax.ShapeDtypeStruct((half, tokens, width), bf)
    wide = jax.ShapeDtypeStruct((per_device, rows, width), bf)
    thin = jax.ShapeDtypeStruct((per_device, rows, ff), bf)
    vmem = pl.BlockSpec(memory_space=pltpu.VMEM)
    sem = pltpu.SemaphoreType.DMA
    return pl.pallas_call(
        lambda *refs: expert_kernel(plan, capacity, *refs),
        out_shape=(back, back, outs, outs, wide, wide, thin, thin, thin),
        in_specs=[smem_spec(), vmem, any_spec(), any_spec(), vmem] + [any_spec()] * len(inputs),
        out_specs=tuple([any_spec()] * 9),
        scratch_shapes=[
            pltpu.VMEM((per_device, width, ff), bf),
            pltpu.VMEM((per_device, width, ff), bf),
            pltpu.VMEM((per_device, ff, width), bf),
            pltpu.VMEM((2, 2 * tokens, width), bf),
            pltpu.VMEM((2, 2 * tokens, width), bf),
            pltpu.VMEM((blocks // 2, 2 * tokens, per_device * 2 * capacity), bf),
            pltpu.VMEM((per_device, rows, width), bf),
            pltpu.VMEM((per_device, rows, width), bf),
            pltpu.VMEM((per_device, rows, width), bf),
            pltpu.VMEM((per_device, rows, width), bf),
            pltpu.VMEM((per_device, rows, ff), bf),
            pltpu.VMEM((per_device, rows, ff), bf),
            pltpu.VMEM((per_device, rows, ff), bf),
            pltpu.VMEM((rows, ff), f32),
            pltpu.VMEM((rows, ff), f32),
            pltpu.VMEM((blocks, table_rows, tokens), bf),
            pltpu.VMEM((per_device, blocks // 2, 1, 2 * tokens), f32),
            pltpu.VMEM((experts, 2 * tokens), f32),
            pltpu.VMEM((experts, 2 * tokens), f32),
            pltpu.VMEM((per_device, rows, 128), f32),
            pltpu.VMEM((per_device, rows, 128), f32),
            pltpu.VMEM((2, 2, tokens + table_rows, width), bf),
            pltpu.VMEM((2, 2, tokens, width), bf),
            sem((3 * per_device, 4)),
            sem((2, 2, 2)),
            sem((2,)),
            sem,
            sem((5, per_device)),
            sem((2,)),
            sem((2,)),
        ],
        cost_estimate=pl.CostEstimate(flops=55000000000, transcendentals=0, bytes_accessed=50000000),
        compiler_params=pltpu.CompilerParams(vmem_limit_bytes=61 * MIB),
    )(scalars, router_t, codes, grads_all, res, *inputs)


def weight_kernel(x_ref, dga_ref, dua_ref, hid_ref, dy_ref, out_ref):
    dtype = jnp.bfloat16
    out_ref[0, 0, 0] = dot_tn(x_ref[0], dga_ref[0]).astype(dtype)
    out_ref[0, 1, 0] = dot_tn(x_ref[0], dua_ref[0]).astype(dtype)
    ff = hid_ref.shape[2]
    step = dy_ref.shape[2]
    for i in range(ff // step):
        part = dot_tn(hid_ref[0, :, i * step : (i + 1) * step], dy_ref[0])
        out_ref[0, 2, 0, :, i * step : (i + 1) * step] = part.astype(dtype)


def expert_weight_grads(x, dga, dua, hid, dy, parts):
    per_device, rows, ff = dga.shape
    step = x.shape[2] // parts
    whole = pl.BlockSpec((1, rows, ff), lambda e, d: (e, 0, 0))
    piece = pl.BlockSpec((1, rows, step), lambda e, d: (e, 0, d))
    return pl.pallas_call(
        weight_kernel,
        grid=(per_device, parts),
        out_shape=jax.ShapeDtypeStruct((parts, 3, per_device, step, ff), jnp.bfloat16),
        in_specs=[piece, whole, whole, whole, piece],
        out_specs=pl.BlockSpec((1, 3, 1, step, ff), lambda e, d: (d, 0, e, 0, 0)),
        cost_estimate=pl.CostEstimate(
            flops=18700000000, transcendentals=0, bytes_accessed=17000000
        ),
        compiler_params=pltpu.CompilerParams(vmem_limit_bytes=56 * MIB),
    )(x, dga, dua, hid, dy)


def down_kernel(hid_ref, dy_ref, out_ref):
    out_ref[0] = dot_tn(hid_ref[0], dy_ref[0]).astype(jnp.bfloat16)


def gate_up_kernel(x_ref, dga_ref, dua_ref, out_ref):
    out_ref[0, 0] = dot_tn(x_ref[0], dga_ref[0]).astype(jnp.bfloat16)
    out_ref[1, 0] = dot_tn(x_ref[0], dua_ref[0]).astype(jnp.bfloat16)


def whole_weight_grads(x, dga, dua, hid, dy):
    per_device, rows, ff = dga.shape
    width = x.shape[2]
    thin = pl.BlockSpec((1, rows, ff), lambda e: (e, 0, 0))
    wide = pl.BlockSpec((1, rows, width), lambda e: (e, 0, 0))
    down = pl.pallas_call(
        down_kernel,
        grid=(per_device,),
        out_shape=jax.ShapeDtypeStruct((per_device, ff, width), jnp.bfloat16),
        in_specs=[thin, wide],
        out_specs=pl.BlockSpec((1, ff, width), lambda e: (e, 0, 0)),
        compiler_params=pltpu.CompilerParams(vmem_limit_bytes=40 * MIB),
    )(hid, dy)
    gate_up = pl.pallas_call(
        gate_up_kernel,
        grid=(per_device,),
        out_shape=jax.ShapeDtypeStruct((2, per_device, width, ff), jnp.bfloat16),
        in_specs=[wide, thin, thin],
        out_specs=pl.BlockSpec((2, 1, width, ff), lambda e: (0, e, 0, 0)),
        compiler_params=pltpu.CompilerParams(vmem_limit_bytes=40 * MIB),
    )(x, dga, dua)
    return gate_up, down


def gather_inputs(value, weights, count, tuned):
    rows = value.shape[0]
    if not tuned:
        full = lax.all_gather(value, "expert", axis=0, tiled=False)
        places = [[[(t, (e,), None)] for e in range(count)] for t in range(3)]
        return list(weights) + [full], places, [[(3, b, 0, rows)] for b in range(full.shape[0])]
    both, both_x, both_y, down, down_x, down_y, down_a, down_b = weights
    below = shift_up(value)
    above = shift_down(value)
    below, above, both_x, both_y = lax.optimization_barrier((below, above, both_x, both_y))
    tokens = [value, below, above, shift_up(below)]
    tokens = tokens + [swap_core(v) for v in tokens]
    arrays = [both, both_x, both_y, swap_x(both_y[0]), swap_y(both_x[1])]
    arrays = arrays + [down, down_x, down_y, down_a, down_b]
    places = [
        [[(k, (t, e), k) for k in range(3)] + [(3 + t, (e,), 3)] for e in range(count)]
        for t in range(2)
    ]
    places.append(
        [[(5 + k, (e,), k) for k in range(3)] + [(8 + e, (0,), 3)] for e in range(count)]
    )
    token_places = []
    for base in (10, 14):
        token_places += [[(base + k, None, 0, rows)] for k in range(4)]
    return arrays + tokens, places, token_places


def rotate(values, cos_wide, sin_wide):
    return values * cos_wide + pltpu.roll(values, HEAD_SIZE // 2, 1) * sin_wide


def tile_cols(j, size):
    return pl.ds(pl.multiple_of(j * size, size), size)


def forward_kernel(plan, *refs):
    order_ref, x_ref, cos_ref, sin_ref, lab_col_ref, lab_row_ref = refs[:6]
    count = plan["inputs"]
    inputs = refs[6 : 6 + count]
    (
        h2_ref,
        res_ref,
        h1_ref,
        q_ref,
        k_ref,
        v_ref,
        p_ref,
        o_ref,
        aux_ref,
        w_full_out,
        w_full,
        sem_in,
        sem_save,
    ) = refs[6 + count :]
    width = x_ref.shape[1]
    tokens = x_ref.shape[0]
    bf = jnp.bfloat16
    heads = QUERY_HEADS // KEY_VALUE_HEADS
    kv_width = KEY_VALUE_HEADS * HEAD_SIZE
    main = width + 2 * kv_width
    base = main + 128
    for ref_index, lead, order_index in plan["places"]:
        src = inputs[ref_index]
        for at in lead:
            src = src.at[at]
        rows = src.shape[0]
        if order_index is None:
            dst = w_full
        else:
            start = pl.multiple_of(order_ref[order_index] * rows, rows)
            dst = w_full.at[pl.ds(start, rows), :]
        pltpu.make_async_copy(src, dst, sem_in).start()
    x = x_ref[...].astype(jnp.float32)
    inverse = lax.rsqrt(jnp.mean(x * x, axis=1, keepdims=True) + EPSILON)
    pltpu.make_async_copy(w_full, w_full, sem_in).wait()
    save = pltpu.make_async_copy(w_full, w_full_out, sem_save)
    save.start()
    side = w_full[:, main : main + 128].astype(jnp.float32).T
    gain = side[:1]
    h1_ref[...] = (x * inverse * gain).astype(bf)
    cos_wide, sin_wide = cos_ref[...], sin_ref[...]

    @pl.loop(0, width // 768)
    def _(j):
        raw = dot_nn(h1_ref[...], w_full[:, tile_cols(j, 768)])
        both = [
            rotate(raw[:, half * HEAD_SIZE : (half + 1) * HEAD_SIZE], cos_wide, sin_wide)
            for half in range(768 // HEAD_SIZE)
        ]
        q_ref[:, tile_cols(j, 768)] = jnp.concatenate(both, axis=1).astype(bf)

    raw = dot_nn(h1_ref[...], w_full[:, width:main])
    both = [
        rotate(raw[:, half * HEAD_SIZE : (half + 1) * HEAD_SIZE], cos_wide, sin_wide)
        for half in range(KEY_VALUE_HEADS)
    ]
    k_ref[...] = jnp.concatenate(both, axis=1).astype(bf)
    v_ref[...] = raw[:, kv_width:].astype(bf)
    seq_len = tokens // SEQ_DEV
    query_step = lax.broadcasted_iota(jnp.int32, (seq_len, seq_len), 0)
    key_step = lax.broadcasted_iota(jnp.int32, (seq_len, seq_len), 1)
    for s in range(SEQ_DEV):
        rows = slice(s * seq_len, (s + 1) * seq_len)
        same = lab_col_ref[rows, :] == lab_row_ref[:, rows]
        allowed = jnp.logical_and(same, query_step >= key_step)[None]
        for h in range(KEY_VALUE_HEADS):
            cols = slice(h * HEAD_SIZE, (h + 1) * HEAD_SIZE)
            stack = jnp.concatenate(
                [
                    q_ref[rows, (h * heads + g) * HEAD_SIZE : (h * heads + g + 1) * HEAD_SIZE]
                    for g in range(heads)
                ],
                axis=0,
            )
            scores = dot_nt(stack, k_ref[rows, cols]) * HEAD_SIZE ** (-0.5)
            scores = scores.reshape(heads, seq_len, seq_len)
            scores = jnp.where(allowed, scores, NEG_FILL)
            top = jnp.max(scores, axis=2, keepdims=True)
            raised = jnp.exp(scores - top)
            probs = raised / jnp.sum(raised, axis=2, keepdims=True)
            probs = probs.reshape(heads * seq_len, seq_len)
            p_ref[s, h] = probs
            mixed = dot_nn(probs.astype(bf), v_ref[rows, cols]).astype(bf)
            for g in range(heads):
                o_ref[rows, (h * heads + g) * HEAD_SIZE : (h * heads + g + 1) * HEAD_SIZE] = mixed[
                    g * seq_len : (g + 1) * seq_len
                ]
    side_out = w_full[:, base + width : base + width + 128].astype(jnp.float32).T
    aux_ref[...] = jnp.concatenate([side_out, side[:8]], axis=0)

    @pl.loop(0, width // 768)
    def _(j):
        cols = tile_cols(j, 768)
        at = pl.ds(pl.multiple_of(base + j * 768, 128), 768)
        res_ref[:, cols] = x_ref[:, cols].astype(jnp.float32) + dot_nn(o_ref[...], w_full[:, at])

    res = res_ref[...]
    inverse = lax.rsqrt(jnp.mean(res * res, axis=1, keepdims=True) + EPSILON)
    moe_row = plan["experts"]
    h2_ref[...] = (res * inverse * side_out[moe_row : moe_row + 1]).astype(bf)
    save.wait()


def run_forward(plan, order, x, cos_wide, sin_wide, lab_col, lab_row, inputs, w_cols):
    tokens, width = x.shape
    bf, f32 = jnp.bfloat16, jnp.float32
    kv_width = KEY_VALUE_HEADS * HEAD_SIZE
    seq_len = tokens // SEQ_DEV
    stack = QUERY_HEADS // KEY_VALUE_HEADS * seq_len
    vmem = pl.BlockSpec(memory_space=pltpu.VMEM)
    shape = jax.ShapeDtypeStruct
    sem = pltpu.SemaphoreType.DMA
    return pl.pallas_call(
        lambda *refs: forward_kernel(plan, *refs),
        out_shape=(
            shape((tokens, width), bf),
            shape((tokens, width), f32),
            shape((tokens, width), bf),
            shape((tokens, width), bf),
            shape((tokens, kv_width), bf),
            shape((tokens, kv_width), bf),
            shape((SEQ_DEV, KEY_VALUE_HEADS, stack, seq_len), f32),
            shape((tokens, width), bf),
            shape((136, width), f32),
            shape((width, w_cols), bf),
        ),
        in_specs=[smem_spec()] + [vmem] * 5 + [any_spec()] * len(inputs),
        out_specs=tuple([vmem] * 9 + [any_spec()]),
        scratch_shapes=[
            pltpu.VMEM((width, w_cols), bf),
            sem,
            sem,
        ],
        cost_estimate=pl.CostEstimate(flops=110000000000, transcendentals=0, bytes_accessed=16000000),
        compiler_params=pltpu.CompilerParams(vmem_limit_bytes=56 * MIB),
    )(order, x, cos_wide, sin_wide, lab_col, lab_row, *inputs)


def send_payload(order_ref, payload, start_col, outs, sem):
    cols = pl.ds(start_col, outs[0].shape[-1])
    if len(outs) == 1:
        pltpu.make_async_copy(payload.at[:, cols], outs[0], sem).start()
        return
    rows = payload.shape[0] // 32
    for c in range(2):
        x_one, y_one, x_two, y_two, own = outs[c * 5 : c * 5 + 5]
        places = [own.at[r] for r in range(4)]
        places += [x_one.at[1, 0], x_one.at[1, 1], x_two.at[0], x_two.at[1]]
        places += [y_two.at[0], y_two.at[1], y_one.at[1, 0], y_one.at[1, 1]]
        places += [x_one.at[0, 0], x_one.at[0, 1], y_one.at[0, 0], y_one.at[0, 1]]
        for j, dst in enumerate(places):
            start = pl.multiple_of(order_ref[c * 16 + j] * rows, rows)
            pltpu.make_async_copy(payload.at[pl.ds(start, rows), cols], dst, sem).start()


def payload_shapes(tuned, rows, cols):
    if not tuned:
        return (jax.ShapeDtypeStruct((rows, cols), jnp.bfloat16),)
    piece = rows // 32
    shapes = [(2, 2), (2, 2), (2,), (2,), (4,)]
    one = tuple(jax.ShapeDtypeStruct(v + (piece, cols), jnp.bfloat16) for v in shapes)
    return one + one


def backward_kernel(experts, sums, piece, order_ref, own_ref, *refs):
    given = 8 if piece else 2
    early, refs = refs[:given], refs[given:]
    back_refs = refs[:sums]
    res_ref, h2_ref, o_ref, aux_ref, x_ref, cos_ref, sin_ref = refs[sums : sums + 7]
    h1_ref, q_ref, k_ref, v_ref, p_ref, w_full_ref = refs[sums + 7 : sums + 13]
    rest = refs[sums + 13 :]
    outs = rest[:-13]
    dx_ref, w_full, dy, codes, payload, dres_ref, dres_low, dmix_ref, dqkv, dh1 = rest[-13:-3]
    sem_w, sem_d, sem_p = rest[-3:]
    tokens, width = res_ref.shape
    bf = jnp.bfloat16
    heads = QUERY_HEADS // KEY_VALUE_HEADS
    kv_width = KEY_VALUE_HEADS * HEAD_SIZE
    main = width + 2 * kv_width
    base = main + 128
    scale = HEAD_SIZE ** (-0.5)
    load = pltpu.make_async_copy(w_full_ref, w_full, sem_w.at[0])
    load.start()
    if piece:
        src = early[0].at[pl.ds(tokens, codes.shape[0]), pl.ds(0, tokens)]
        loads = deal_copies(own_ref, early, piece, 0, dy, 0, sem_d)
    else:
        src = early[1].at[own_ref[0]]
        loads = [pltpu.make_async_copy(early[0].at[own_ref[0]], dy, sem_d)]
    load_codes = pltpu.make_async_copy(src, codes, sem_w.at[1])
    load_codes.start()
    for copy in loads:
        copy.start()
    back = back_refs[0][...]
    for ref in back_refs[1:]:
        back = back + ref[...].astype(jnp.float32)
    grad_pair = (
        back[tokens : tokens + experts, :tokens]
        + back[tokens : tokens + experts, tokens : 2 * tokens]
    )
    back = back[:tokens]
    router_t = aux_ref[:experts, :].astype(bf)
    gain = aux_ref[experts : experts + 1, :]
    logits = dot_nt(router_t, h2_ref[...])
    load_codes.wait()
    chosen = codes[...].astype(jnp.float32)[:experts] > 0.0
    top = jnp.max(jnp.where(chosen, logits, NEG_FILL), axis=0, keepdims=True)
    raised = jnp.where(chosen, jnp.exp(logits - top), 0.0)
    gates = raised / jnp.sum(raised, axis=0, keepdims=True)
    inner = jnp.sum(gates * grad_pair, axis=0, keepdims=True)
    dlog = jnp.where(chosen, gates * (grad_pair - inner), 0.0).astype(bf)
    grad_router = dot_nn(dlog, h2_ref[...])
    dh2 = back + dot_tn(dlog, router_t)
    res = res_ref[...]
    inverse = lax.rsqrt(jnp.mean(res * res, axis=1, keepdims=True) + EPSILON)
    scaled = dh2 * gain
    grad_gain = jnp.sum(dh2 * res * inverse, axis=0, keepdims=True)
    pltpu.make_async_copy(dy, dy, sem_d).wait()
    dres = (
        dy[...].astype(jnp.float32)
        + inverse * scaled
        - res * inverse**3 * jnp.mean(scaled * res, axis=1, keepdims=True)
    )
    dres_ref[...] = dres
    dres_low[...] = dres.astype(bf)
    pad = jnp.zeros((128 - experts - 8, width), jnp.float32)
    side = jnp.concatenate(
        [grad_router, jnp.broadcast_to(grad_gain, (8, width)), pad], axis=0
    )
    payload[:, base + width : base + width + 128] = side.T.astype(bf)

    @pl.loop(0, width // 768)
    def _(j):
        cols = tile_cols(j, 768)
        at = pl.ds(pl.multiple_of(base + j * 768, 128), 768)
        payload[:, at] = dot_tn(o_ref[...], dres_low[:, cols]).astype(bf)

    send_payload(order_ref, payload, base, outs[len(outs) // 2 :], sem_p)
    load.wait()

    @pl.loop(0, width // 768)
    def _(j):
        cols = tile_cols(j, 768)
        dmix_ref[:, cols] = dot_nt(dres_low[...], w_full[cols, base : base + width]).astype(bf)

    seq_len = tokens // SEQ_DEV
    for s in range(SEQ_DEV):
        rows = slice(s * seq_len, (s + 1) * seq_len)
        cos_wide, sin_wide = cos_ref[rows, :], -sin_ref[rows, :]
        cos_tall = jnp.concatenate([cos_wide] * heads, axis=0)
        sin_tall = jnp.concatenate([sin_wide] * heads, axis=0)
        for h in range(KEY_VALUE_HEADS):
            cols = slice(h * HEAD_SIZE, (h + 1) * HEAD_SIZE)
            places = [
                slice((h * heads + g) * HEAD_SIZE, (h * heads + g + 1) * HEAD_SIZE)
                for g in range(heads)
            ]
            q_tall = jnp.concatenate([q_ref[rows, place] for place in places], axis=0)
            dmix = jnp.concatenate([dmix_ref[rows, place] for place in places], axis=0)
            probs = p_ref[s, h]
            dprobs = dot_nt(dmix, v_ref[rows, cols])
            dv = dot_tn(probs.astype(bf), dmix)
            inner = jnp.sum(probs * dprobs, axis=1, keepdims=True)
            dscores = (probs * (dprobs - inner)).astype(bf)
            dq = rotate(dot_nn(dscores, k_ref[rows, cols]) * scale, cos_tall, sin_tall)
            dk = rotate(dot_tn(dscores, q_tall) * scale, cos_wide, sin_wide)
            for g, place in enumerate(places):
                dqkv[rows, place] = dq[g * seq_len : (g + 1) * seq_len].astype(bf)
            dqkv[rows, width + h * HEAD_SIZE : width + (h + 1) * HEAD_SIZE] = dk.astype(bf)
            at = width + kv_width + h * HEAD_SIZE
            dqkv[rows, at : at + HEAD_SIZE] = dv.astype(bf)
    @pl.loop(0, width // 768)
    def _(j):
        cols = tile_cols(j, 768)
        dh1[:, cols] = dot_nt(dqkv[...], w_full[cols, :main])

    @pl.loop(0, main // 1024)
    def _(j):
        cols = tile_cols(j, 1024)
        payload[:, cols] = dot_tn(h1_ref[...], dqkv[:, cols]).astype(bf)

    x = x_ref[...].astype(jnp.float32)
    gain = aux_ref[128:129, :]
    inverse = lax.rsqrt(jnp.mean(x * x, axis=1, keepdims=True) + EPSILON)
    grad = dh1[...]
    scaled = grad * gain
    grad_gain = jnp.sum(grad * x * inverse, axis=0, keepdims=True)
    payload[:, main : main + 128] = jnp.broadcast_to(grad_gain, (128, width)).T.astype(bf)
    dx = (
        dres_ref[...]
        + inverse * scaled
        - x * inverse**3 * jnp.mean(scaled * x, axis=1, keepdims=True)
    )
    send_payload(order_ref, payload, 0, outs[: len(outs) // 2], sem_p)
    dx_ref[...] = dx.astype(bf)
    pltpu.make_async_copy(payload, payload, sem_p).wait()


def run_backward(tuned, experts, piece, order, own, early, rows, backs, saved, w_full):
    tokens, width = saved[0].shape
    bf, f32 = jnp.bfloat16, jnp.float32
    vmem = pl.BlockSpec(memory_space=pltpu.VMEM)
    shape = jax.ShapeDtypeStruct
    sem = pltpu.SemaphoreType.DMA
    main = width + 2 * KEY_VALUE_HEADS * HEAD_SIZE
    payload = payload_shapes(tuned, width, main + 128)
    payload = payload + payload_shapes(tuned, width, width + 128)
    return pl.pallas_call(
        lambda *refs: backward_kernel(experts, len(backs), piece, *refs),
        out_shape=payload + (shape((tokens, width), bf),),
        in_specs=[smem_spec()] * 2
        + [any_spec()] * len(early)
        + [vmem] * (len(backs) + len(saved))
        + [any_spec()],
        out_specs=tuple([any_spec()] * len(payload) + [vmem]),
        scratch_shapes=[
            pltpu.VMEM(w_full.shape, bf),
            pltpu.VMEM((tokens, width), bf),
            pltpu.VMEM((rows, tokens), bf),
            pltpu.VMEM(w_full.shape, bf),
            pltpu.VMEM((tokens, width), f32),
            pltpu.VMEM((tokens, width), bf),
            pltpu.VMEM((tokens, width), bf),
            pltpu.VMEM((tokens, main), bf),
            pltpu.VMEM((tokens, width), f32),
            sem((2,)),
            sem,
            sem,
        ],
        cost_estimate=pl.CostEstimate(
            flops=165000000000, transcendentals=0, bytes_accessed=32000000
        ),
        compiler_params=pltpu.CompilerParams(vmem_limit_bytes=60 * MIB),
    )(order, own, *early, *backs, *saved, w_full)


def after(value, *others):
    return lax.optimization_barrier((value,) + others)[0]


def swap_diagonal(value):
    return lax.ppermute(value, "dp", [(i, i ^ 3) for i in range(4)])


def shift_two(value):
    return lax.ppermute(value, "expert", [(i, (i + 4) % 8) for i in range(8)])


def gather_front(pack, early, sent, w_gate, w_up, w_down, tuned):
    if not tuned:
        got = lax.all_to_all(sent, "expert", split_axis=0, concat_axis=2, tiled=True)
        full = lax.all_gather(pack, ("dp", "expert"), axis=0, tiled=True)
        dealt = [lax.all_gather(early, "expert", axis=0, tiled=False)]
        weights = [
            lax.all_gather(w_gate, "dp", axis=1, tiled=True),
            lax.all_gather(w_up, "dp", axis=1, tiled=True),
            lax.all_gather(w_down, "dp", axis=2, tiled=True),
        ]
        return got, [full], [(0, (), None)], dealt, weights
    both = jnp.stack([w_gate, w_up])
    ring = (pack, shift_up(pack), shift_down(pack), shift_two(pack))
    down_x = swap_x(w_down)
    down_y = swap_y(w_down)
    down = [w_down, down_x, down_y, swap_x(down_y[:1]), swap_y(down_x[1:])]
    *ring, _, _, both = lax.optimization_barrier(ring + tuple(down[1:3]) + (both,))
    level = after(jnp.stack(ring), *down)
    from_x = swap_x(level)
    from_y = swap_y(level)
    sent = after(sent, level)
    got = lax.all_to_all(sent, "expert", split_axis=0, concat_axis=2, tiled=True)
    early = after(early, level)
    below = shift_up(early)
    above = shift_down(early)
    far_a = swap_x(from_y[:2])
    far_b = swap_y(from_x[2:])
    both = after(both, far_a, far_b)
    both_x = swap_x(both)
    both_y = swap_y(both)
    dealt = [early, below, above, shift_up(below)]
    dealt = dealt + [swap_core(v) for v in dealt]
    arrays = [level, from_x, from_y, far_a, far_b]
    late = lax.optimization_barrier((far_a, far_b, below, above))[:2]
    arrays = arrays + [swap_core(v) for v in arrays[:3]] + [swap_core(v) for v in late]
    places = []
    for c in range(2):
        for k in range(4):
            for r in range(4):
                ref, lead = (k, r) if k < 3 else ((3, r) if r < 2 else (4, r - 2))
                places.append((c * 5 + ref, (lead,), (c * 4 + k) * 4 + r))
    return got, arrays, places, dealt, (both, both_x, both_y) + tuple(down)


def scatter_core(outs):
    got = [swap_core(v) for v in outs[5:]]
    return [add_low(outs[k], got[k]) for k in range(4)] + [outs[4], got[4]]


def scatter_planes(sums, first):
    x_one, y_one, x_two, y_two, own, got_own = sums
    x_two = swap_x(add_low(x_two, first[1][0]))
    y_two = swap_y(add_low(y_two, first[0][0]))
    level = []
    for r in range(4):
        near = (first[0][1, r], y_two[r]) if r < 2 else (x_two[r - 2], first[1][1, r - 2])
        total = own[r].astype(jnp.float32) + got_own[r].astype(jnp.float32)
        total = total + near[0].astype(jnp.float32) + near[1].astype(jnp.float32)
        level.append(total if r == 0 else total.astype(jnp.bfloat16))
    return level


def scatter_ring(level, others, short):
    below, above, far = level[1:]
    if short:
        got = [shift_down(below), shift_up(add_low(above, shift_up(far)))]
    else:
        got = [shift_down(below), shift_up(above), shift_two(far)]
    last, *others = lax.optimization_barrier((level[0],) + tuple(others))
    for v in got:
        last = last + v.astype(jnp.float32)
    return last, others


def scatter_payload(outs, tuned, others, more, grad_x):
    half = len(outs) // 2
    if not tuned:
        owned = [
            lax.psum_scatter(v, ("dp", "expert"), scatter_dimension=0, tiled=True) for v in outs
        ]
        return [v.astype(jnp.float32) for v in owned], others, more, grad_x
    first = scatter_core(outs[:half])
    second = scatter_core(outs[half:])
    first_got = [swap_x(first[0]), swap_y(first[1])]
    tied = lax.optimization_barrier(tuple(first_got) + (first[2], first[3], grad_x) + tuple(more[1:]))
    first_got, first[2:4], grad_x, more[1:] = list(tied[:2]), tied[2:4], tied[4], tied[5:]
    first_level = scatter_planes(first, first_got)
    sent = lax.optimization_barrier((second[0], second[1]) + tuple(first_got))
    second_got = [swap_x(sent[0]), swap_y(sent[1])]
    second_level = scatter_planes(second, second_got)
    more = lax.optimization_barrier(tuple(more) + (first_level[1],))[:-1]
    owned_in, _ = scatter_ring(first_level, second_level[1:2], True)
    owned_out, others = scatter_ring(second_level, others, False)
    return [owned_in, owned_out], others, more, grad_x


def sum_whole(keep, send):
    blocks = jnp.concatenate([keep, send], axis=0)
    sums = lax.psum_scatter(blocks, "expert", scatter_dimension=0, tiled=False)
    return [sums.astype(jnp.float32)]


def sum_messages(keep, got):
    sums = [keep[i].astype(jnp.float32) + got[i].astype(jnp.float32) for i in range(4)]
    return [sums[0]] + [v.astype(jnp.bfloat16) for v in sums[1:]]


def sum_ring(messages, between):
    own, to_below, to_above, far = messages
    got_far = shift_up(far)
    from_above = shift_down(to_below)
    if between is not None:
        to_above = after(to_above, between)
    onward = add_low(to_above, got_far)
    return [own, from_above, shift_up(onward)], onward


def deal_back(value, placement):
    tokens, width = value.shape
    value = value.reshape(1, SEQ_DEV, tokens // SEQ_DEV, width)
    value = lax.all_to_all(value, "expert", split_axis=2, concat_axis=0, tiled=True)
    return value.reshape(placement.shape[0], -1, width)[placement]


def pad_columns(value, width):
    return jnp.pad(value, ((0, 0), (0, width - value.shape[1])))


def body(
    tokens,
    cotangent,
    lengths,
    placement,
    routes,
    priority,
    g_attn,
    w_query,
    key_projection,
    value_projection,
    w_out,
    g_moe,
    w_router,
    w_gate,
    w_up,
    w_down,
):
    row_seqs, piece_len, width = tokens.shape
    expert_devices = lax.axis_size("expert")
    plane_size = lax.axis_size("dp")
    tuned = expert_devices == 8 and plane_size == 4
    my_index = lax.axis_index("expert")
    seq_len = piece_len * expert_devices
    token_count = SEQ_DEV * seq_len
    query_width = w_query.shape[1]
    kv_width = key_projection.shape[1]
    expert_count = w_router.shape[1]
    per_device = expert_count // expert_devices
    capacity = (9 * token_count * TOPK + 64 * expert_count - 1) // (64 * expert_count) * 8
    code_list = jnp.arange(row_seqs, dtype=jnp.int32)
    source = jnp.sum(
        jnp.where(placement[:, None] == code_list[None, :], code_list[:, None], 0), axis=0
    )
    pack = jnp.concatenate(
        [
            w_query,
            key_projection,
            value_projection,
            pad_columns(g_attn[:, None], 128),
            w_out,
            pad_columns(jnp.concatenate([w_router, g_moe[:, None]], axis=1), 128),
        ],
        axis=1,
    )
    sent = tokens[source].reshape(expert_devices, SEQ_DEV, piece_len, width)
    ranks = slot_ranks(routes.reshape(-1), priority.reshape(-1)).reshape(token_count, TOPK)
    codes = jnp.minimum(ranks, capacity) + 1
    expert_list = jnp.arange(expert_count, dtype=jnp.int32)
    picks = routes[None, :, :] == expert_list[:, None, None]
    code_table = jnp.sum(jnp.where(picks, codes[None], 0), axis=2)
    table_rows = -(-expert_count // 16) * 16
    table = jnp.zeros((table_rows, width), jnp.bfloat16)
    table = table.at[:expert_count, :token_count].set(code_table.astype(jnp.bfloat16))
    early = jnp.concatenate([cotangent.reshape(token_count, width), table], axis=0)
    got_tokens, pack_parts, pack_places, early_parts, weights = gather_front(
        pack, early, sent, w_gate, w_up, w_down, tuned
    )
    x_local = got_tokens.reshape(token_count, width)
    order = expert_order(tuned, expert_devices)
    seqs = source.reshape(expert_devices, SEQ_DEV)[order].reshape(-1)
    rel_of = jnp.sum(
        jnp.where(
            order[None, :] == jnp.arange(expert_devices)[:, None],
            jnp.arange(expert_devices)[None, :],
            0,
        ),
        axis=1,
    )
    plane = lax.axis_index("dp").reshape(1)
    scalars = jnp.concatenate([my_index.reshape(1), seqs, order, rel_of, plane])
    scalars = scalars.astype(jnp.int32)
    grads_all = jnp.zeros((16, 128), jnp.bfloat16)
    codes_all = grads_all
    if not tuned:
        early_all = early_parts[0]
        pieces = early_all[:, :token_count].reshape(expert_devices, row_seqs, piece_len, width)
        pieces = pieces[:, seqs].reshape(
            expert_devices, expert_devices, SEQ_DEV, piece_len, width
        )
        grads_all = pieces.transpose(1, 2, 0, 3, 4).reshape(expert_devices, token_count, width)
        codes_all = early_all[:, token_count:, :token_count]
        early_parts = []
    own_seqs = lax.dynamic_slice_in_dim(source, my_index * SEQ_DEV, SEQ_DEV)
    positions, labels = device_layout(lengths[own_seqs], seq_len)
    cosine_table, sine_values = rope_tables(positions, HEAD_SIZE)
    cos_wide = jnp.concatenate([cosine_table, cosine_table], axis=1)
    sin_wide = jnp.concatenate([-sine_values, sine_values], axis=1)
    plan = {
        "inputs": len(pack_parts),
        "experts": expert_count,
        "places": pack_places,
    }
    row_order = all_order()
    normed_moe, residual, h1, q, k, v, probs, mixed, aux, w_full = run_forward(
        plan,
        row_order,
        x_local,
        cos_wide,
        sin_wide,
        labels[:, None],
        labels[None, :],
        pack_parts,
        pack.shape[1],
    )
    inputs, weight_places, token_places = gather_inputs(normed_moe, weights, per_device, tuned)
    inputs = inputs + early_parts
    plan = {
        "inputs": len(inputs),
        "blocks": expert_devices,
        "per_device": per_device,
        "ff": w_gate.shape[2],
        "weights": weight_places,
        "tokens": token_places,
        "token_count": token_count,
        "piece": piece_len,
        "early": list(range(len(inputs) - len(early_parts), len(inputs))),
    }
    router_t = aux[:expert_count].astype(jnp.bfloat16)
    back_keep, back_send, out_keep, out_send, x_slots, dy_slots, hid, dga, dua = run_experts(
        plan, capacity, table_rows, scalars, router_t, codes_all, grads_all, residual, inputs
    )
    if tuned:
        back_got = swap_core(back_send)
        out_got = swap_core(after(out_send, back_got))
        messages = sum_messages(back_keep, back_got)
        x_slots = after(x_slots, *messages)
    if width // plane_size * 2 == w_gate.shape[2] and width % (128 * plane_size) == 0:
        weight_grads = expert_weight_grads(x_slots, dga, dua, hid, dy_slots, plane_size)
        flat = weight_grads.reshape(-1, weight_grads.shape[-1])
        owned = lax.psum_scatter(flat, "dp", scatter_dimension=0, tiled=True)
        owned = owned.reshape(weight_grads.shape[1:])
        half = owned.shape[-1] // 2
        owned_gate, owned_up = owned[0].astype(jnp.float32), owned[1].astype(jnp.float32)
        owned_down = jnp.concatenate([owned[2, :, :, :half], owned[2, :, :, half:]], axis=1)
    else:
        gate_up, down = whole_weight_grads(x_slots, dga, dua, hid, dy_slots)
        owned = lax.psum_scatter(gate_up, "dp", scatter_dimension=2, tiled=True)
        owned_gate, owned_up = owned[0].astype(jnp.float32), owned[1].astype(jnp.float32)
        owned_down = lax.psum_scatter(down, "dp", scatter_dimension=2, tiled=True)
    owned_down = owned_down.astype(jnp.float32)
    if tuned:
        backs, _ = sum_ring(messages, weight_grads)
        messages = sum_messages(after(out_keep, backs[1]), out_got)
        backs[0] = after(backs[0], *messages)
        messages[1:] = lax.optimization_barrier(tuple(messages[1:]) + tuple(backs[1:]))[:3]
    else:
        backs = sum_whole(back_keep, back_send)
        sums = sum_whole(out_keep, out_send)
    final = run_backward(
        tuned,
        expert_count,
        piece_len if tuned else 0,
        row_order,
        scalars,
        early_parts if tuned else [grads_all, codes_all],
        table_rows,
        backs,
        [
            residual,
            normed_moe,
            mixed,
            aux,
            x_local,
            cos_wide,
            sin_wide,
            h1,
            q,
            k,
            v,
            probs,
        ],
        w_full,
    )
    payload, grad_x = final[:-1], final[-1]
    if tuned:
        sums, onward = sum_ring(messages, grad_x)
        *payload, _ = lax.optimization_barrier(tuple(payload) + (onward,))
    others = (owned_gate, owned_up, owned_down)
    (owned_in, owned_out), others, more, grad_x = scatter_payload(
        payload, tuned, others, sums, grad_x
    )
    owned_gate, owned_up, owned_down = others
    if tuned:
        sums = list(more)
    if tuned:
        total = sums[0] + sums[1].astype(jnp.float32) + sums[2].astype(jnp.float32)
        output = total.astype(jnp.bfloat16).reshape(row_seqs, piece_len, width)
    else:
        output = deal_back((residual + sums[0]).astype(jnp.bfloat16), placement)
    input_grad = deal_back(grad_x, placement)
    return (
        output,
        input_grad,
        owned_in[:, query_width + 2 * kv_width],
        owned_in[:, :query_width],
        owned_in[:, query_width : query_width + kv_width],
        owned_in[:, query_width + kv_width : query_width + 2 * kv_width],
        owned_out[:, :width],
        owned_out[:, width + expert_count],
        owned_out[:, width : width + expert_count],
        owned_gate,
        owned_up,
        owned_down,
    )


def solution(mesh):
    return jax.shard_map(
        body,
        mesh=mesh,
        in_specs=(
            P("dp", "expert", None),
            P("dp", "expert", None),
            P("dp", None),
            P("dp"),
            P(("dp", "expert"), None),
            P(("dp", "expert"), None),
            P(("dp", "expert")),
            P(("dp", "expert"), None),
            P(("dp", "expert"), None),
            P(("dp", "expert"), None),
            P(("dp", "expert"), None),
            P(("dp", "expert")),
            P(("dp", "expert"), None),
            P("expert", "dp", None),
            P("expert", "dp", None),
            P("expert", None, "dp"),
        ),
        out_specs=(
            P("dp", "expert", None),
            P("dp", "expert", None),
            P(("dp", "expert")),
            P(("dp", "expert"), None),
            P(("dp", "expert"), None),
            P(("dp", "expert"), None),
            P(("dp", "expert"), None),
            P(("dp", "expert")),
            P(("dp", "expert"), None),
            P("expert", "dp", None),
            P("expert", "dp", None),
            P("expert", None, "dp"),
        ),
        check_vma=False,
    )
```

```python
import math

import jax
import jax.numpy as jnp
from jax import lax
from jax.experimental import pallas as pl
from jax.experimental.pallas import tpu as pltpu
from jax.sharding import PartitionSpec as P

QUERY_HEADS = 12
KEY_VALUE_HEADS = 2
HEAD_SIZE = 128
TOPK = 4
SEQ_DEV = 2


EPSILON = 1e-06
ROPE_BASE = 1000000.0
NEG_FILL = -1e30


def sequence_layout(doc_lens, seq_len):
    token_steps = jnp.arange(seq_len, dtype=jnp.int32)
    doc_ends = jnp.cumsum(doc_lens)
    doc_index = jnp.sum((token_steps[:, None] >= doc_ends[None, :-1]).astype(jnp.int32), axis=1)
    doc_starts = doc_ends - doc_lens
    doc_slots = jnp.arange(doc_lens.shape[0], dtype=jnp.int32)
    start_of = jnp.sum(
        jnp.where(doc_slots[None, :] == doc_index[:, None], doc_starts[None, :], 0), axis=1
    )
    return ((token_steps - start_of).astype(jnp.float32), doc_index)


def device_layout(dev_lens, seq_len):
    positions, doc_index = jax.vmap(lambda single: sequence_layout(single, seq_len))(dev_lens)
    doc_count = dev_lens.shape[1]
    labels = doc_index + doc_count * jnp.arange(dev_lens.shape[0], dtype=jnp.int32)[:, None]
    return (positions.reshape(-1), labels.reshape(-1))


def rope_tables(positions, head_dim):
    freq_index = jnp.arange(head_dim // 2, dtype=jnp.float32)
    frequency = jnp.exp(freq_index * (-2.0 / head_dim) * math.log(ROPE_BASE))
    angle_table = positions[:, None] * frequency[None, :]
    return (jnp.cos(angle_table), jnp.sin(angle_table))


def slot_ranks(route_flat, prio_flat):
    same = route_flat[:, None] == route_flat[None, :]
    ahead = prio_flat[None, :] < prio_flat[:, None]
    return jnp.sum(jnp.logical_and(same, ahead).astype(jnp.int32), axis=1)


def swap_x(value):
    return lax.ppermute(value, "dp", [(i, i ^ 1) for i in range(4)])


def swap_y(value):
    return lax.ppermute(value, "dp", [(i, i ^ 2) for i in range(4)])


def swap_core(value):
    return lax.ppermute(value, "expert", [(i, i ^ 1) for i in range(8)])


def shift_up(value):
    return lax.ppermute(value, "expert", [(i, (i + 2) % 8) for i in range(8)])


def shift_down(value):
    return lax.ppermute(value, "expert", [(i, (i + 6) % 8) for i in range(8)])


def add_low(left, right):
    return (left.astype(jnp.float32) + right.astype(jnp.float32)).astype(jnp.bfloat16)


def any_spec():
    return pl.BlockSpec(memory_space=pl.ANY)


def smem_spec():
    return pl.BlockSpec(memory_space=pltpu.SMEM)


def expert_order(tuned, count):
    if not tuned:
        return jnp.arange(count, dtype=jnp.int32)
    me = lax.axis_index("expert")
    level, core = me // 2, me % 2
    order = [
        ((level + off) % 4) * 2 + (core + flip) % 2 for flip in range(2) for off in (0, 3, 1, 2)
    ]
    return jnp.stack(order).astype(jnp.int32)


def all_order():
    me = lax.axis_index("expert")
    plane = lax.axis_index("dp")
    level, core = me // 2, me % 2
    order = [
        ((plane ^ k) * 4 + (level + off) % 4) * 2 + (core + flip) % 2
        for flip in range(2)
        for k in range(4)
        for off in (0, 3, 1, 2)
    ]
    return jnp.stack(order).astype(jnp.int32)


def dot_nn(left, right):
    return lax.dot_general(
        left, right, (((1,), (0,)), ((), ())), preferred_element_type=jnp.float32
    )


def dot_nt(left, right):
    return lax.dot_general(
        left, right, (((1,), (1,)), ((), ())), preferred_element_type=jnp.float32
    )


def dot_tn(left, right):
    return lax.dot_general(
        left, right, (((0,), (0,)), ((), ())), preferred_element_type=jnp.float32
    )


GELU_SCALE = math.sqrt(2.0 / math.pi)
GELU_CUBE = 0.044715
MIB = 1024 * 1024


def deal_copies(scalar_ref, early, piece, block, dst, row, sem):
    devices = len(early)
    copies = []
    for k in range(SEQ_DEV):
        start = pl.multiple_of(scalar_ref[1 + block * SEQ_DEV + k] * piece, piece)
        for q in range(devices):
            place = scalar_ref[1 + devices * SEQ_DEV + q] * piece
            to = pl.multiple_of(row + k * devices * piece + place, piece)
            copies.append(
                pltpu.make_async_copy(
                    early[q].at[pl.ds(start, piece), :], dst.at[pl.ds(to, piece), :], sem
                )
            )
    return copies


def give_back(scalar_ref, piece, block, src, keep, send, sem):
    devices = keep.shape[0] + send.shape[0]
    half = devices // 2
    for j in range(devices):
        to = scalar_ref[1 + devices * SEQ_DEV + devices + j]
        for k in range(SEQ_DEV):
            start = pl.multiple_of(scalar_ref[1 + block * SEQ_DEV + k] * piece, piece)
            part = src.at[pl.ds((k * devices + j) * piece, piece), :]

            @pl.when(to < half)
            def _(part=part, to=to, start=start):
                dst = keep.at[to, pl.ds(start, piece), :]
                pltpu.make_async_copy(part, dst, sem).start()

            @pl.when(to >= half)
            def _(part=part, to=to, start=start):
                dst = send.at[to - half, pl.ds(start, piece), :]
                pltpu.make_async_copy(part, dst, sem).start()


def expert_kernel(plan, capacity, *refs):
    count = plan["inputs"]
    my_ref, router_ref, codes_ref, grads_ref, res_ref = refs[:5]
    inputs = refs[5 : 5 + count]
    (
        back_keep,
        back_send,
        out_keep,
        out_send,
        x_out,
        dy_out,
        hid_out,
        dga_out,
        dua_out,
    ) = refs[5 + count : 14 + count]
    (
        gate_w,
        up_w,
        down_w,
        h_buf,
        d_buf,
        hot,
        x_s,
        dy_s,
        y_s,
        dx_s,
        hid_s,
        dga_s,
        dua_s,
        act_s,
        slope_s,
        codes_all,
        code_lines,
        code_s,
        gates_s,
        sgate_s,
        dg_s,
        stage_b,
        stage_o,
        sem_w,
        sem_h,
        sem_d,
        sem_c,
        sem_s,
        sem_b,
        sem_o,
    ) = refs[14 + count :]
    blocks = plan["blocks"]
    pairs = blocks // 2
    per_device, width, ff = gate_w.shape
    tokens = h_buf.shape[1] // 2
    slots = 2 * capacity
    experts = router_ref.shape[0]
    rows_all = x_s.shape[1]
    my_first = my_ref[0] * per_device
    dtype = jnp.bfloat16

    plane = my_ref[my_ref.shape[0] - 1]

    def window(hold, axis, e, flip, step):
        start = 0 if flip is None else pl.multiple_of((plane ^ flip) * step, step)
        if axis == 1:
            return hold.at[e, pl.ds(start, step), :]
        return hold.at[e, :, pl.ds(start, step)]

    weight_copies = []
    for t, (hold, axis) in enumerate(((gate_w, 1), (up_w, 1), (down_w, 2))):
        for e in range(per_device):
            copies = []
            for ref_index, lead, flip in plan["weights"][t][e]:
                src = inputs[ref_index].at[lead]
                step = src.shape[axis - 1]
                sem = sem_w.at[t * per_device + e, len(copies)]
                copy = pltpu.make_async_copy(src, window(hold, axis, e, flip, step), sem)
                copy.start()
                copies.append(copy)
            weight_copies.append(copies)

    early = [inputs[i] for i in plan["early"]]
    if early:
        for b, ref in enumerate(early):
            src = ref.at[pl.ds(tokens, codes_all.shape[1]), pl.ds(0, tokens)]
            pltpu.make_async_copy(src, codes_all.at[b], sem_c).start()
    else:
        pltpu.make_async_copy(codes_ref, codes_all, sem_c).start()

    def fetch(p):
        slot = p % 2
        copies = []
        for half in range(2):
            for k, (ref_index, lead, row, rows) in enumerate(plan["tokens"][2 * p + half]):
                src = inputs[ref_index] if lead is None else inputs[ref_index].at[lead]
                dst = h_buf.at[slot, pl.ds(half * tokens + row, rows), :]
                copies.append(pltpu.make_async_copy(src, dst, sem_h.at[slot, half, k]))
        if early:
            deals = []
            for half in range(2):
                deals += deal_copies(
                    my_ref,
                    early,
                    plan["piece"],
                    2 * p + half,
                    d_buf.at[slot],
                    half * tokens,
                    sem_d.at[slot],
                )
        else:
            deals = [
                pltpu.make_async_copy(
                    grads_ref.at[2 * p + half],
                    d_buf.at[slot, pl.ds(half * tokens, tokens), :],
                    sem_d.at[slot],
                )
                for half in range(2)
            ]
        for copy in copies + deals:
            copy.start()
        return copies + [pltpu.make_async_copy(d_buf.at[slot], d_buf.at[slot], sem_d.at[slot])]

    def hits(codes_of, shape, slot_axis):
        slot = lax.broadcasted_iota(jnp.int32, shape, slot_axis)
        token = lax.broadcasted_iota(jnp.int32, shape, 1 - slot_axis)
        second = slot >= capacity
        same = jnp.logical_xor(second, token < tokens)
        rank = slot - jnp.where(second, capacity, 0)
        return jnp.logical_and(same, codes_of == (rank + 1).astype(jnp.float32))

    flying = fetch(0)
    pltpu.make_async_copy(codes_all, codes_all, sem_c).wait()
    for p in range(pairs):
        slot = p % 2
        later = fetch(p + 1) if p + 1 < pairs else []
        for copy in flying:
            copy.wait()
        flying = later
        codes = jnp.concatenate([codes_all[2 * p], codes_all[2 * p + 1]], axis=1)
        codes = codes.astype(jnp.float32)[:experts]
        logits = dot_nt(router_ref[...], h_buf[slot])
        chosen = codes > 0.0
        top = jnp.max(jnp.where(chosen, logits, NEG_FILL), axis=0, keepdims=True)
        raised = jnp.where(chosen, jnp.exp(logits - top), 0.0)
        code_s[...] = codes
        gates_s[...] = raised / jnp.sum(raised, axis=0, keepdims=True)
        flipped = codes.T
        lane = lax.broadcasted_iota(jnp.int32, flipped.shape, 1)
        picks, ones = [], []
        for e in range(per_device):
            code_row = code_s[pl.ds(my_first + e, 1), :]
            gate_row = gates_s[pl.ds(my_first + e, 1), :]
            hit = hits(code_row, (slots, 2 * tokens), 0)
            code_lines[e, p] = code_row
            picks.append(jnp.where(hit, 1.0, 0.0).astype(dtype))
            gate_slot = jnp.sum(jnp.where(hit, gate_row, 0.0), axis=1, keepdims=True)
            sgate_s[e, pl.ds(p * slots, slots), :] = jnp.broadcast_to(gate_slot, (slots, 128))
            code_col = jnp.sum(
                jnp.where(lane == my_first + e, flipped, 0.0), axis=1, keepdims=True
            )
            ones.append(jnp.where(hits(code_col, (2 * tokens, slots), 1), 1.0, 0.0).astype(dtype))
        pick = jnp.concatenate(picks, axis=0)
        hot[p] = jnp.concatenate(ones, axis=1)
        for hold, buf in ((x_s, h_buf), (dy_s, d_buf)):
            taken = dot_nn(pick, buf[slot]).astype(dtype)
            for e in range(per_device):
                hold[e, pl.ds(p * slots, slots), :] = taken[e * slots : (e + 1) * slots]

    saves = []
    for e in range(per_device):
        for copy in weight_copies[e] + weight_copies[per_device + e]:
            copy.wait()
        save = pltpu.make_async_copy(x_s.at[e], x_out.at[e], sem_s.at[0, e])
        save.start()
        saves.append(save)
        gate_slot = sgate_s[e][:, :1]

        act_s[...] = dot_nn(x_s[e], gate_w[e])
        slope_s[...] = dot_nn(x_s[e], up_w[e])

        @pl.loop(0, rows_all // slots)
        def _(j):
            rows = pl.ds(pl.multiple_of(j * slots, slots), slots)
            ga = act_s[rows, :]
            ua = slope_s[rows, :]
            square = ga * ga
            tan = jnp.tanh(GELU_SCALE * (ga + GELU_CUBE * square * ga))
            act = 0.5 * ga * (1.0 + tan)
            slope = 0.5 * (1.0 + tan) + 0.5 * ga * (1.0 - tan * tan) * GELU_SCALE * (
                1.0 + 3.0 * GELU_CUBE * square
            )
            act_s[rows, :] = act
            slope_s[rows, :] = ua * slope
            hid_s[e, rows, :] = (act * ua).astype(dtype)

        save = pltpu.make_async_copy(hid_s.at[e], hid_out.at[e], sem_s.at[1, e])
        save.start()
        saves.append(save)
        for copy in weight_copies[2 * per_device + e]:
            copy.wait()
        dg_s[e] = jnp.zeros(dg_s.shape[1:], jnp.float32)

        @pl.loop(0, width // 768)
        def _(j):
            cols = pl.ds(pl.multiple_of(j * 768, 768), 768)
            y = dot_nn(hid_s[e], down_w[e, :, cols]).astype(dtype).astype(jnp.float32)
            dy = dy_s[e, :, cols].astype(jnp.float32)
            dg_s[e] += jnp.broadcast_to(
                jnp.sum(dy * y, axis=1, keepdims=True), dg_s.shape[1:]
            )
            y_s[e, :, cols] = (gate_slot * y).astype(dtype)
            dy_s[e, :, cols] = (gate_slot * dy).astype(dtype)

        save = pltpu.make_async_copy(dy_s.at[e], dy_out.at[e], sem_s.at[2, e])
        save.start()
        saves.append(save)

        dhid = dot_nt(dy_s[e], down_w[e])
        dga_s[e] = (dhid * slope_s[...]).astype(dtype)
        dua_s[e] = (dhid * act_s[...]).astype(dtype)

        for k, (hold, out) in enumerate(((dga_s, dga_out), (dua_s, dua_out))):
            save = pltpu.make_async_copy(hold.at[e], out.at[e], sem_s.at[3 + k, e])
            save.start()
            saves.append(save)

        @pl.loop(0, width // 768)
        def _(j):
            cols = pl.ds(pl.multiple_of(j * 768, 768), 768)
            dx = dot_nt(dga_s[e], gate_w[e, cols, :]) + dot_nt(dua_s[e], up_w[e, cols, :])
            dx_s[e, :, cols] = dx.astype(dtype)

    table_rows = stage_b.shape[2] - tokens
    table_row = lax.broadcasted_iota(jnp.int32, (table_rows, 2 * tokens), 0)
    sends = {}
    for p in range(pairs):
        slot = p % 2
        for copy in sends.pop(p - 2, []):
            copy.wait()
        rows = pl.ds(p * slots, slots)

        @pl.loop(0, width // 768)
        def _(j):
            cols = pl.ds(pl.multiple_of(j * 768, 768), 768)
            back, outs = [
                dot_nn(
                    hot[p],
                    jnp.concatenate([hold[e, rows, cols] for e in range(per_device)], axis=0),
                )
                for hold in (dx_s, y_s)
            ]
            for half in range(2):
                part = slice(half * tokens, (half + 1) * tokens)
                stage_b[slot, half, :tokens, cols] = back[part].astype(dtype)
                mixed = outs[part]
                if early and p == 0 and half == 0:
                    mixed = mixed + res_ref[:, cols]
                stage_o[slot, half, :, cols] = mixed.astype(dtype)

        tables = [jnp.zeros((table_rows, 2 * tokens), jnp.float32) for _ in range(2)]
        for e in range(per_device):
            dg = dg_s[e, rows, :][:, :1]
            code_row = code_lines[e, p]
            line = jnp.sum(
                jnp.where(hits(code_row, (slots, 2 * tokens), 0), dg, 0.0), axis=0, keepdims=True
            )
            mine = table_row == my_first + e
            for half in range(2):
                part = line[:, half * tokens : (half + 1) * tokens]
                high = part.astype(dtype).astype(jnp.float32)
                both = jnp.concatenate([high, part - high], axis=1)
                tables[half] = jnp.where(mine, both, tables[half])
        for half in range(2):
            stage_b[slot, half, tokens:, : 2 * tokens] = tables[half].astype(dtype)
            stage_b[slot, half, tokens:, 2 * tokens :] = jnp.zeros(
                (table_rows, width - 2 * tokens), dtype
            )
        first = 2 * p
        keep = first < blocks // 2
        at = pl.ds(first if keep else first - blocks // 2, 2)
        copies = [
            pltpu.make_async_copy(
                stage_b.at[slot], (back_keep if keep else back_send).at[at], sem_b.at[slot]
            )
        ]
        if early:
            for half in range(2):
                give_back(
                    my_ref,
                    plan["piece"],
                    first + half,
                    stage_o.at[slot, half],
                    out_keep,
                    out_send,
                    sem_o.at[slot],
                )
        else:
            copies.append(
                pltpu.make_async_copy(
                    stage_o.at[slot], (out_keep if keep else out_send).at[at], sem_o.at[slot]
                )
            )
        for copy in copies:
            copy.start()
        if early:
            copies.append(
                pltpu.make_async_copy(stage_o.at[slot], stage_o.at[slot], sem_o.at[slot])
            )
        sends[p] = copies
    for copies in sends.values():
        for copy in copies:
            copy.wait()
    for save in saves:
        save.wait()


def run_experts(plan, capacity, table_rows, scalars, router_t, codes, grads_all, res, inputs):
    experts, width = router_t.shape
    blocks, tokens = plan["blocks"], plan["token_count"]
    per_device, ff = plan["per_device"], plan["ff"]
    rows = blocks * capacity
    bf, f32 = jnp.bfloat16, jnp.float32
    half = blocks // 2
    back = jax.ShapeDtypeStruct((half, tokens + table_rows, width), bf)
    outs = jax.ShapeDtypeStruct((half, tokens, width), bf)
    wide = jax.ShapeDtypeStruct((per_device, rows, width), bf)
    thin = jax.ShapeDtypeStruct((per_device, rows, ff), bf)
    vmem = pl.BlockSpec(memory_space=pltpu.VMEM)
    sem = pltpu.SemaphoreType.DMA
    return pl.pallas_call(
        lambda *refs: expert_kernel(plan, capacity, *refs),
        out_shape=(back, back, outs, outs, wide, wide, thin, thin, thin),
        in_specs=[smem_spec(), vmem, any_spec(), any_spec(), vmem] + [any_spec()] * len(inputs),
        out_specs=tuple([any_spec()] * 9),
        scratch_shapes=[
            pltpu.VMEM((per_device, width, ff), bf),
            pltpu.VMEM((per_device, width, ff), bf),
            pltpu.VMEM((per_device, ff, width), bf),
            pltpu.VMEM((2, 2 * tokens, width), bf),
            pltpu.VMEM((2, 2 * tokens, width), bf),
            pltpu.VMEM((blocks // 2, 2 * tokens, per_device * 2 * capacity), bf),
            pltpu.VMEM((per_device, rows, width), bf),
            pltpu.VMEM((per_device, rows, width), bf),
            pltpu.VMEM((per_device, rows, width), bf),
            pltpu.VMEM((per_device, rows, width), bf),
            pltpu.VMEM((per_device, rows, ff), bf),
            pltpu.VMEM((per_device, rows, ff), bf),
            pltpu.VMEM((per_device, rows, ff), bf),
            pltpu.VMEM((rows, ff), f32),
            pltpu.VMEM((rows, ff), f32),
            pltpu.VMEM((blocks, table_rows, tokens), bf),
            pltpu.VMEM((per_device, blocks // 2, 1, 2 * tokens), f32),
            pltpu.VMEM((experts, 2 * tokens), f32),
            pltpu.VMEM((experts, 2 * tokens), f32),
            pltpu.VMEM((per_device, rows, 128), f32),
            pltpu.VMEM((per_device, rows, 128), f32),
            pltpu.VMEM((2, 2, tokens + table_rows, width), bf),
            pltpu.VMEM((2, 2, tokens, width), bf),
            sem((3 * per_device, 4)),
            sem((2, 2, 2)),
            sem((2,)),
            sem,
            sem((5, per_device)),
            sem((2,)),
            sem((2,)),
        ],
        cost_estimate=pl.CostEstimate(flops=55000000000, transcendentals=0, bytes_accessed=50000000),
        compiler_params=pltpu.CompilerParams(vmem_limit_bytes=61 * MIB),
    )(scalars, router_t, codes, grads_all, res, *inputs)


def weight_kernel(x_ref, dga_ref, dua_ref, hid_ref, dy_ref, out_ref):
    group, _, _, step, ff = out_ref.shape
    dtype = jnp.bfloat16
    for i, right in enumerate((dga_ref, dua_ref)):
        grads = dot_tn(x_ref[0], right[0]).astype(dtype)
        for d in range(group):
            out_ref[d, i, 0] = grads[d * step : (d + 1) * step]
    grads = dot_tn(hid_ref[0], dy_ref[0]).astype(dtype)
    for d in range(group):
        for i in range(ff // step):
            part = slice(i * step, (i + 1) * step)
            out_ref[d, 2, 0, :, part] = grads[part, d * step : (d + 1) * step]


def expert_weight_grads(x, dga, dua, hid, dy, parts):
    per_device, rows, ff = dga.shape
    step = x.shape[2] // parts
    group = 2
    whole = pl.BlockSpec((1, rows, ff), lambda e, d: (e, 0, 0))
    piece = pl.BlockSpec((1, rows, group * step), lambda e, d: (e, 0, d))
    return pl.pallas_call(
        weight_kernel,
        grid=(per_device, parts // group),
        out_shape=jax.ShapeDtypeStruct((parts, 3, per_device, step, ff), jnp.bfloat16),
        in_specs=[piece, whole, whole, whole, piece],
        out_specs=pl.BlockSpec((group, 3, 1, step, ff), lambda e, d: (d, 0, e, 0, 0)),
        cost_estimate=pl.CostEstimate(
            flops=18700000000, transcendentals=0, bytes_accessed=17000000
        ),
        compiler_params=pltpu.CompilerParams(vmem_limit_bytes=56 * MIB),
    )(x, dga, dua, hid, dy)


def down_kernel(hid_ref, dy_ref, out_ref):
    out_ref[0] = dot_tn(hid_ref[0], dy_ref[0]).astype(jnp.bfloat16)


def gate_up_kernel(x_ref, dga_ref, dua_ref, out_ref):
    out_ref[0, 0] = dot_tn(x_ref[0], dga_ref[0]).astype(jnp.bfloat16)
    out_ref[1, 0] = dot_tn(x_ref[0], dua_ref[0]).astype(jnp.bfloat16)


def whole_weight_grads(x, dga, dua, hid, dy):
    per_device, rows, ff = dga.shape
    width = x.shape[2]
    thin = pl.BlockSpec((1, rows, ff), lambda e: (e, 0, 0))
    wide = pl.BlockSpec((1, rows, width), lambda e: (e, 0, 0))
    down = pl.pallas_call(
        down_kernel,
        grid=(per_device,),
        out_shape=jax.ShapeDtypeStruct((per_device, ff, width), jnp.bfloat16),
        in_specs=[thin, wide],
        out_specs=pl.BlockSpec((1, ff, width), lambda e: (e, 0, 0)),
        compiler_params=pltpu.CompilerParams(vmem_limit_bytes=40 * MIB),
    )(hid, dy)
    gate_up = pl.pallas_call(
        gate_up_kernel,
        grid=(per_device,),
        out_shape=jax.ShapeDtypeStruct((2, per_device, width, ff), jnp.bfloat16),
        in_specs=[wide, thin, thin],
        out_specs=pl.BlockSpec((2, 1, width, ff), lambda e: (0, e, 0, 0)),
        compiler_params=pltpu.CompilerParams(vmem_limit_bytes=40 * MIB),
    )(x, dga, dua)
    return gate_up, down


def gather_inputs(value, weights, count, tuned):
    rows = value.shape[0]
    if not tuned:
        full = lax.all_gather(value, "expert", axis=0, tiled=False)
        places = [[[(t, (e,), None)] for e in range(count)] for t in range(3)]
        return list(weights) + [full], places, [[(3, b, 0, rows)] for b in range(full.shape[0])]
    both, both_x, both_y, down, down_x, down_y, down_a, down_b = weights
    below = shift_up(value)
    above = shift_down(value)
    below, above, both_x, both_y = lax.optimization_barrier((below, above, both_x, both_y))
    tokens = [value, below, above, shift_up(below)]
    tokens = tokens + [swap_core(v) for v in tokens]
    arrays = [both, both_x, both_y, swap_x(both_y[0]), swap_y(both_x[1])]
    arrays = arrays + [down, down_x, down_y, down_a, down_b]
    places = [
        [[(k, (t, e), k) for k in range(3)] + [(3 + t, (e,), 3)] for e in range(count)]
        for t in range(2)
    ]
    places.append(
        [[(5 + k, (e,), k) for k in range(3)] + [(8 + e, (0,), 3)] for e in range(count)]
    )
    token_places = []
    for base in (10, 14):
        token_places += [[(base + k, None, 0, rows)] for k in range(4)]
    return arrays + tokens, places, token_places


def rotate(values, cos_wide, sin_wide):
    return values * cos_wide + pltpu.roll(values, HEAD_SIZE // 2, 1) * sin_wide


def tile_cols(j, size):
    return pl.ds(pl.multiple_of(j * size, size), size)


def forward_kernel(plan, *refs):
    order_ref, x_ref, cos_ref, sin_ref, lab_col_ref, lab_row_ref = refs[:6]
    count = plan["inputs"]
    inputs = refs[6 : 6 + count]
    (
        h2_ref,
        res_ref,
        h1_ref,
        q_ref,
        k_ref,
        v_ref,
        p_ref,
        o_ref,
        aux_ref,
        w_full_out,
        w_full,
        sem_in,
        sem_save,
    ) = refs[6 + count :]
    width = x_ref.shape[1]
    tokens = x_ref.shape[0]
    bf = jnp.bfloat16
    heads = QUERY_HEADS // KEY_VALUE_HEADS
    kv_width = KEY_VALUE_HEADS * HEAD_SIZE
    main = width + 2 * kv_width
    base = main + 128
    for ref_index, lead, order_index in plan["places"]:
        src = inputs[ref_index]
        for at in lead:
            src = src.at[at]
        rows = src.shape[0]
        if order_index is None:
            dst = w_full
        else:
            start = pl.multiple_of(order_ref[order_index] * rows, rows)
            dst = w_full.at[pl.ds(start, rows), :]
        pltpu.make_async_copy(src, dst, sem_in).start()
    x = x_ref[...].astype(jnp.float32)
    inverse = lax.rsqrt(jnp.mean(x * x, axis=1, keepdims=True) + EPSILON)
    pltpu.make_async_copy(w_full, w_full, sem_in).wait()
    save = pltpu.make_async_copy(w_full, w_full_out, sem_save)
    save.start()
    side = w_full[:, main : main + 128].astype(jnp.float32).T
    gain = side[:1]
    h1_ref[...] = (x * inverse * gain).astype(bf)
    cos_wide, sin_wide = cos_ref[...], sin_ref[...]

    @pl.loop(0, width // 768)
    def _(j):
        raw = dot_nn(h1_ref[...], w_full[:, tile_cols(j, 768)])
        both = [
            rotate(raw[:, half * HEAD_SIZE : (half + 1) * HEAD_SIZE], cos_wide, sin_wide)
            for half in range(768 // HEAD_SIZE)
        ]
        q_ref[:, tile_cols(j, 768)] = jnp.concatenate(both, axis=1).astype(bf)

    raw = dot_nn(h1_ref[...], w_full[:, width:main])
    both = [
        rotate(raw[:, half * HEAD_SIZE : (half + 1) * HEAD_SIZE], cos_wide, sin_wide)
        for half in range(KEY_VALUE_HEADS)
    ]
    k_ref[...] = jnp.concatenate(both, axis=1).astype(bf)
    v_ref[...] = raw[:, kv_width:].astype(bf)
    seq_len = tokens // SEQ_DEV
    query_step = lax.broadcasted_iota(jnp.int32, (seq_len, seq_len), 0)
    key_step = lax.broadcasted_iota(jnp.int32, (seq_len, seq_len), 1)
    for s in range(SEQ_DEV):
        rows = slice(s * seq_len, (s + 1) * seq_len)
        same = lab_col_ref[rows, :] == lab_row_ref[:, rows]
        allowed = jnp.logical_and(same, query_step >= key_step)[None]
        for h in range(KEY_VALUE_HEADS):
            cols = slice(h * HEAD_SIZE, (h + 1) * HEAD_SIZE)
            stack = jnp.concatenate(
                [
                    q_ref[rows, (h * heads + g) * HEAD_SIZE : (h * heads + g + 1) * HEAD_SIZE]
                    for g in range(heads)
                ],
                axis=0,
            )
            scores = dot_nt(stack, k_ref[rows, cols]) * HEAD_SIZE ** (-0.5)
            scores = scores.reshape(heads, seq_len, seq_len)
            scores = jnp.where(allowed, scores, NEG_FILL)
            top = jnp.max(scores, axis=2, keepdims=True)
            raised = jnp.exp(scores - top)
            probs = raised / jnp.sum(raised, axis=2, keepdims=True)
            probs = probs.reshape(heads * seq_len, seq_len)
            p_ref[s, h] = probs
            mixed = dot_nn(probs.astype(bf), v_ref[rows, cols]).astype(bf)
            for g in range(heads):
                o_ref[rows, (h * heads + g) * HEAD_SIZE : (h * heads + g + 1) * HEAD_SIZE] = mixed[
                    g * seq_len : (g + 1) * seq_len
                ]
    side_out = w_full[:, base + width : base + width + 128].astype(jnp.float32).T
    aux_ref[...] = jnp.concatenate([side_out, side[:8]], axis=0)

    @pl.loop(0, width // 768)
    def _(j):
        cols = tile_cols(j, 768)
        at = pl.ds(pl.multiple_of(base + j * 768, 128), 768)
        res_ref[:, cols] = x_ref[:, cols].astype(jnp.float32) + dot_nn(o_ref[...], w_full[:, at])

    res = res_ref[...]
    inverse = lax.rsqrt(jnp.mean(res * res, axis=1, keepdims=True) + EPSILON)
    moe_row = plan["experts"]
    h2_ref[...] = (res * inverse * side_out[moe_row : moe_row + 1]).astype(bf)
    save.wait()


def run_forward(plan, order, x, cos_wide, sin_wide, lab_col, lab_row, inputs, w_cols):
    tokens, width = x.shape
    bf, f32 = jnp.bfloat16, jnp.float32
    kv_width = KEY_VALUE_HEADS * HEAD_SIZE
    seq_len = tokens // SEQ_DEV
    stack = QUERY_HEADS // KEY_VALUE_HEADS * seq_len
    vmem = pl.BlockSpec(memory_space=pltpu.VMEM)
    shape = jax.ShapeDtypeStruct
    sem = pltpu.SemaphoreType.DMA
    return pl.pallas_call(
        lambda *refs: forward_kernel(plan, *refs),
        out_shape=(
            shape((tokens, width), bf),
            shape((tokens, width), f32),
            shape((tokens, width), bf),
            shape((tokens, width), bf),
            shape((tokens, kv_width), bf),
            shape((tokens, kv_width), bf),
            shape((SEQ_DEV, KEY_VALUE_HEADS, stack, seq_len), f32),
            shape((tokens, width), bf),
            shape((136, width), f32),
            shape((width, w_cols), bf),
        ),
        in_specs=[smem_spec()] + [vmem] * 5 + [any_spec()] * len(inputs),
        out_specs=tuple([vmem] * 9 + [any_spec()]),
        scratch_shapes=[
            pltpu.VMEM((width, w_cols), bf),
            sem,
            sem,
        ],
        cost_estimate=pl.CostEstimate(flops=110000000000, transcendentals=0, bytes_accessed=16000000),
        compiler_params=pltpu.CompilerParams(vmem_limit_bytes=56 * MIB),
    )(order, x, cos_wide, sin_wide, lab_col, lab_row, *inputs)


def send_payload(order_ref, payload, start_col, outs, sem):
    cols = pl.ds(start_col, outs[0].shape[-1])
    if len(outs) == 1:
        pltpu.make_async_copy(payload.at[:, cols], outs[0], sem).start()
        return
    rows = payload.shape[0] // 32
    for c in range(2):
        x_one, y_one, x_two, y_two, own = outs[c * 5 : c * 5 + 5]
        places = [own.at[r] for r in range(4)]
        places += [x_one.at[1, 0], x_one.at[1, 1], x_two.at[0], x_two.at[1]]
        places += [y_two.at[0], y_two.at[1], y_one.at[1, 0], y_one.at[1, 1]]
        places += [x_one.at[0, 0], x_one.at[0, 1], y_one.at[0, 0], y_one.at[0, 1]]
        for j, dst in enumerate(places):
            start = pl.multiple_of(order_ref[c * 16 + j] * rows, rows)
            pltpu.make_async_copy(payload.at[pl.ds(start, rows), cols], dst, sem).start()


def payload_shapes(tuned, rows, cols):
    if not tuned:
        return (jax.ShapeDtypeStruct((rows, cols), jnp.bfloat16),)
    piece = rows // 32
    shapes = [(2, 2), (2, 2), (2,), (2,), (4,)]
    one = tuple(jax.ShapeDtypeStruct(v + (piece, cols), jnp.bfloat16) for v in shapes)
    return one + one


def backward_kernel(experts, sums, piece, order_ref, own_ref, *refs):
    given = 8 if piece else 2
    early, refs = refs[:given], refs[given:]
    back_refs = refs[:sums]
    res_ref, h2_ref, o_ref, aux_ref, x_ref, cos_ref, sin_ref = refs[sums : sums + 7]
    h1_ref, q_ref, k_ref, v_ref, p_ref, w_full_ref = refs[sums + 7 : sums + 13]
    rest = refs[sums + 13 :]
    outs = rest[:-13]
    dx_ref, w_full, dy, codes, payload, dres_ref, dres_low, dmix_ref, dqkv, dh1 = rest[-13:-3]
    sem_w, sem_d, sem_p = rest[-3:]
    tokens, width = res_ref.shape
    bf = jnp.bfloat16
    heads = QUERY_HEADS // KEY_VALUE_HEADS
    kv_width = KEY_VALUE_HEADS * HEAD_SIZE
    main = width + 2 * kv_width
    base = main + 128
    scale = HEAD_SIZE ** (-0.5)
    load = pltpu.make_async_copy(w_full_ref, w_full, sem_w.at[0])
    load.start()
    if piece:
        src = early[0].at[pl.ds(tokens, codes.shape[0]), pl.ds(0, tokens)]
        loads = deal_copies(own_ref, early, piece, 0, dy, 0, sem_d)
    else:
        src = early[1].at[own_ref[0]]
        loads = [pltpu.make_async_copy(early[0].at[own_ref[0]], dy, sem_d)]
    load_codes = pltpu.make_async_copy(src, codes, sem_w.at[1])
    load_codes.start()
    for copy in loads:
        copy.start()
    back = back_refs[0][...]
    for ref in back_refs[1:]:
        back = back + ref[...].astype(jnp.float32)
    grad_pair = (
        back[tokens : tokens + experts, :tokens]
        + back[tokens : tokens + experts, tokens : 2 * tokens]
    )
    back = back[:tokens]
    router_t = aux_ref[:experts, :].astype(bf)
    gain = aux_ref[experts : experts + 1, :]
    logits = dot_nt(router_t, h2_ref[...])
    load_codes.wait()
    chosen = codes[...].astype(jnp.float32)[:experts] > 0.0
    top = jnp.max(jnp.where(chosen, logits, NEG_FILL), axis=0, keepdims=True)
    raised = jnp.where(chosen, jnp.exp(logits - top), 0.0)
    gates = raised / jnp.sum(raised, axis=0, keepdims=True)
    inner = jnp.sum(gates * grad_pair, axis=0, keepdims=True)
    dlog = jnp.where(chosen, gates * (grad_pair - inner), 0.0).astype(bf)
    grad_router = dot_nn(dlog, h2_ref[...])
    dh2 = back + dot_tn(dlog, router_t)
    res = res_ref[...]
    inverse = lax.rsqrt(jnp.mean(res * res, axis=1, keepdims=True) + EPSILON)
    scaled = dh2 * gain
    grad_gain = jnp.sum(dh2 * res * inverse, axis=0, keepdims=True)
    pltpu.make_async_copy(dy, dy, sem_d).wait()
    dres = (
        dy[...].astype(jnp.float32)
        + inverse * scaled
        - res * inverse**3 * jnp.mean(scaled * res, axis=1, keepdims=True)
    )
    dres_ref[...] = dres
    dres_low[...] = dres.astype(bf)
    pad = jnp.zeros((128 - experts - 8, width), jnp.float32)
    side = jnp.concatenate(
        [grad_router, jnp.broadcast_to(grad_gain, (8, width)), pad], axis=0
    )
    payload[:, base + width : base + width + 128] = side.T.astype(bf)

    @pl.loop(0, width // 768)
    def _(j):
        cols = tile_cols(j, 768)
        at = pl.ds(pl.multiple_of(base + j * 768, 128), 768)
        payload[:, at] = dot_tn(o_ref[...], dres_low[:, cols]).astype(bf)

    send_payload(order_ref, payload, base, outs[len(outs) // 2 :], sem_p)
    load.wait()

    @pl.loop(0, width // 768)
    def _(j):
        cols = tile_cols(j, 768)
        dmix_ref[:, cols] = dot_nt(dres_low[...], w_full[cols, base : base + width]).astype(bf)

    seq_len = tokens // SEQ_DEV
    for s in range(SEQ_DEV):
        rows = slice(s * seq_len, (s + 1) * seq_len)
        cos_wide, sin_wide = cos_ref[rows, :], -sin_ref[rows, :]
        cos_tall = jnp.concatenate([cos_wide] * heads, axis=0)
        sin_tall = jnp.concatenate([sin_wide] * heads, axis=0)
        for h in range(KEY_VALUE_HEADS):
            cols = slice(h * HEAD_SIZE, (h + 1) * HEAD_SIZE)
            places = [
                slice((h * heads + g) * HEAD_SIZE, (h * heads + g + 1) * HEAD_SIZE)
                for g in range(heads)
            ]
            q_tall = jnp.concatenate([q_ref[rows, place] for place in places], axis=0)
            dmix = jnp.concatenate([dmix_ref[rows, place] for place in places], axis=0)
            probs = p_ref[s, h]
            dprobs = dot_nt(dmix, v_ref[rows, cols])
            dv = dot_tn(probs.astype(bf), dmix)
            inner = jnp.sum(probs * dprobs, axis=1, keepdims=True)
            dscores = (probs * (dprobs - inner)).astype(bf)
            dq = rotate(dot_nn(dscores, k_ref[rows, cols]) * scale, cos_tall, sin_tall)
            dk = rotate(dot_tn(dscores, q_tall) * scale, cos_wide, sin_wide)
            for g, place in enumerate(places):
                dqkv[rows, place] = dq[g * seq_len : (g + 1) * seq_len].astype(bf)
            dqkv[rows, width + h * HEAD_SIZE : width + (h + 1) * HEAD_SIZE] = dk.astype(bf)
            at = width + kv_width + h * HEAD_SIZE
            dqkv[rows, at : at + HEAD_SIZE] = dv.astype(bf)
    @pl.loop(0, width // 768)
    def _(j):
        cols = tile_cols(j, 768)
        dh1[:, cols] = dot_nt(dqkv[...], w_full[cols, :main])

    @pl.loop(0, main // 1024)
    def _(j):
        cols = tile_cols(j, 1024)
        payload[:, cols] = dot_tn(h1_ref[...], dqkv[:, cols]).astype(bf)

    x = x_ref[...].astype(jnp.float32)
    gain = aux_ref[128:129, :]
    inverse = lax.rsqrt(jnp.mean(x * x, axis=1, keepdims=True) + EPSILON)
    grad = dh1[...]
    scaled = grad * gain
    grad_gain = jnp.sum(grad * x * inverse, axis=0, keepdims=True)
    payload[:, main : main + 128] = jnp.broadcast_to(grad_gain, (128, width)).T.astype(bf)
    dx = (
        dres_ref[...]
        + inverse * scaled
        - x * inverse**3 * jnp.mean(scaled * x, axis=1, keepdims=True)
    )
    send_payload(order_ref, payload, 0, outs[: len(outs) // 2], sem_p)
    dx_ref[...] = dx.astype(bf)
    pltpu.make_async_copy(payload, payload, sem_p).wait()


def run_backward(tuned, experts, piece, order, own, early, rows, backs, saved, w_full):
    tokens, width = saved[0].shape
    bf, f32 = jnp.bfloat16, jnp.float32
    vmem = pl.BlockSpec(memory_space=pltpu.VMEM)
    shape = jax.ShapeDtypeStruct
    sem = pltpu.SemaphoreType.DMA
    main = width + 2 * KEY_VALUE_HEADS * HEAD_SIZE
    payload = payload_shapes(tuned, width, main + 128)
    payload = payload + payload_shapes(tuned, width, width + 128)
    return pl.pallas_call(
        lambda *refs: backward_kernel(experts, len(backs), piece, *refs),
        out_shape=payload + (shape((tokens, width), bf),),
        in_specs=[smem_spec()] * 2
        + [any_spec()] * len(early)
        + [vmem] * (len(backs) + len(saved))
        + [any_spec()],
        out_specs=tuple([any_spec()] * len(payload) + [vmem]),
        scratch_shapes=[
            pltpu.VMEM(w_full.shape, bf),
            pltpu.VMEM((tokens, width), bf),
            pltpu.VMEM((rows, tokens), bf),
            pltpu.VMEM(w_full.shape, bf),
            pltpu.VMEM((tokens, width), f32),
            pltpu.VMEM((tokens, width), bf),
            pltpu.VMEM((tokens, width), bf),
            pltpu.VMEM((tokens, main), bf),
            pltpu.VMEM((tokens, width), f32),
            sem((2,)),
            sem,
            sem,
        ],
        cost_estimate=pl.CostEstimate(
            flops=165000000000, transcendentals=0, bytes_accessed=32000000
        ),
        compiler_params=pltpu.CompilerParams(vmem_limit_bytes=60 * MIB),
    )(order, own, *early, *backs, *saved, w_full)


def after(value, *others):
    return lax.optimization_barrier((value,) + others)[0]


def swap_diagonal(value):
    return lax.ppermute(value, "dp", [(i, i ^ 3) for i in range(4)])


def shift_two(value):
    return lax.ppermute(value, "expert", [(i, (i + 4) % 8) for i in range(8)])


def gather_front(pack, early, sent, w_gate, w_up, w_down, tuned):
    if not tuned:
        got = lax.all_to_all(sent, "expert", split_axis=0, concat_axis=2, tiled=True)
        full = lax.all_gather(pack, ("dp", "expert"), axis=0, tiled=True)
        dealt = [lax.all_gather(early, "expert", axis=0, tiled=False)]
        weights = [
            lax.all_gather(w_gate, "dp", axis=1, tiled=True),
            lax.all_gather(w_up, "dp", axis=1, tiled=True),
            lax.all_gather(w_down, "dp", axis=2, tiled=True),
        ]
        return got, [full], [(0, (), None)], dealt, weights
    both = jnp.stack([w_gate, w_up])
    ring = (pack, shift_up(pack), shift_down(pack), shift_two(pack))
    down_x = swap_x(w_down)
    down_y = swap_y(w_down)
    down = [w_down, down_x, down_y, swap_x(down_y[:1]), swap_y(down_x[1:])]
    *ring, _, _, both = lax.optimization_barrier(ring + tuple(down[1:3]) + (both,))
    level = after(jnp.stack(ring), *down)
    from_x = swap_x(level)
    from_y = swap_y(level)
    sent = after(sent, level)
    got = lax.all_to_all(sent, "expert", split_axis=0, concat_axis=2, tiled=True)
    early = after(early, level)
    below = shift_up(early)
    above = shift_down(early)
    far_a = swap_x(from_y[:2])
    far_b = swap_y(from_x[2:])
    both = after(both, far_a, far_b)
    both_x = swap_x(both)
    both_y = swap_y(both)
    dealt = [early, below, above, shift_up(below)]
    dealt = dealt + [swap_core(v) for v in dealt]
    arrays = [level, from_x, from_y, far_a, far_b]
    late = lax.optimization_barrier((far_a, far_b, below, above))[:2]
    arrays = arrays + [swap_core(v) for v in arrays[:3]] + [swap_core(v) for v in late]
    places = []
    for c in range(2):
        for k in range(4):
            for r in range(4):
                ref, lead = (k, r) if k < 3 else ((3, r) if r < 2 else (4, r - 2))
                places.append((c * 5 + ref, (lead,), (c * 4 + k) * 4 + r))
    return got, arrays, places, dealt, (both, both_x, both_y) + tuple(down)


def scatter_core(outs):
    got = [swap_core(v) for v in outs[5:]]
    return [add_low(outs[k], got[k]) for k in range(4)] + [outs[4], got[4]]


def scatter_planes(sums, first):
    x_one, y_one, x_two, y_two, own, got_own = sums
    x_two = swap_x(add_low(x_two, first[1][0]))
    y_two = swap_y(add_low(y_two, first[0][0]))
    level = []
    for r in range(4):
        near = (first[0][1, r], y_two[r]) if r < 2 else (x_two[r - 2], first[1][1, r - 2])
        total = own[r].astype(jnp.float32) + got_own[r].astype(jnp.float32)
        total = total + near[0].astype(jnp.float32) + near[1].astype(jnp.float32)
        level.append(total if r == 0 else total.astype(jnp.bfloat16))
    return level


def scatter_ring(level, others, short):
    below, above, far = level[1:]
    if short:
        got = [shift_down(below), shift_up(add_low(above, shift_up(far)))]
    else:
        got = [shift_down(below), shift_up(above), shift_two(far)]
    last, *others = lax.optimization_barrier((level[0],) + tuple(others))
    for v in got:
        last = last + v.astype(jnp.float32)
    return last, others


def scatter_payload(outs, tuned, others, more, grad_x):
    half = len(outs) // 2
    if not tuned:
        owned = [
            lax.psum_scatter(v, ("dp", "expert"), scatter_dimension=0, tiled=True) for v in outs
        ]
        return [v.astype(jnp.float32) for v in owned], others, more, grad_x
    first = scatter_core(outs[:half])
    second = scatter_core(outs[half:])
    first_got = [swap_x(first[0]), swap_y(first[1])]
    tied = lax.optimization_barrier(tuple(first_got) + (first[2], first[3], grad_x) + tuple(more[1:]))
    first_got, first[2:4], grad_x, more[1:] = list(tied[:2]), tied[2:4], tied[4], tied[5:]
    first_level = scatter_planes(first, first_got)
    sent = lax.optimization_barrier((second[0], second[1]) + tuple(first_got))
    second_got = [swap_x(sent[0]), swap_y(sent[1])]
    second_level = scatter_planes(second, second_got)
    more = lax.optimization_barrier(tuple(more) + (first_level[1],))[:-1]
    owned_in, _ = scatter_ring(first_level, second_level[1:2], True)
    owned_out, others = scatter_ring(second_level, others, False)
    return [owned_in, owned_out], others, more, grad_x


def sum_whole(keep, send):
    blocks = jnp.concatenate([keep, send], axis=0)
    sums = lax.psum_scatter(blocks, "expert", scatter_dimension=0, tiled=False)
    return [sums.astype(jnp.float32)]


def sum_messages(keep, got):
    sums = [keep[i].astype(jnp.float32) + got[i].astype(jnp.float32) for i in range(4)]
    return [sums[0]] + [v.astype(jnp.bfloat16) for v in sums[1:]]


def sum_ring(messages, between):
    own, to_below, to_above, far = messages
    got_far = shift_up(far)
    from_above = shift_down(to_below)
    if between is not None:
        to_above = after(to_above, between)
    onward = add_low(to_above, got_far)
    return [own, from_above, shift_up(onward)], onward


def deal_back(value, placement):
    tokens, width = value.shape
    value = value.reshape(1, SEQ_DEV, tokens // SEQ_DEV, width)
    value = lax.all_to_all(value, "expert", split_axis=2, concat_axis=0, tiled=True)
    return value.reshape(placement.shape[0], -1, width)[placement]


def pad_columns(value, width):
    return jnp.pad(value, ((0, 0), (0, width - value.shape[1])))


def body(
    tokens,
    cotangent,
    lengths,
    placement,
    routes,
    priority,
    g_attn,
    w_query,
    key_projection,
    value_projection,
    w_out,
    g_moe,
    w_router,
    w_gate,
    w_up,
    w_down,
):
    row_seqs, piece_len, width = tokens.shape
    expert_devices = lax.axis_size("expert")
    plane_size = lax.axis_size("dp")
    tuned = expert_devices == 8 and plane_size == 4
    my_index = lax.axis_index("expert")
    seq_len = piece_len * expert_devices
    token_count = SEQ_DEV * seq_len
    query_width = w_query.shape[1]
    kv_width = key_projection.shape[1]
    expert_count = w_router.shape[1]
    per_device = expert_count // expert_devices
    capacity = (9 * token_count * TOPK + 64 * expert_count - 1) // (64 * expert_count) * 8
    code_list = jnp.arange(row_seqs, dtype=jnp.int32)
    source = jnp.sum(
        jnp.where(placement[:, None] == code_list[None, :], code_list[:, None], 0), axis=0
    )
    pack = jnp.concatenate(
        [
            w_query,
            key_projection,
            value_projection,
            pad_columns(g_attn[:, None], 128),
            w_out,
            pad_columns(jnp.concatenate([w_router, g_moe[:, None]], axis=1), 128),
        ],
        axis=1,
    )
    sent = tokens[source].reshape(expert_devices, SEQ_DEV, piece_len, width)
    ranks = slot_ranks(routes.reshape(-1), priority.reshape(-1)).reshape(token_count, TOPK)
    codes = jnp.minimum(ranks, capacity) + 1
    expert_list = jnp.arange(expert_count, dtype=jnp.int32)
    picks = routes[None, :, :] == expert_list[:, None, None]
    code_table = jnp.sum(jnp.where(picks, codes[None], 0), axis=2)
    table_rows = -(-expert_count // 16) * 16
    table = jnp.zeros((table_rows, width), jnp.bfloat16)
    table = table.at[:expert_count, :token_count].set(code_table.astype(jnp.bfloat16))
    early = jnp.concatenate([cotangent.reshape(token_count, width), table], axis=0)
    got_tokens, pack_parts, pack_places, early_parts, weights = gather_front(
        pack, early, sent, w_gate, w_up, w_down, tuned
    )
    x_local = got_tokens.reshape(token_count, width)
    order = expert_order(tuned, expert_devices)
    seqs = source.reshape(expert_devices, SEQ_DEV)[order].reshape(-1)
    rel_of = jnp.sum(
        jnp.where(
            order[None, :] == jnp.arange(expert_devices)[:, None],
            jnp.arange(expert_devices)[None, :],
            0,
        ),
        axis=1,
    )
    plane = lax.axis_index("dp").reshape(1)
    scalars = jnp.concatenate([my_index.reshape(1), seqs, order, rel_of, plane])
    scalars = scalars.astype(jnp.int32)
    grads_all = jnp.zeros((16, 128), jnp.bfloat16)
    codes_all = grads_all
    if not tuned:
        early_all = early_parts[0]
        pieces = early_all[:, :token_count].reshape(expert_devices, row_seqs, piece_len, width)
        pieces = pieces[:, seqs].reshape(
            expert_devices, expert_devices, SEQ_DEV, piece_len, width
        )
        grads_all = pieces.transpose(1, 2, 0, 3, 4).reshape(expert_devices, token_count, width)
        codes_all = early_all[:, token_count:, :token_count]
        early_parts = []
    own_seqs = lax.dynamic_slice_in_dim(source, my_index * SEQ_DEV, SEQ_DEV)
    positions, labels = device_layout(lengths[own_seqs], seq_len)
    cosine_table, sine_values = rope_tables(positions, HEAD_SIZE)
    cos_wide = jnp.concatenate([cosine_table, cosine_table], axis=1)
    sin_wide = jnp.concatenate([-sine_values, sine_values], axis=1)
    plan = {
        "inputs": len(pack_parts),
        "experts": expert_count,
        "places": pack_places,
    }
    row_order = all_order()
    normed_moe, residual, h1, q, k, v, probs, mixed, aux, w_full = run_forward(
        plan,
        row_order,
        x_local,
        cos_wide,
        sin_wide,
        labels[:, None],
        labels[None, :],
        pack_parts,
        pack.shape[1],
    )
    inputs, weight_places, token_places = gather_inputs(normed_moe, weights, per_device, tuned)
    inputs = inputs + early_parts
    plan = {
        "inputs": len(inputs),
        "blocks": expert_devices,
        "per_device": per_device,
        "ff": w_gate.shape[2],
        "weights": weight_places,
        "tokens": token_places,
        "token_count": token_count,
        "piece": piece_len,
        "early": list(range(len(inputs) - len(early_parts), len(inputs))),
    }
    router_t = aux[:expert_count].astype(jnp.bfloat16)
    back_keep, back_send, out_keep, out_send, x_slots, dy_slots, hid, dga, dua = run_experts(
        plan, capacity, table_rows, scalars, router_t, codes_all, grads_all, residual, inputs
    )
    if tuned:
        back_got = swap_core(back_send)
        out_got = swap_core(after(out_send, back_got))
        messages = sum_messages(back_keep, back_got)
        x_slots = after(x_slots, *messages)
    if width // plane_size * 2 == w_gate.shape[2] and width % (128 * plane_size) == 0:
        weight_grads = expert_weight_grads(x_slots, dga, dua, hid, dy_slots, plane_size)
        flat = weight_grads.reshape(-1, weight_grads.shape[-1])
        owned = lax.psum_scatter(flat, "dp", scatter_dimension=0, tiled=True)
        owned = owned.reshape(weight_grads.shape[1:])
        half = owned.shape[-1] // 2
        owned_gate, owned_up = owned[0].astype(jnp.float32), owned[1].astype(jnp.float32)
        owned_down = jnp.concatenate([owned[2, :, :, :half], owned[2, :, :, half:]], axis=1)
    else:
        gate_up, down = whole_weight_grads(x_slots, dga, dua, hid, dy_slots)
        owned = lax.psum_scatter(gate_up, "dp", scatter_dimension=2, tiled=True)
        owned_gate, owned_up = owned[0].astype(jnp.float32), owned[1].astype(jnp.float32)
        owned_down = lax.psum_scatter(down, "dp", scatter_dimension=2, tiled=True)
    owned_down = owned_down.astype(jnp.float32)
    if tuned:
        backs, _ = sum_ring(messages, weight_grads)
        messages = sum_messages(after(out_keep, backs[1]), out_got)
        backs[0] = after(backs[0], *messages)
        messages[1:] = lax.optimization_barrier(tuple(messages[1:]) + tuple(backs[1:]))[:3]
    else:
        backs = sum_whole(back_keep, back_send)
        sums = sum_whole(out_keep, out_send)
    final = run_backward(
        tuned,
        expert_count,
        piece_len if tuned else 0,
        row_order,
        scalars,
        early_parts if tuned else [grads_all, codes_all],
        table_rows,
        backs,
        [
            residual,
            normed_moe,
            mixed,
            aux,
            x_local,
            cos_wide,
            sin_wide,
            h1,
            q,
            k,
            v,
            probs,
        ],
        w_full,
    )
    payload, grad_x = final[:-1], final[-1]
    if tuned:
        sums, onward = sum_ring(messages, grad_x)
        *payload, _ = lax.optimization_barrier(tuple(payload) + (onward,))
    others = (owned_gate, owned_up, owned_down)
    (owned_in, owned_out), others, more, grad_x = scatter_payload(
        payload, tuned, others, sums, grad_x
    )
    owned_gate, owned_up, owned_down = others
    if tuned:
        sums = list(more)
    if tuned:
        total = sums[0] + sums[1].astype(jnp.float32) + sums[2].astype(jnp.float32)
        output = total.astype(jnp.bfloat16).reshape(row_seqs, piece_len, width)
    else:
        output = deal_back((residual + sums[0]).astype(jnp.bfloat16), placement)
    input_grad = deal_back(grad_x, placement)
    return (
        output,
        input_grad,
        owned_in[:, query_width + 2 * kv_width],
        owned_in[:, :query_width],
        owned_in[:, query_width : query_width + kv_width],
        owned_in[:, query_width + kv_width : query_width + 2 * kv_width],
        owned_out[:, :width],
        owned_out[:, width + expert_count],
        owned_out[:, width : width + expert_count],
        owned_gate,
        owned_up,
        owned_down,
    )


def solution(mesh):
    return jax.shard_map(
        body,
        mesh=mesh,
        in_specs=(
            P("dp", "expert", None),
            P("dp", "expert", None),
            P("dp", None),
            P("dp"),
            P(("dp", "expert"), None),
            P(("dp", "expert"), None),
            P(("dp", "expert")),
            P(("dp", "expert"), None),
            P(("dp", "expert"), None),
            P(("dp", "expert"), None),
            P(("dp", "expert"), None),
            P(("dp", "expert")),
            P(("dp", "expert"), None),
            P("expert", "dp", None),
            P("expert", "dp", None),
            P("expert", None, "dp"),
        ),
        out_specs=(
            P("dp", "expert", None),
            P("dp", "expert", None),
            P(("dp", "expert")),
            P(("dp", "expert"), None),
            P(("dp", "expert"), None),
            P(("dp", "expert"), None),
            P(("dp", "expert"), None),
            P(("dp", "expert")),
            P(("dp", "expert"), None),
            P("expert", "dp", None),
            P("expert", "dp", None),
            P("expert", None, "dp"),
        ),
        check_vma=False,
    )
```
